128 devices in a mesh: ctx: 32 (over z, y, x_hi), wa: 4 (over x_lo, core).
Axes of the slice: x: 4 (x_hi: 2, x_lo: 2; x = x_hi * 2 + x_lo), y: 4, z: 4, core: 2. Of those that a mesh axis runs over, the one named last changes fastest.
Arguments:
- tokens: bfloat16 [4096, 1024], P('ctx'), may hold values from -6 to 6
- norm1_gain: float32 [1024], replicated, may hold values from 0.5 to 1.5
- w_query: bfloat16 [1024, 1024], P(None, 'wa'), may hold values from -0.5 to 0.5
- key_weight: bfloat16 [1024, 512], P(None, 'wa'), may hold values from -0.5 to 0.5
- value_weight: bfloat16 [1024, 512], P(None, 'wa'), may hold values from -0.1875 to 0.1875
- w_out: bfloat16 [1024, 1024], P('wa'), may hold values from -6 to 6
- norm2_gain: float32 [1024], replicated, may hold values from 0.5 to 1.5
- w_router: bfloat16 [1024, 32], replicated, may hold values from -0.09375 to 0.09375
- w_gate: bfloat16 [32, 1024, 512], P('ctx', None, 'wa'), may hold values from -0.1875 to 0.1875
- w_up: bfloat16 [32, 1024, 512], P('ctx', None, 'wa'), may hold values from -0.1875 to 0.1875
- w_down: bfloat16 [32, 512, 1024], P('ctx', 'wa'), may hold values from -1 to 1
- routes: int32 [4096, 8], P('ctx'), may hold values from 0 to 31, all different within a row; in each aligned block of 128 rows (0 to 127, 128 to 255, ...) at most 64 rows name the same one
- cotangent: bfloat16 [4096, 1024], P('ctx'), may hold values from -6 to 6
Outputs:
- output: bfloat16 [4096, 1024], P('ctx')
- grad_tokens: bfloat16 [4096, 1024], P('ctx')
- grad_norm1_gain: float32 [1024], replicated
- grad_w_query: float32 [1024, 1024], P(None, 'wa')
- grad_w_key: float32 [1024, 512], P(None, 'wa')
- grad_w_value: float32 [1024, 512], P(None, 'wa')
- grad_w_out: float32 [1024, 1024], P('wa')
- grad_norm2_gain: float32 [1024], replicated
- grad_w_router: float32 [1024, 32], replicated
- grad_w_gate: float32 [32, 1024, 512], P('ctx', None, 'wa')
- grad_w_up: float32 [32, 1024, 512], P('ctx', None, 'wa')
- grad_w_down: float32 [32, 512, 1024], P('ctx', 'wa')
The draws below stay inside these ranges and needn't reach their ends.
Inputs may be any that keep to these rules, and one draw needn't show every extreme that they name: `routes`: each row names 8 different experts; in each aligned block of 128 rows no expert is named by more than 64 rows.
All inputs are finite; a program needn't handle non-finite values.
Results may differ from the reference program's by a relative error of at most 0.04.
Values may be sent and summed in bfloat16 or wider, within the bound.
No kernel may reach another device: no remote copies, remote signals or barrier semaphores. Data moves between devices by JAX's collectives and lax.ppermute only.
A program may use at most 128 MiB of HBM per device.

```python
import math
import jax
import jax.numpy as jnp
import numpy as np
from jax import lax

MODEL_DIM = 1024
QUERY_HEAD_COUNT = 16
KV_HEAD_COUNT = 8
HEAD_DIM = 64
EXPERTS = 32
FF = 512
TOP = 8
TOK_DEV = 128
CAP = 64
TOKEN_COUNT = 4096
N_CTX = 32
N_WA = 4


def level_of(key, extent, pieces, smallest, high):
    level, own = 1.0, jax.random.fold_in(key, 6)
    for axis_at, blocks in pieces:
        draws = jnp.exp(jax.random.uniform(jax.random.fold_in(own, axis_at), (blocks,), jnp.float32, smallest / len(pieces), high / len(pieces)))
        level = level * jnp.repeat(draws, extent[axis_at] // blocks).reshape([-1 if axis == axis_at else 1 for axis in range(len(extent))])
    return level


def assign_block(own_key, own, number, rows, amount, top, most, skew):
    sequence = jax.random.permutation(own_key, amount)
    packed, ordinary = load_shares(amount, rows * top, most, skew, True), load_shares(amount, rows * top, most, skew, False)
    places = jnp.arange(amount)

    def named(lengths, offset_by):
        used = int((lengths > 0).sum())
        fixed = max(1, used // 4)
        shifted = fixed + (places - fixed + offset_by * (used - fixed)) % max(1, amount - fixed)
        return jnp.zeros((amount,), jnp.int32).at[sequence[jnp.where(places < fixed, places, shifted)]].set(jnp.asarray(lengths, jnp.int32))

    lengths = jnp.where(number % 4 == 0, named(packed, number // 4), named(ordinary, number - number // 4 - 1))
    mixed = jax.random.permutation(jax.random.fold_in(own, 3), amount)
    donor, receiver = mixed[0:amount // 2 * 2:2], mixed[1:amount // 2 * 2:2]
    room = jnp.minimum(lengths[donor] - 1, most - lengths[receiver]) // 2
    room = jnp.where((donor == sequence[0]) | (receiver == sequence[0]) | (lengths[receiver] == 0), 0, jnp.maximum(room, 0))
    shifted = jax.random.randint(jax.random.fold_in(own, 4), (amount // 2,), 0, 1 << 20) % (room + 1)
    lengths = lengths.at[donor].add(-shifted).at[receiver].add(shifted)
    members = jnp.searchsorted(jnp.cumsum(lengths), jnp.arange(rows * top), side="right").astype(jnp.int32)
    table = members.reshape(top, rows).T
    table = table[jax.random.permutation(jax.random.fold_in(own, 1), rows)]
    offset_by = jax.random.randint(jax.random.fold_in(own, 2), (rows, 1), 0, top)
    return jnp.take_along_axis(table, (jnp.arange(top)[None, :] + offset_by) % top, axis=1)


def load_shares(number_of, total, most, lean, full):
    portions = [(1 << 20) // math.isqrt(grade ** lean) + 1 for grade in range(1, number_of + 1)]
    largest = most if full else min(most, max(-(-total // number_of), total * portions[0] // sum(portions)))
    least = 1 if total - largest >= number_of - 1 else 0
    counts, surplus = [largest] + [least] * (number_of - 1), total - largest - least * (number_of - 1)
    while surplus > 0:
        candidates = [i for i in range(1, number_of) if counts[i] < largest] or [i for i in range(1, number_of) if counts[i] < most]
        pool, budget = sum([portions[i] for i in candidates]), surplus
        for i in candidates:
            addition = min(most - counts[i], max(1, budget * portions[i] // pool), surplus)
            counts[i] = counts[i] + addition
            surplus = surplus - addition
    return np.array(counts)


def centred(own_key, dims, scale, most, split=(), held_as=jnp.bfloat16):
    level = level_of(own_key, dims, split, -0.22, 0.18) if split else 1.0
    values = jax.random.normal(own_key, dims, jnp.float32) * scale * level
    return jnp.minimum(jnp.maximum(values, -most), most).astype(held_as)


def setup_inputs(seed: int = 0) -> dict:
    key_list = jax.random.split(jax.random.key(seed), 14)
    tokens = centred(key_list[0], (TOKEN_COUNT, MODEL_DIM), 1.0, 6.0, ((0, 32),))
    norm1_gain = jnp.clip(1.0 + 0.1 * jax.random.normal(key_list[1], (MODEL_DIM,), jnp.float32), 0.5, 1.5)
    w_query = centred(key_list[2], (MODEL_DIM, QUERY_HEAD_COUNT * HEAD_DIM), (MODEL_DIM // 8) ** -0.5, 0.5, ((1, 4),))
    key_weight = centred(key_list[3], (MODEL_DIM, KV_HEAD_COUNT * HEAD_DIM), (MODEL_DIM // 8) ** -0.5, 0.5, ((1, 4),))
    value_weight = centred(key_list[4], (MODEL_DIM, KV_HEAD_COUNT * HEAD_DIM), MODEL_DIM ** -0.5, 0.1875, ((1, 4),))
    w_out = centred(key_list[5], (QUERY_HEAD_COUNT * HEAD_DIM, MODEL_DIM), (max(1, QUERY_HEAD_COUNT * HEAD_DIM * 4 // TOKEN_COUNT)) ** -0.5, 6.0, ((0, 4),))
    norm2_gain = jnp.clip(1.0 + 0.1 * jax.random.normal(key_list[6], (MODEL_DIM,), jnp.float32), 0.5, 1.5)
    w_router = centred(key_list[7], (MODEL_DIM, EXPERTS), (4 * MODEL_DIM) ** -0.5, 0.09375)
    w_gate = centred(key_list[8], (EXPERTS, MODEL_DIM, FF), MODEL_DIM ** -0.5, 0.1875, ((0, 32), (2, 4)))
    w_up = centred(key_list[9], (EXPERTS, MODEL_DIM, FF), MODEL_DIM ** -0.5, 0.1875, ((0, 32), (2, 4)))
    w_down = centred(key_list[10], (EXPERTS, FF, MODEL_DIM), (FF // 16) ** -0.5, 1.0, ((0, 32), (1, 4)))
    routes_keys = jax.random.split(jax.random.fold_in(key_list[11], 1), TOKEN_COUNT // TOK_DEV)
    routes_turns = jax.random.permutation(jax.random.fold_in(key_list[11], 3), TOKEN_COUNT // TOK_DEV)
    routes = jax.vmap(lambda own, number: assign_block(jax.random.fold_in(key_list[11], 2), own, number, TOK_DEV, EXPERTS, TOP, CAP, 1))(routes_keys, routes_turns).reshape((TOKEN_COUNT, TOP))
    cotangent = centred(key_list[12], (TOKEN_COUNT, MODEL_DIM), 1.0, 6.0, ((0, 32),))
    return dict(tokens=tokens, norm1_gain=norm1_gain, w_query=w_query, key_weight=key_weight, value_weight=value_weight, w_out=w_out, norm2_gain=norm2_gain, w_router=w_router, w_gate=w_gate, w_up=w_up, w_down=w_down, routes=routes, cotangent=cotangent)


@jax.custom_vjp
def lower_precision(v):
    return lax.optimization_barrier(v.astype(jnp.bfloat16)).astype(jnp.float32)

@jax.custom_vjp
def lower_backward(v):
    return v

def low_keep(v):
    return (lower_precision(v), None)

def low_pass(kept, grad):
    return (grad,)

def back_keep(v):
    return (v, None)

def back_low(kept, grad):
    return (lower_precision(grad),)
lower_precision.defvjp(low_keep, low_pass)
lower_backward.defvjp(back_keep, back_low)
epsilon = 1e-06
highest_precision = lax.Precision.HIGHEST

def local_positions(first_row, row_count, device_rows, group_count):
    numbers = first_row + jnp.arange(row_count, dtype=jnp.int32)
    owner_index = numbers // device_rows
    within = numbers % device_rows
    halfway = device_rows // 2
    return jnp.where(within < halfway, owner_index * halfway + within, (2 * group_count - 1 - owner_index) * halfway + within - halfway)

def rotary_turn(vectors, token_positions, direction):
    halfway = vectors.shape[-1] // 2
    inverse = jnp.power(10000.0, -2.0 * jnp.arange(halfway, dtype=jnp.float32) / vectors.shape[-1])
    angles = token_positions.astype(jnp.float32)[:, None] * inverse[None, :]
    cosine = jnp.cos(angles)[:, None, :]
    sine_part = direction * jnp.sin(angles)[:, None, :]
    leading = vectors[..., :halfway]
    trailing = vectors[..., halfway:]
    return jnp.concatenate([leading * cosine - trailing * sine_part, trailing * cosine + leading * sine_part], -1)

def soft_weights(scores):
    largest = lax.optimization_barrier(jnp.max(scores, -1, keepdims=True))
    raised = jnp.exp(scores - largest)
    return raised / lax.optimization_barrier(jnp.sum(raised, -1, keepdims=True))

def rms_scale(inputs, gain):
    return inputs * lax.rsqrt(lax.optimization_barrier(jnp.mean(inputs * inputs, -1, keepdims=True)) + epsilon) * gain

def attend_block(query_rows, query_pos, keys, values, token_positions):
    grouped_heads = query_rows.reshape(-1, KV_HEAD_COUNT, QUERY_HEAD_COUNT // KV_HEAD_COUNT, HEAD_DIM)
    scores = lower_backward(jnp.einsum('rjgd,sjd->jgrs', grouped_heads, keys, precision=highest_precision) / HEAD_DIM)
    allowed = token_positions[None, :] <= query_pos[:, None]
    probs = soft_weights(jnp.where(allowed, scores, -1e+30))
    mixed = jnp.einsum('jgrs,sjd->rjgd', lower_precision(probs), values, precision=highest_precision)
    return mixed.reshape(-1, QUERY_HEAD_COUNT * HEAD_DIM)

def expert_layer(normed, routes, picks, gates, gate_w, up_w, down_w):
    share = lax.optimization_barrier(jnp.sum(jnp.where(picks, gates[:, :, None], 0.0), 1))
    padded = jnp.concatenate([normed, jnp.zeros((1, MODEL_DIM), jnp.float32)], 0)
    share_pad = jnp.concatenate([share, jnp.zeros((1, EXPERTS), jnp.float32)], 0)
    stripe = FF // N_WA
    slot_total = N_CTX * CAP

    def one_expert(summed_out, expert_item):
        number, gate_matrix, up_matrix, down_matrix = expert_item
        member = jnp.any(routes == number, axis=1)
        picked = jnp.nonzero(member, size=slot_total, fill_value=TOKEN_COUNT)[0].astype(jnp.int32)
        inputs = padded[picked]
        result = jnp.zeros((slot_total, MODEL_DIM), jnp.float32)
        for stripe_index in range(N_WA):
            start_col = stripe_index * stripe
            entry_rows = lower_backward(inputs)
            gate_pre = lower_backward(jnp.dot(entry_rows, gate_matrix[:, start_col:start_col + stripe], precision=highest_precision))
            up_pre = lower_backward(jnp.dot(entry_rows, up_matrix[:, start_col:start_col + stripe], precision=highest_precision))
            active = lower_precision(gate_pre * jax.nn.sigmoid(gate_pre) * up_pre)
            result = result + lower_backward(lower_precision(jnp.dot(active, down_matrix[start_col:start_col + stripe, :], precision=highest_precision)))
        weight_col = share_pad[picked, number]
        return (summed_out.at[picked].add(weight_col[:, None] * result), None)
    summed_out, unused = lax.scan(jax.checkpoint(one_expert), jnp.zeros((TOKEN_COUNT + 1, MODEL_DIM), jnp.float32), (jnp.arange(EXPERTS, dtype=jnp.int32), gate_w, up_w, down_w))
    return summed_out[:TOKEN_COUNT]

def forward(widened, gain_first, query_w, key_matrix, value_matrix, out_w, gain_second, router_w, gate_w, up_w, down_w, routes, token_positions):
    first_normalized = lower_precision(rms_scale(widened, gain_first))
    query_rot = lower_precision(rotary_turn(lower_backward(jnp.dot(first_normalized, query_w, precision=highest_precision)).reshape(TOKEN_COUNT, QUERY_HEAD_COUNT, HEAD_DIM), token_positions, 1.0))
    rotated_key = lower_precision(rotary_turn(lower_backward(jnp.dot(first_normalized, key_matrix, precision=highest_precision)).reshape(TOKEN_COUNT, KV_HEAD_COUNT, HEAD_DIM), token_positions, 1.0))
    value_expanded = lower_precision(lower_backward(jnp.dot(first_normalized, value_matrix, precision=highest_precision))).reshape(TOKEN_COUNT, KV_HEAD_COUNT, HEAD_DIM)
    block_rows = math.gcd(TOKEN_COUNT, 512)
    block_count = TOKEN_COUNT // block_rows

    def one_block(block_pair):
        return attend_block(block_pair[0], block_pair[1], rotated_key, value_expanded, token_positions)
    context = lax.map(jax.checkpoint(one_block), (query_rot.reshape(block_count, block_rows, QUERY_HEAD_COUNT, HEAD_DIM), token_positions.reshape(block_count, block_rows)))
    context = lower_precision(lower_backward(context.reshape(TOKEN_COUNT, QUERY_HEAD_COUNT * HEAD_DIM)))
    mixed = lower_backward(jnp.dot(context, out_w, precision=highest_precision))
    middle = widened + mixed
    normed_second = lower_precision(rms_scale(middle, gain_second))
    logits = lower_backward(jnp.dot(normed_second, router_w, precision=highest_precision))
    picks = routes[:, :, None] == jnp.arange(EXPERTS, dtype=jnp.int32)[None, None, :]
    chosen = lax.optimization_barrier(jnp.sum(jnp.where(picks, logits[:, None, :], 0.0), -1))
    gates = soft_weights(chosen)
    return middle + expert_layer(normed_second, routes, picks, gates, gate_w, up_w, down_w)

def reference(tokens, norm1_gain, w_query, key_weight, value_weight, w_out, norm2_gain, w_router, w_gate, w_up, w_down, routes, cotangent):
    token_positions = local_positions(0, TOKEN_COUNT, TOK_DEV, N_CTX)
    floats = (tokens.astype(jnp.float32), norm1_gain.astype(jnp.float32), w_query.astype(jnp.float32), key_weight.astype(jnp.float32), value_weight.astype(jnp.float32), w_out.astype(jnp.float32), norm2_gain.astype(jnp.float32), w_router.astype(jnp.float32), w_gate.astype(jnp.float32), w_up.astype(jnp.float32), w_down.astype(jnp.float32))

    def whole_layer(*weights):
        return forward(*weights, routes, token_positions)
    output, pullback = jax.vjp(whole_layer, *floats)
    gradients = pullback(cotangent.astype(jnp.float32))
    return (output.astype(jnp.bfloat16), gradients[0].astype(jnp.bfloat16), gradients[1], gradients[2], gradients[3], gradients[4], gradients[5], gradients[6], gradients[7], gradients[8], gradients[9], gradients[10])
```

```python
import jax
import jax.numpy as jnp
from jax import lax
from jax.experimental import pallas as pl
from jax.experimental.pallas import tpu as pltpu
from jax.sharding import PartitionSpec as P

HEAD_DIM = 64
CHUNK = 8

epsilon = 1e-06
f32 = jnp.float32
bf16 = jnp.bfloat16
CORE_SWAP = [(0, 1), (1, 0), (2, 3), (3, 2)]
CHIP_SWAP = [(0, 2), (2, 0), (1, 3), (3, 1)]
PARTNER = [(i, i ^ 2) for i in range(32)]
VMEM = pl.BlockSpec(memory_space=pltpu.VMEM)
SMEM = pl.BlockSpec(memory_space=pltpu.SMEM)


def dot(a, b):
    return jnp.dot(a, b, preferred_element_type=f32)


def dot_nt(a, b):
    return lax.dot_general(a, b, (((1,), (1,)), ((), ())), preferred_element_type=f32)


def dot_tn(a, b):
    return lax.dot_general(a, b, (((0,), (0,)), ((), ())), preferred_element_type=f32)


def exchange(value, axes):
    return lax.all_to_all(value, axes, split_axis=0, concat_axis=0, tiled=True)


def shape(dims, dtype=bf16):
    return jax.ShapeDtypeStruct(dims, dtype)


def on_device(kernel, name, in_specs, outs, scratch=(), megabytes=16, flops=0):
    return pl.pallas_call(
        kernel,
        out_shape=outs,
        in_specs=in_specs,
        out_specs=tuple(VMEM for _ in outs),
        scratch_shapes=list(scratch),
        cost_estimate=pl.CostEstimate(flops=flops, bytes_accessed=8_000_000, transcendentals=0) if flops else None,
        compiler_params=pltpu.CompilerParams(vmem_limit_bytes=megabytes * 1024 * 1024),
        name=name,
    )


def local_positions(first_row, row_count, device_rows, group_count):
    numbers = first_row + jnp.arange(row_count, dtype=jnp.int32)
    owner_index = numbers // device_rows
    within = numbers % device_rows
    halfway = device_rows // 2
    return jnp.where(
        within < halfway,
        owner_index * halfway + within,
        (2 * group_count - 1 - owner_index) * halfway + within - halfway,
    )


def angles_of(block):
    positions = local_positions(block * 128, 128, 128, 32)
    inverse = jnp.power(10000.0, -2.0 * jnp.arange(32, dtype=f32) / HEAD_DIM)
    return positions.astype(f32)[:, None] * inverse[None, :]


def lanes_of(dims):
    return lax.broadcasted_iota(jnp.int32, dims, len(dims) - 1)


def swap_halves(x):
    return pltpu.roll(x, 64, 1)


def turn_lanes(x, cosine, sine):
    lead = (lanes_of(x.shape) & 63) < 32
    return x * cosine + jnp.where(lead, pltpu.roll(x, 96, 1), pltpu.roll(x, 32, 1)) * sine


def turn_rows(x, cosine, sine):
    lead, trail = x[0:32], x[32:64]
    return jnp.concatenate([lead * cosine - trail * sine, trail * cosine + lead * sine], 0)


def prelude_kernel(
    at_ref, tokens_ref, gain_ref, wq_ref, wk_ref, wv_ref, cos_ref, sin_ref, cos_t_ref, sin_t_ref,
    kv_ref, normed_ref, q_ref, q_give_ref,
):
    side = at_ref[2]
    x = tokens_ref[...].astype(f32)
    root = lax.rsqrt(jnp.mean(x * x, -1, keepdims=True) + epsilon)
    normed = (x * root * gain_ref[...]).astype(bf16)
    normed_ref[...] = normed
    k = dot(normed, wk_ref[...])
    v = dot(normed, wv_ref[...])
    low = lanes_of(k.shape) < 64
    heads = (
        jnp.where(low, k, swap_halves(v)),
        jnp.where(low, swap_halves(k), v),
    )
    heads = [turn_lanes(y, cos_ref[...], sin_ref[...]).astype(bf16) for y in heads]
    for d in range(32):
        kv_ref[d] = heads[(d >> 1) & 1]
    qt = dot(normed, wq_ref[...]).T
    turned = [
        turn_rows(qt[64 * h : 64 * h + 64], cos_t_ref[...], sin_t_ref[...]).astype(bf16) * jnp.asarray(1.0 / HEAD_DIM, bf16)
        for h in range(4)
    ]
    pairs = [jnp.concatenate(turned[2 * j : 2 * j + 2], 0).astype(f32) for j in range(2)]
    q_ref[...] = jnp.where(side == 0, pairs[0], pairs[1]).astype(bf16)
    q_give_ref[...] = jnp.where(side == 0, pairs[1], pairs[0]).astype(bf16)


def to_columns(side, own_ref, other_ref, out_ref, first_row):
    for g in range(2):
        own = own_ref[64 * g : 64 * g + 64, :].astype(f32)
        other = other_ref[64 * g : 64 * g + 64, :].astype(f32)
        zero = jnp.where(side == 0, own, other)
        one = jnp.where(side == 0, other, own)
        low = lanes_of(own.shape) < 64
        out_ref[first_row : first_row + 64, 128 * g : 128 * g + 128] = jnp.where(
            low, zero, swap_halves(one)
        ).astype(bf16)
        out_ref[first_row : first_row + 64, 256 + 128 * g : 384 + 128 * g] = jnp.where(
            low, swap_halves(zero), one
        ).astype(bf16)


def from_columns(side, columns, g):
    a = columns[:, 128 * g : 128 * g + 128]
    b = columns[:, 256 + 128 * g : 384 + 128 * g]
    low = lanes_of(a.shape) < 64
    zero = jnp.where(low, a, swap_halves(b))
    one = jnp.where(low, swap_halves(a), b)
    return jnp.where(side == 0, zero, one), jnp.where(side == 0, one, zero)


def masked_early(scores, base, c):
    rows = lax.broadcasted_iota(jnp.int32, scores.shape, 0) + base * 64
    columns = lanes_of(scores.shape)
    block = (c & 29) + ((columns >> 6) & 1) * 2
    return jnp.where(rows <= block * 64 + (columns & 63), scores, -1e30)


def masked_late(scores, base, c):
    rows = lax.broadcasted_iota(jnp.int32, scores.shape, 0)
    columns = lanes_of(scores.shape)
    block = (c & 29) + ((columns >> 6) & 1) * 2
    key_at = (63 - base - (rows >> 6)) * 64 + (rows & 63)
    return jnp.where(key_at <= (63 - block) * 64 + (columns & 63), scores, -1e30)


def attend_kernel(
    at_ref, own_ref, other_ref, kv_ref,
    mine_ref, give_ref, o_ref, lse_ref,
    q_ref, m_ref, l_ref, acc_ref,
):
    c, side = at_ref[3], at_ref[2]
    to_columns(side, own_ref, other_ref, q_ref, 0)
    q_ref[64:128, :] = jnp.zeros((64, 512), bf16)
    m_ref[...] = jnp.full(m_ref.shape, -1e30, f32)
    l_ref[...] = jnp.zeros(l_ref.shape, f32)
    acc_ref[...] = jnp.zeros(acc_ref.shape, f32)

    def step(base, keys_half, cols, mask):
        kv = kv_ref[base : base + CHUNK, keys_half, :].reshape(CHUNK * 64, 128)
        s = dot(kv, q_ref[:, cols])
        if mask is not None:
            s = mask(s, base, c)
        m_old = m_ref[:, cols]
        m_new = jnp.maximum(m_old, jnp.max(s, 0, keepdims=True))
        p = jnp.exp(s - m_new)
        factor = jnp.exp(m_old - m_new)
        m_ref[:, cols] = m_new
        l_ref[:, cols] = l_ref[:, cols] * factor + jnp.sum(p, 0, keepdims=True)
        acc_ref[:, cols] = acc_ref[:, cols] * factor + dot_tn(kv, p.astype(bf16))

    early, late = slice(0, 64), slice(64, 128)
    first, second = slice(0, 256), slice(256, 512)
    for base in range(0, 32, CHUNK):
        step(base, early, second, None)

        @pl.when(base <= (c | 2))
        def _():
            step(base, early, first, masked_early)

        @pl.when(base + CHUNK > (c & 29))
        def _():
            step(base, late, second, masked_late)

    total = l_ref[...]
    o_ref[...] = acc_ref[64:128, :] / total
    lse_ref[...] = m_ref[...] + jnp.log(total)
    for g in range(2):
        own, other = from_columns(side, o_ref[...], g)
        mine_ref[64 * g : 64 * g + 64, :] = own.astype(bf16)
        give_ref[64 * g : 64 * g + 64, :] = other.astype(bf16)


def reverse_kernel(
    at_ref, own_ref, other_ref, kv_ref, do_own_ref, do_other_ref, o_ref, lse_ref,
    cos_ref, sin_ref, cos2_ref, sin2_ref,
    dq_ref, dq_give_ref, dkv_ref,
    q_ref, do_ref, delta_ref, acc_ref,
):
    c, side = at_ref[3], at_ref[2]
    to_columns(side, own_ref, other_ref, q_ref, 0)
    q_ref[64:128, :] = jnp.zeros((64, 512), bf16)
    to_columns(side, do_own_ref, do_other_ref, do_ref, 64)
    do_ref[0:64, :] = jnp.zeros((64, 512), bf16)
    delta_ref[...] = jnp.sum(do_ref[64:128, :].astype(f32) * o_ref[...], 0, keepdims=True)
    acc_ref[...] = jnp.zeros(acc_ref.shape, f32)

    def step(base, keys_half, cols, mask, add):
        kv = kv_ref[base : base + CHUNK, keys_half, :].reshape(CHUNK * 64, 128)
        q = q_ref[:, cols]
        do = do_ref[:, cols]
        s = dot(kv, q)
        if mask is not None:
            s = mask(s, base, c)
        p = jnp.exp(s - lse_ref[:, cols])
        dp = dot(kv, do)
        ds = (p * (dp - delta_ref[:, cols])).astype(bf16)
        acc_ref[:, cols] += dot_tn(kv, ds)
        dkv = (dot_nt(ds, q) + dot_nt(p.astype(bf16), do)).reshape(CHUNK, 64, 128)
        if add:
            dkv += dkv_ref[base : base + CHUNK, keys_half, :].astype(f32)
        dkv_ref[base : base + CHUNK, keys_half, :] = dkv.astype(bf16)

    early, late = slice(0, 64), slice(64, 128)
    first, second = slice(0, 256), slice(256, 512)
    for base in range(0, 32, CHUNK):
        step(base, early, second, None, False)

        @pl.when(base <= (c | 2))
        def _():
            step(base, early, first, masked_early, True)

        @pl.when(base + CHUNK > (c & 29))
        def _():
            step(base, late, second, masked_late, False)

        @pl.when(base + CHUNK <= (c & 29))
        def _():
            dkv_ref[base : base + CHUNK, late, :] = jnp.zeros((CHUNK, 64, 128), bf16)

    for g in range(2):
        own, other = from_columns(side, acc_ref[0:64, :] * (1.0 / HEAD_DIM), g)
        here = slice(64 * g, 64 * g + 64)
        dq_ref[here, :] = turn_rows(own, cos_ref[...], -sin_ref[...]).astype(bf16)
        dq_give_ref[here, :] = turn_rows(other, cos2_ref[...], -sin2_ref[...]).astype(bf16)


def mix_kernel(at_ref, mine_ref, got_ref, w_out_ref, context_ref, keep_ref, give_ref):
    core, side = at_ref[1], at_ref[2]
    mine, got = mine_ref[...].astype(f32), got_ref[...].astype(f32)
    context_ref[0:128, :] = jnp.where(side == 0, mine, got).astype(bf16)
    context_ref[128:256, :] = jnp.where(side == 0, got, mine).astype(bf16)
    mixed = dot_tn(context_ref[...], w_out_ref[...])
    top, bottom = mixed[0:64], mixed[64:128]
    keep_ref[...] = jnp.where(core == 0, top, bottom).astype(bf16)
    give_ref[...] = jnp.where(core == 0, bottom, top).astype(bf16)


def selection(rank_ref, first, count):
    slot = lax.broadcasted_iota(jnp.int32, (64, 128), 0).astype(f32)
    return jnp.concatenate([(slot == rank_ref[e : e + 1, :]).astype(f32) for e in range(first, first + count)], 0)


def route_kernel(
    at_ref, tokens_ref, mine_ref, theirs_ref, gain_ref, router_ref, rank_ref, cot_ref,
    middle_ref, normed_ref, gates_ref, out_ref,
):
    wa, core = at_ref[0], at_ref[1]
    for half in range(2):
        here = slice(64 * half, 64 * half + 64)
        mixed = jnp.where(core == half, mine_ref[...].astype(f32), theirs_ref[...].astype(f32))
        middle = tokens_ref[here, :].astype(f32) + mixed
        middle_ref[here, :] = middle
        root = lax.rsqrt(jnp.mean(middle * middle, -1, keepdims=True) + epsilon)
        normed_ref[here, :] = (middle * root * gain_ref[...]).astype(bf16)
    logits = dot_nt(router_ref[...], normed_ref[...])
    member = rank_ref[...] >= 0.0
    top = jnp.max(jnp.where(member, logits, -1e30), 0, keepdims=True)
    raised = jnp.where(member, jnp.exp(jnp.where(member, logits - top, 0.0)), 0.0)
    gates_ref[...] = raised / jnp.sum(raised, 0, keepdims=True)
    quarter = normed_ref[:, pl.ds(pl.multiple_of(wa * 256, 256), 256)]
    for first in range(0, 32, 4):
        chosen = selection(rank_ref, first, 4)
        weights = jnp.concatenate(
            [
                jnp.sum(chosen[64 * n : 64 * n + 64] * gates_ref[first + n : first + n + 1, :], 1, keepdims=True)
                for n in range(4)
            ],
            0,
        )
        chosen = chosen.astype(bf16)
        here = slice(64 * first, 64 * first + 256)
        out_ref[here, 0:256] = dot(chosen, quarter).astype(bf16)
        out_ref[here, 256:512] = (weights * dot(chosen, cot_ref[...])).astype(bf16)


def expert_kernel(
    in_ref, w0_ref, w1_ref, w2_ref, w3_ref,
    out_ref, act_ref, dgate_ref, dup_ref,
    gate_ref, up_ref, down_ref,
):
    for p, w in enumerate((w0_ref, w1_ref, w2_ref, w3_ref)):
        here = slice(128 * p, 128 * p + 128)
        gate_ref[:, here] = w[0]
        up_ref[:, here] = w[1]
        for n in range(8):
            down_ref[here, 128 * n : 128 * n + 128] = w[2, 128 * n : 128 * n + 128, :]
    gate_pre = jnp.zeros((512, 512), f32)
    up_pre = jnp.zeros((512, 512), f32)
    d_act = jnp.zeros((512, 512), f32)
    for q in range(4):
        here = slice(256 * q, 256 * q + 256)
        x = in_ref[:, q, :, 0:256].reshape(512, 256)
        gate_pre += dot(x, gate_ref[here, :])
        up_pre += dot(x, up_ref[here, :])
        d_act += dot_nt(in_ref[:, q, :, 256:512].reshape(512, 256), down_ref[:, here])
    sigma = jax.nn.sigmoid(gate_pre)
    act_ref[...] = (gate_pre * sigma * up_pre).astype(bf16)
    dgate_ref[...] = (d_act * up_pre * sigma * (1.0 + gate_pre * (1.0 - sigma))).astype(bf16)
    dup_ref[...] = (d_act * gate_pre * sigma).astype(bf16)
    for q in range(4):
        here = slice(256 * q, 256 * q + 256)
        part = dot(act_ref[...], down_ref[:, here])
        out_ref[:, q, :, 0:256] = part.astype(bf16).reshape(32, 16, 256)
        d_x = dot_nt(dgate_ref[...], gate_ref[here, :]) + dot_nt(dup_ref[...], up_ref[here, :])
        out_ref[:, q, :, 256:512] = d_x.astype(bf16).reshape(32, 16, 256)


def expert_grad_kernel(in_ref, act_ref, dgate_ref, dup_ref, near_ref, far_ref):
    for q in range(4):
        here = slice(256 * q, 256 * q + 256)
        x = in_ref[:, q, :, 0:256].reshape(512, 256)
        d = in_ref[:, q, :, 256:512].reshape(512, 256)
        g_gate = dot_tn(x, dgate_ref[...]).astype(bf16)
        g_up = dot_tn(x, dup_ref[...]).astype(bf16)
        g_down = dot_tn(act_ref[...], d).astype(bf16)
        for p in range(4):
            to = near_ref if p < 2 else far_ref
            to[p % 2, 0, here, :] = g_gate[:, 128 * p : 128 * p + 128]
            to[p % 2, 1, here, :] = g_up[:, 128 * p : 128 * p + 128]
            for n in range(2):
                at = 256 * q + 128 * n
                to[p % 2, 2, at : at + 128, :] = g_down[128 * p : 128 * p + 128, 128 * n : 128 * n + 128]


def combine_kernel(back_ref, rank_ref, gates_ref, cot_ref, sent_ref, moe_ref, dgates_ref):
    d_normed = jnp.zeros((128, 256), f32)
    moe = jnp.zeros((128, 256), f32)
    for first in range(0, 32, 4):
        here = slice(64 * first, 64 * first + 256)
        chosen = selection(rank_ref, first, 4)
        gated = jnp.concatenate(
            [chosen[64 * n : 64 * n + 64] * gates_ref[first + n : first + n + 1, :] for n in range(4)], 0
        )
        high = gated.astype(bf16)
        low = (gated - high.astype(f32)).astype(bf16)
        picked = chosen.astype(bf16)
        part = back_ref[here, 0:256]
        d_normed += dot_tn(picked, back_ref[here, 256:512])
        moe += dot_tn(high, part) + dot_tn(low, part)
        along = jnp.sum(dot(picked, cot_ref[...]) * part.astype(f32), 1, keepdims=True)
        placed = chosen * along
        for n in range(4):
            dgates_ref[first + n : first + n + 1, :] = jnp.sum(
                placed[64 * n : 64 * n + 64], 0, keepdims=True
            )
    moe_ref[...] = moe.astype(bf16)
    sent_ref[0:128, :] = d_normed.astype(bf16)
    sent_ref[128:144, 0:128] = dgates_ref[0:16, :].astype(bf16)
    sent_ref[128:144, 128:256] = dgates_ref[16:32, :].astype(bf16)


def second_norm_kernel(
    at_ref, own_ref, across_ref, beside_ref, diagonal_ref, gates_ref, middle_ref, normed_ref, cot_ref,
    gain_ref, router_ref, w_out_ref, context_ref,
    dmiddle_ref, dmine_ref, dgive_ref, parts_ref, dnormed_ref, extra_ref,
):
    wa, side = at_ref[0], at_ref[2]
    pieces = [(own_ref, 0), (across_ref, 2), (beside_ref, 1), (diagonal_ref, 3)]
    for ref, flip in pieces:
        at = pl.multiple_of((wa ^ flip) * 256, 256)
        dnormed_ref[:, pl.ds(at, 256)] = ref[0:128, :].astype(f32)
    terms = [
        jnp.concatenate([ref[128:144, 0:128], ref[128:144, 128:256]], 0).astype(f32) for ref, _ in pieces
    ]
    d_gates = (terms[0] + terms[1]) + (terms[2] + terms[3])
    gates = gates_ref[...]
    d_logits = (gates * (d_gates - jnp.sum(gates * d_gates, 0, keepdims=True))).astype(bf16)
    gain = gain_ref[...]
    d_normed = dnormed_ref[...] + dot_tn(d_logits, router_ref[...])
    middle = middle_ref[...]
    root = lax.rsqrt(jnp.mean(middle * middle, -1, keepdims=True) + epsilon)
    unit = middle * root
    scaled = d_normed * gain
    gain_grad = jnp.sum(d_normed * unit, 0, keepdims=True)
    d_middle = cot_ref[...].astype(f32) + root * (
        scaled - unit * jnp.mean(scaled * unit, -1, keepdims=True)
    )
    dmiddle_ref[...] = d_middle
    d_mixed = d_middle.astype(bf16)
    d_context = dot_nt(w_out_ref[...], d_mixed)
    dmine_ref[...] = jnp.where(side == 0, d_context[0:128], d_context[128:256]).astype(bf16)
    dgive_ref[...] = jnp.where(side == 0, d_context[128:256], d_context[0:128]).astype(bf16)
    router_grad = dot(d_logits, normed_ref[...])
    extra_ref[...] = jnp.zeros(extra_ref.shape, f32)
    for q in range(4):
        here = slice(256 * q, 256 * q + 256)
        extra_ref[:, q, :] = router_grad[:, here]
        extra_ref[:, 4 + q, :] = jnp.broadcast_to(gain_grad[:, here], (32, 256))
        parts_ref[8 * q : 8 * q + 8, 0:32, :] = (
            dot(context_ref[...], d_mixed[:, here]).astype(bf16).reshape(8, 32, 256)
        )
    parts_ref[:, 32:48, :] = extra_ref[...].astype(bf16)


def late_kernel(
    at_ref, back_ref, cos_ref, sin_ref, normed_ref, wk_ref, wv_ref, first_ref, query_ref, early_ref,
    parts_ref, keep_ref, give_ref,
):
    core = at_ref[1]
    parts_ref[:, 0:32, :] = query_ref[...]
    parts_ref[:, 32:80, :] = early_ref[...]
    heads = []
    for j in range(2):
        total = jnp.zeros((128, 128), f32)
        for d in range(32):
            if (d >> 1) & 1 == j:
                total += back_ref[d].astype(f32)
        heads.append(turn_lanes(total, cos_ref[...], -sin_ref[...]))
    low = lanes_of((128, 128)) < 64
    d_k = jnp.where(low, heads[0], swap_halves(heads[1])).astype(bf16)
    d_v = jnp.where(low, swap_halves(heads[0]), heads[1]).astype(bf16)
    parts_ref[:, 80:112, 0:128] = dot_tn(normed_ref[...], d_k).astype(bf16).reshape(32, 32, 128)
    parts_ref[:, 80:112, 128:256] = dot_tn(normed_ref[...], d_v).astype(bf16).reshape(32, 32, 128)
    first = first_ref[...] + dot_nt(d_k, wk_ref[...]) + dot_nt(d_v, wv_ref[...])
    keep_ref[...] = jnp.where(core == 0, first[0:64], first[64:128]).astype(bf16)
    give_ref[...] = jnp.where(core == 0, first[64:128], first[0:64]).astype(bf16)


def share_kernel(in_ref, gain_ref, out_ref, gain2_ref, total_ref):
    total_ref[...] = jnp.sum(in_ref[...].astype(f32), 0)
    gain2_ref[...] = total_ref[68:72, :]
    total_ref[68:72, :] = gain_ref[...].astype(f32)
    out_ref[...] = jnp.broadcast_to(total_ref[...].astype(bf16)[None], (32, 112, 256))


def sum_over_wa(keep, give):
    got = lax.ppermute(give, "wa", CORE_SWAP)
    pair = (keep.astype(f32) + got.astype(f32)).astype(bf16)
    other = lax.ppermute(pair, "wa", CHIP_SWAP)
    mine = (pair.astype(f32) + other.astype(f32)).astype(bf16)
    return mine, lax.ppermute(mine, "wa", CORE_SWAP)


def pieces_over_wa(part):
    across = lax.ppermute(part, "wa", CHIP_SWAP)
    beside = lax.ppermute(part, "wa", CORE_SWAP)
    return across, beside, lax.ppermute(across, "wa", CORE_SWAP)


def local(
    tokens,
    norm1_gain,
    w_query,
    key_weight,
    value_weight,
    w_out,
    norm2_gain,
    w_router,
    w_gate,
    w_up,
    w_down,
    routes,
    cotangent,
):
    ctx = lax.axis_index("ctx").astype(jnp.int32)
    wa = lax.axis_index("wa").astype(jnp.int32)
    core, chip, side = wa % 2, wa // 2, (ctx >> 1) & 1
    at = jnp.stack([wa, core, side, ctx])
    rows, width, experts = 128, 1024, 32

    angles = angles_of(ctx)
    cosine, sine = jnp.cos(angles), jnp.sin(angles)
    one, zero = jnp.ones((rows, 64), f32), jnp.zeros((rows, 64), f32)
    cos_lanes = jnp.concatenate([cosine, cosine, one], 1)
    sin_lanes = jnp.concatenate([-sine, sine, zero], 1)
    cos_rows, sin_rows = cosine.T, sine.T
    gain1 = norm1_gain.reshape(1, width)
    kv_send, normed1, q_own, q_give = on_device(
        prelude_kernel,
        "prelude",
        [SMEM] + [VMEM] * 9,
        (shape((32, rows, 128)), shape((rows, width)), shape((rows, 128)), shape((rows, 128))),
    )(
        at, tokens, gain1, w_query, key_weight, value_weight, cos_lanes, sin_lanes, cos_rows, sin_rows
    )
    kv = exchange(kv_send, "ctx")
    q_other = lax.ppermute(q_give, "ctx", PARTNER)

    member = jnp.any(
        routes[:, :, None] == jnp.arange(experts, dtype=jnp.int32)[None, None, :], axis=1
    )
    lower = (jnp.arange(rows)[:, None] >= jnp.arange(rows)[None, :]).astype(bf16)
    rank = jnp.where(member, dot(lower, member.astype(bf16)) - 1.0, -1.0).T
    cot_quarter = lax.dynamic_slice_in_dim(cotangent, wa * 256, 256, 1)
    router_t = w_router.T
    gain2 = norm2_gain.reshape(1, width)
    down_lanes = w_down[0].reshape(128, 8, 128).transpose(1, 0, 2).reshape(width, 128)
    weights = jnp.stack([w_gate[0], w_up[0], down_lanes])

    kv, weights, rank, q_other = lax.optimization_barrier((kv, weights, rank, q_other))
    w_across, w_beside, w_diagonal = pieces_over_wa(weights)
    ctx_mine, ctx_give, context_o, lse = on_device(
        attend_kernel,
        "attend",
        [SMEM] + [VMEM] * 3,
        (shape((rows, 128)), shape((rows, 128)), shape((64, 512), f32), shape((1, 512), f32)),
        [
            pltpu.VMEM((128, 512), bf16),
            pltpu.VMEM((1, 512), f32),
            pltpu.VMEM((1, 512), f32),
            pltpu.VMEM((128, 512), f32),
        ],
    )(at, q_own, q_other, kv)
    ctx_got = lax.ppermute(ctx_give, "ctx", PARTNER)
    context_t, mix_keep, mix_give = on_device(
        mix_kernel,
        "mix",
        [SMEM] + [VMEM] * 3,
        (shape((256, rows)), shape((64, width)), shape((64, width))),
    )(at, ctx_mine, ctx_got, w_out)
    mine, theirs = sum_over_wa(mix_keep, mix_give)
    middle, normed2, gates, outgoing = on_device(
        route_kernel,
        "route",
        [SMEM] + [VMEM] * 7,
        (
            shape((rows, width), f32),
            shape((rows, width)),
            shape((experts, rows), f32),
            shape((2048, 512)),
        ),
    )(at, tokens, mine, theirs, gain2, router_t, rank, cot_quarter)

    outgoing, w_across, w_beside, w_diagonal = lax.optimization_barrier(
        (outgoing, w_across, w_beside, w_diagonal)
    )
    arrived = exchange(outgoing.reshape(128, 16, 512), ("ctx", "wa")).reshape(32, 4, 16, 512)
    returning, active, d_gate, d_up = on_device(
        expert_kernel,
        "experts",
        [VMEM] * 5,
        (shape((32, 4, 16, 512)), shape((512, 512)), shape((512, 512)), shape((512, 512))),
        [pltpu.VMEM((width, 512), bf16), pltpu.VMEM((width, 512), bf16), pltpu.VMEM((512, width), bf16)],
        megabytes=24,
    )(arrived, weights, w_across, w_beside, w_diagonal)
    back = exchange(returning.reshape(128, 16, 512), ("ctx", "wa")).reshape(2048, 512)
    near, far = on_device(
        expert_grad_kernel,
        "expert_grads",
        [VMEM] * 4,
        (shape((2, 3, width, 128)), shape((2, 3, width, 128))),
        flops=3_000_000_000,
    )(arrived, active, d_gate, d_up)
    far = lax.ppermute(far, "wa", CORE_SWAP)
    near = near.astype(f32) + far.astype(f32)
    near_own, near_give = near[0], near[1].astype(bf16)
    back, near_own, near_give = lax.optimization_barrier((back, near_own, near_give))
    sent, moe = on_device(
        combine_kernel,
        "combine",
        [VMEM] * 4,
        (shape((144, 256)), shape((rows, 256))),
        [pltpu.VMEM((32, 128), f32)],
    )(back, rank, gates, cot_quarter)

    pieces = pieces_over_wa(sent)
    pieces, moe, near_give = lax.optimization_barrier((pieces, moe, near_give))
    near_got = lax.ppermute(near_give, "wa", CHIP_SWAP)
    d_middle, do_own, do_give, parts = on_device(
        second_norm_kernel,
        "second_norm",
        [SMEM] + [VMEM] * 12,
        (
            shape((rows, width), f32),
            shape((rows, 128)),
            shape((rows, 128)),
            shape((32, 48, 256)),
        ),
        [pltpu.VMEM((rows, width), f32), pltpu.VMEM((32, 16, 256), f32)],
    )(
        at, sent, *pieces, gates, middle, normed2, cotangent, gain2, router_t, w_out, context_t
    )
    do_other = lax.ppermute(do_give, "ctx", PARTNER)

    angles2 = angles_of(ctx ^ 2)
    dq_own, dq_give, dkv = on_device(
        reverse_kernel,
        "reverse",
        [SMEM] + [VMEM] * 11,
        (shape((rows, 128)), shape((rows, 128)), shape((32, rows, 128))),
        [
            pltpu.VMEM((128, 512), bf16),
            pltpu.VMEM((128, 512), bf16),
            pltpu.VMEM((1, 512), f32),
            pltpu.VMEM((128, 512), f32),
        ],
    )(
        at, q_own, q_other, kv, do_own, do_other, context_o, lse,
        cos_rows, sin_rows, jnp.cos(angles2).T, jnp.sin(angles2).T,
    )
    dkv, near_got = lax.optimization_barrier((dkv, near_got))
    kv_back = exchange(dkv, "ctx")

    dq_got = lax.ppermute(dq_give, "ctx", PARTNER)
    d_query = jnp.where(
        side == 0, jnp.concatenate([dq_own, dq_got], 0), jnp.concatenate([dq_got, dq_own], 0)
    ).T
    parts_query = dot_tn(normed1, d_query).astype(bf16).reshape(32, 32, 256)
    first_query = dot_nt(d_query, w_query)
    kv_back, parts_query, first_query = lax.optimization_barrier((kv_back, parts_query, first_query))

    parts_all, first_keep, first_give = on_device(
        late_kernel,
        "late",
        [SMEM] + [VMEM] * 9,
        (shape((32, 112, 256)), shape((64, width)), shape((64, width))),
    )(
        at, kv_back, cos_lanes, sin_lanes, normed1, key_weight, value_weight, first_query,
        parts_query, parts,
    )
    parts_all, moe = lax.optimization_barrier((parts_all, moe))
    summed = exchange(parts_all, "ctx")
    moe_all = jnp.stack((moe,) + pieces_over_wa(moe))
    moe_all = moe_all.reshape(2, 2, rows, 256)
    moe_all = jnp.where(core == 0, moe_all, moe_all[::-1])
    moe_all = jnp.where(chip == 0, moe_all, moe_all[:, ::-1])
    moe_sum = moe_all.transpose(2, 1, 0, 3).reshape(rows, width).astype(f32)
    output = (middle + moe_sum).astype(bf16)
    near_all = near_own + near_got.astype(f32)
    g_down = near_all[2].reshape(8, 128, 128).transpose(1, 0, 2).reshape(128, width)
    first_mine, first_theirs = sum_over_wa(first_keep, first_give)
    d_first = jnp.where(
        core == 0, jnp.stack([first_mine, first_theirs]), jnp.stack([first_theirs, first_mine])
    ).reshape(rows, width).astype(f32)
    widened = tokens.astype(f32)
    root_first = lax.rsqrt(jnp.mean(widened * widened, -1, keepdims=True) + epsilon)
    unit_first = widened * root_first
    scaled_first = d_first * norm1_gain
    grad_gain_first = jnp.sum(d_first * unit_first, 0).astype(bf16).reshape(4, 256)
    grad_tokens = (
        d_middle
        + root_first
        * (scaled_first - unit_first * jnp.mean(scaled_first * unit_first, -1, keepdims=True))
    ).astype(bf16)
    shared, out_gain2 = on_device(
        share_kernel,
        "share",
        [VMEM] * 2,
        (shape((32, 112, 256)), shape((4, 256), f32)),
        [pltpu.VMEM((112, 256), f32)],
    )(summed, grad_gain_first)
    spread_out = exchange(shared, "ctx").astype(f32)

    out_query = spread_out[:, 0:32].reshape(width, 256)
    out_out = spread_out[:, 32:64].reshape(4, 256, 256).transpose(1, 0, 2).reshape(256, width)
    out_router = spread_out[:, 64:68].reshape(experts, width).T
    return (
        output,
        grad_tokens,
        jnp.sum(spread_out[:, 68:72], 0).reshape(width),
        out_query,
        spread_out[:, 80:112, :128].reshape(width, 128),
        spread_out[:, 80:112, 128:].reshape(width, 128),
        out_out,
        out_gain2.reshape(width),
        out_router,
        near_all[0][None],
        near_all[1][None],
        g_down[None],
    )


def solution(mesh):
    in_specs = (
        P("ctx", None),
        P(),
        P(None, "wa"),
        P(None, "wa"),
        P(None, "wa"),
        P("wa", None),
        P(),
        P(),
        P("ctx", None, "wa"),
        P("ctx", None, "wa"),
        P("ctx", "wa", None),
        P("ctx", None),
        P("ctx", None),
    )
    out_specs = (
        P("ctx", None),
        P("ctx", None),
        P(),
        P(None, "wa"),
        P(None, "wa"),
        P(None, "wa"),
        P("wa", None),
        P(),
        P(),
        P("ctx", None, "wa"),
        P("ctx", None, "wa"),
        P("ctx", "wa", None),
    )
    return jax.shard_map(local, mesh=mesh, in_specs=in_specs, out_specs=out_specs, check_vma=False)
```

```python
import jax
import jax.numpy as jnp
from jax import lax
from jax.experimental import pallas as pl
from jax.experimental.pallas import tpu as pltpu
from jax.sharding import PartitionSpec as P

HEAD_DIM = 64
CHUNK = 8

epsilon = 1e-06
f32 = jnp.float32
bf16 = jnp.bfloat16
CORE_SWAP = [(0, 1), (1, 0), (2, 3), (3, 2)]
CHIP_SWAP = [(0, 2), (2, 0), (1, 3), (3, 1)]
PARTNER = [(i, i ^ 2) for i in range(32)]
def dot(a, b):
    return jnp.dot(a, b, preferred_element_type=f32)


def dot_nt(a, b):
    return lax.dot_general(a, b, (((1,), (1,)), ((), ())), preferred_element_type=f32)


def dot_tn(a, b):
    return lax.dot_general(a, b, (((0,), (0,)), ((), ())), preferred_element_type=f32)


def exchange(value, axes):
    return lax.all_to_all(value, axes, split_axis=0, concat_axis=0, tiled=True)


def shape(dims, dtype=bf16):
    return jax.ShapeDtypeStruct(dims, dtype)


def on_device(kernel, name, ins, outs, scratch=(), megabytes=16, us=1.0, lazy=False, aliases=None):
    spaces = {"V": pltpu.VMEM, "F": pltpu.HBM, "Q": pltpu.HBM, "H": pltpu.HBM, "S": pltpu.HBM}
    fetched = [n for n, kind in enumerate(ins) if kind in "FQ"]
    staged = [n for n, (kind, _) in enumerate(outs) if kind == "S"]

    def call(*operands):
        def held(n):
            dims = operands[n].shape
            return pltpu.VMEM((dims[0], 256) if ins[n] == "Q" else dims, operands[n].dtype)

        buffers = [held(n) for n in fetched]
        stages = [pltpu.VMEM(outs[n][1].shape, outs[n][1].dtype) for n in staged]

        def body(*refs):
            refs = list(refs)
            in_refs, refs = refs[: len(ins)], refs[len(ins) :]
            out_refs, refs = refs[: len(outs)], refs[len(outs) :]
            own, refs = refs[: len(scratch)], refs[len(scratch) :]
            held_refs, refs = refs[: len(buffers)], refs[len(buffers) :]
            stage_refs, sems = refs[: len(stages)], refs[len(stages)]
            copies = []
            for k, n in enumerate(fetched):
                source = in_refs[n]
                if ins[n] == "Q":
                    quarter = lax.axis_index("wa").astype(jnp.int32) * 256
                    source = source.at[:, pl.ds(pl.multiple_of(quarter, 256), 256)]
                copies.append(pltpu.make_async_copy(source, held_refs[k], sems.at[k]))
                in_refs[n] = held_refs[k]
            for copy in copies:
                copy.start()
            pending = {}
            for k, n in enumerate(staged):
                pending[n] = pltpu.make_async_copy(stage_refs[k], out_refs[n], sems.at[len(buffers) + k])
                out_refs[n] = stage_refs[k]
            sent = set()

            def send(n):
                if n in pending:
                    pending[n].start()
                    sent.add(n)

            if lazy:
                kernel(*in_refs, *out_refs, *own, send=send, ready=lambda n: copies[fetched.index(n)].wait())
            else:
                for copy in copies:
                    copy.wait()
                kernel(*in_refs, *out_refs, *own, send=send)
            for n in staged:
                if n not in sent:
                    send(n)
            for n in staged:
                pending[n].wait()

        return pl.pallas_call(
            body,
            out_shape=tuple(o for _, o in outs),
            in_specs=[pl.BlockSpec(memory_space=spaces[kind]) for kind in ins],
            out_specs=tuple(pl.BlockSpec(memory_space=spaces[kind]) for kind, _ in outs),
            scratch_shapes=[
                *scratch,
                *buffers,
                *stages,
                pltpu.SemaphoreType.DMA((max(1, len(buffers) + len(stages)),)),
            ],
            compiler_params=pltpu.CompilerParams(vmem_limit_bytes=megabytes * 1024 * 1024),
            cost_estimate=pl.CostEstimate(flops=int(us * 1.1e9), bytes_accessed=0, transcendentals=0),
            name=name,
            input_output_aliases=aliases or {},
        )(*operands)

    return call


def places():
    ctx = lax.axis_index("ctx").astype(jnp.int32)
    wa = lax.axis_index("wa").astype(jnp.int32)
    return ctx, (ctx >> 1) & 1, wa, wa & 1


def local_positions(first_row, row_count, device_rows, group_count):
    numbers = first_row + jnp.arange(row_count, dtype=jnp.int32)
    owner_index = numbers // device_rows
    within = numbers % device_rows
    halfway = device_rows // 2
    return jnp.where(
        within < halfway,
        owner_index * halfway + within,
        (2 * group_count - 1 - owner_index) * halfway + within - halfway,
    )


def angles_of(block):
    positions = local_positions(block * 128, 128, 128, 32)
    inverse = jnp.power(10000.0, -2.0 * jnp.arange(32, dtype=f32) / HEAD_DIM)
    return positions.astype(f32)[:, None] * inverse[None, :]


def lanes_of(dims):
    return lax.broadcasted_iota(jnp.int32, dims, len(dims) - 1)


def swap_halves(x):
    return pltpu.roll(x, 64, 1)


def turn_lanes(x, cosine, sine):
    lead = (lanes_of(x.shape) & 63) < 32
    return x * cosine + jnp.where(lead, pltpu.roll(x, 96, 1), pltpu.roll(x, 32, 1)) * sine


def turn_rows(x, cosine, sine):
    lead, trail = x[0:32], x[32:64]
    return jnp.concatenate([lead * cosine - trail * sine, trail * cosine + lead * sine], 0)


def prelude_kernel(
    tokens_ref, gain_ref, wq_ref, wk_ref, wv_ref, cos_ref, sin_ref, cos_t_ref, sin_t_ref,
    kv_ref, normed_ref, q_ref, q_give_ref, *, send, ready
):
    _, side, _, _ = places()
    ready(0)
    ready(1)
    x = tokens_ref[...].astype(f32)
    root = lax.rsqrt(jnp.mean(x * x, -1, keepdims=True) + epsilon)
    normed = (x * root * gain_ref[...]).astype(bf16)
    normed_ref[...] = normed
    send(1)
    ready(3)
    k = dot(normed, wk_ref[...])
    ready(4)
    v = dot(normed, wv_ref[...])
    low = lanes_of(k.shape) < 64
    heads = (
        jnp.where(low, k, swap_halves(v)),
        jnp.where(low, swap_halves(k), v),
    )
    heads = [turn_lanes(y, cos_ref[...], sin_ref[...]).astype(bf16) for y in heads]
    for d in range(32):
        kv_ref[d] = heads[(d >> 1) & 1]
    send(0)
    ready(2)
    qt = dot(normed, wq_ref[...]).T
    turned = [
        turn_rows(qt[64 * h : 64 * h + 64], cos_t_ref[...], sin_t_ref[...]).astype(bf16) * jnp.asarray(1.0 / HEAD_DIM, bf16)
        for h in range(4)
    ]
    pairs = [jnp.concatenate(turned[2 * j : 2 * j + 2], 0).astype(f32) for j in range(2)]
    q_ref[...] = jnp.where(side == 0, pairs[0], pairs[1]).astype(bf16)
    q_give_ref[...] = jnp.where(side == 0, pairs[1], pairs[0]).astype(bf16)


def to_columns(side, own_ref, other_ref, out_ref, first_row):
    for g in range(2):
        own = own_ref[64 * g : 64 * g + 64, :].astype(f32)
        other = other_ref[64 * g : 64 * g + 64, :].astype(f32)
        zero = jnp.where(side == 0, own, other)
        one = jnp.where(side == 0, other, own)
        low = lanes_of(own.shape) < 64
        out_ref[first_row : first_row + 64, 128 * g : 128 * g + 128] = jnp.where(
            low, zero, swap_halves(one)
        ).astype(bf16)
        out_ref[first_row : first_row + 64, 256 + 128 * g : 384 + 128 * g] = jnp.where(
            low, swap_halves(zero), one
        ).astype(bf16)


def from_columns(side, columns, g):
    a = columns[:, 128 * g : 128 * g + 128]
    b = columns[:, 256 + 128 * g : 384 + 128 * g]
    low = lanes_of(a.shape) < 64
    zero = jnp.where(low, a, swap_halves(b))
    one = jnp.where(low, swap_halves(a), b)
    return jnp.where(side == 0, zero, one), jnp.where(side == 0, one, zero)


def masked_early(scores, base, c):
    rows = lax.broadcasted_iota(jnp.int32, scores.shape, 0) + base * 64
    columns = lanes_of(scores.shape)
    block = (c & 29) + ((columns >> 6) & 1) * 2
    return jnp.where(rows <= block * 64 + (columns & 63), scores, -1e30)


def masked_late(scores, base, c):
    rows = lax.broadcasted_iota(jnp.int32, scores.shape, 0)
    columns = lanes_of(scores.shape)
    block = (c & 29) + ((columns >> 6) & 1) * 2
    key_at = (63 - base - (rows >> 6)) * 64 + (rows & 63)
    return jnp.where(key_at <= (63 - block) * 64 + (columns & 63), scores, -1e30)


def attend_kernel(
    own_ref, other_ref, kv_ref,
    mine_ref, give_ref, o_ref,
    q_ref, m_ref, l_ref, acc_ref, *, send
):
    c, side, _, _ = places()
    to_columns(side, own_ref, other_ref, q_ref, 0)
    q_ref[64:128, :] = jnp.zeros((64, 512), bf16)
    m_ref[...] = jnp.full(m_ref.shape, -1e30, f32)
    l_ref[...] = jnp.zeros(l_ref.shape, f32)
    acc_ref[...] = jnp.zeros(acc_ref.shape, f32)

    def step(base, keys_half, cols, mask):
        kv = kv_ref[base : base + CHUNK, keys_half, :].reshape(CHUNK * 64, 128)
        s = dot(kv, q_ref[:, cols])
        if mask is not None:
            s = mask(s, base, c)
        m_old = m_ref[:, cols]
        m_new = jnp.maximum(m_old, jnp.max(s, 0, keepdims=True))
        p = jnp.exp(s - m_new)
        factor = jnp.exp(m_old - m_new)
        m_ref[:, cols] = m_new
        l_ref[:, cols] = l_ref[:, cols] * factor + jnp.sum(p, 0, keepdims=True)
        acc_ref[:, cols] = acc_ref[:, cols] * factor + dot_tn(kv, p.astype(bf16))

    early, late = slice(0, 64), slice(64, 128)
    first, second = slice(0, 256), slice(256, 512)
    for base in range(0, 32, CHUNK):
        step(base, early, second, None)

        @pl.when(base <= (c | 2))
        def _():
            step(base, early, first, masked_early)

        @pl.when(base + CHUNK > (c & 29))
        def _():
            step(base, late, second, masked_late)

    total = l_ref[...]
    o_ref[0:64, :] = acc_ref[64:128, :] / total
    o_ref[64:72, :] = jnp.broadcast_to(m_ref[...] + jnp.log(total), (8, 512))
    send(2)
    for g in range(2):
        own, other = from_columns(side, o_ref[0:64, :], g)
        mine_ref[64 * g : 64 * g + 64, :] = own.astype(bf16)
        give_ref[64 * g : 64 * g + 64, :] = other.astype(bf16)


def reverse_kernel(
    own_ref, other_ref, kv_ref, do_own_ref, do_other_ref, o_ref,
    cos_ref, sin_ref, cos2_ref, sin2_ref,
    dq_ref, dq_give_ref, dkv_ref,
    q_ref, do_ref, delta_ref, acc_ref, *, send
):
    c, side, _, _ = places()
    to_columns(side, own_ref, other_ref, q_ref, 0)
    q_ref[64:128, :] = jnp.zeros((64, 512), bf16)
    to_columns(side, do_own_ref, do_other_ref, do_ref, 64)
    do_ref[0:64, :] = jnp.zeros((64, 512), bf16)
    delta_ref[...] = jnp.sum(do_ref[64:128, :].astype(f32) * o_ref[0:64, :], 0, keepdims=True)
    acc_ref[...] = jnp.zeros(acc_ref.shape, f32)

    def step(base, keys_half, cols, mask, add):
        kv = kv_ref[base : base + CHUNK, keys_half, :].reshape(CHUNK * 64, 128)
        q = q_ref[:, cols]
        do = do_ref[:, cols]
        s = dot(kv, q)
        if mask is not None:
            s = mask(s, base, c)
        p = jnp.exp(s - o_ref[64:65, cols])
        dp = dot(kv, do)
        ds = (p * (dp - delta_ref[:, cols])).astype(bf16)
        acc_ref[:, cols] += dot_tn(kv, ds)
        dkv = (dot_nt(ds, q) + dot_nt(p.astype(bf16), do)).reshape(CHUNK, 64, 128)
        if add:
            dkv += dkv_ref[base : base + CHUNK, keys_half, :].astype(f32)
        dkv_ref[base : base + CHUNK, keys_half, :] = dkv.astype(bf16)

    early, late = slice(0, 64), slice(64, 128)
    first, second = slice(0, 256), slice(256, 512)
    for base in range(0, 32, CHUNK):
        step(base, early, second, None, False)

        @pl.when(base <= (c | 2))
        def _():
            step(base, early, first, masked_early, True)

        @pl.when(base + CHUNK > (c & 29))
        def _():
            step(base, late, second, masked_late, False)

        @pl.when(base + CHUNK <= (c & 29))
        def _():
            dkv_ref[base : base + CHUNK, late, :] = jnp.zeros((CHUNK, 64, 128), bf16)

    for g in range(2):
        own, other = from_columns(side, acc_ref[0:64, :] * (1.0 / HEAD_DIM), g)
        here = slice(64 * g, 64 * g + 64)
        dq_ref[here, :] = turn_rows(own, cos_ref[...], -sin_ref[...]).astype(bf16)
        dq_give_ref[here, :] = turn_rows(other, cos2_ref[...], -sin2_ref[...]).astype(bf16)


def mix_kernel(mine_ref, got_ref, w_out_ref, context_ref, keep_ref, give_ref, *, send
):
    _, side, _, core = places()
    mine, got = mine_ref[...].astype(f32), got_ref[...].astype(f32)
    context_ref[0:128, :] = jnp.where(side == 0, mine, got).astype(bf16)
    context_ref[128:256, :] = jnp.where(side == 0, got, mine).astype(bf16)
    send(0)
    mixed = dot_tn(context_ref[...], w_out_ref[...])
    top, bottom = mixed[0:64], mixed[64:128]
    keep_ref[...] = jnp.where(core == 0, top, bottom).astype(bf16)
    give_ref[...] = jnp.where(core == 0, bottom, top).astype(bf16)


def selection(rank_ref, first, count):
    slot = lax.broadcasted_iota(jnp.int32, (64, 128), 0).astype(f32)
    return jnp.concatenate([(slot == rank_ref[e : e + 1, :]).astype(f32) for e in range(first, first + count)], 0)


def route_kernel(
    tokens_ref, mine_ref, theirs_ref, gain_ref, router_ref, rank_ref, cot_ref,
    middle_ref, normed_ref, gates_ref, out_ref, *, send
):
    _, _, wa, core = places()
    for half in range(2):
        here = slice(64 * half, 64 * half + 64)
        mixed = jnp.where(core == half, mine_ref[...].astype(f32), theirs_ref[...].astype(f32))
        middle = tokens_ref[here, :].astype(f32) + mixed
        middle_ref[here, :] = middle
        root = lax.rsqrt(jnp.mean(middle * middle, -1, keepdims=True) + epsilon)
        normed_ref[here, :] = (middle * root * gain_ref[...]).astype(bf16)
    send(0)
    send(1)
    logits = dot_nt(router_ref[...], normed_ref[...])
    member = rank_ref[...] >= 0.0
    top = jnp.max(jnp.where(member, logits, -1e30), 0, keepdims=True)
    raised = jnp.where(member, jnp.exp(jnp.where(member, logits - top, 0.0)), 0.0)
    gates_ref[0:32, :] = raised / jnp.sum(raised, 0, keepdims=True)
    gates_ref[32:64, :] = rank_ref[...]
    send(2)
    quarter = normed_ref[:, pl.ds(pl.multiple_of(wa * 256, 256), 256)]
    for first in range(0, 32, 4):
        chosen = selection(rank_ref, first, 4)
        weights = jnp.concatenate(
            [
                jnp.sum(chosen[64 * n : 64 * n + 64] * gates_ref[first + n : first + n + 1, :], 1, keepdims=True)
                for n in range(4)
            ],
            0,
        )
        chosen = chosen.astype(bf16)
        here = slice(64 * first, 64 * first + 256)
        out_ref[here, 0:256] = dot(chosen, quarter).astype(bf16)
        out_ref[here, 256:512] = (weights * dot(chosen, cot_ref[...])).astype(bf16)


def expert_kernel(
    in_ref, w0_ref, w1_ref, w2_ref, w3_ref, d0_ref, d1_ref, d2_ref, d3_ref,
    out_ref, hidden_ref,
    gate_ref, up_ref, down_ref, *, send
):
    downs = (d0_ref, d1_ref, d2_ref, d3_ref)
    for p, w in enumerate((w0_ref, w1_ref, w2_ref, w3_ref)):
        here = slice(128 * p, 128 * p + 128)
        gate_ref[:, here] = w[0]
        up_ref[:, here] = w[1]
        for n in range(8):
            down_ref[here, 128 * n : 128 * n + 128] = downs[p][128 * n : 128 * n + 128, :]
    act_ref, dgate_ref, dup_ref = (hidden_ref.at[:, 512 * n : 512 * n + 512] for n in range(3))
    gate_pre = jnp.zeros((512, 512), f32)
    up_pre = jnp.zeros((512, 512), f32)
    d_act = jnp.zeros((512, 512), f32)
    for q in range(4):
        here = slice(256 * q, 256 * q + 256)
        x = in_ref[:, q, :, 0:256].reshape(512, 256)
        gate_pre += dot(x, gate_ref[here, :])
        up_pre += dot(x, up_ref[here, :])
        d_act += dot_nt(in_ref[:, q, :, 256:512].reshape(512, 256), down_ref[:, here])
    sigma = jax.nn.sigmoid(gate_pre)
    act_ref[...] = (gate_pre * sigma * up_pre).astype(bf16)
    dgate_ref[...] = (d_act * up_pre * sigma * (1.0 + gate_pre * (1.0 - sigma))).astype(bf16)
    dup_ref[...] = (d_act * gate_pre * sigma).astype(bf16)
    for q in range(4):
        here = slice(256 * q, 256 * q + 256)
        part = dot(act_ref[...], down_ref[:, here])
        out_ref[:, q, :, 0:256] = part.astype(bf16).reshape(32, 16, 256)
        d_x = dot_nt(dgate_ref[...], gate_ref[here, :]) + dot_nt(dup_ref[...], up_ref[here, :])
        out_ref[:, q, :, 256:512] = d_x.astype(bf16).reshape(32, 16, 256)


def expert_grad_kernel(in_ref, hidden_ref, near_ref, far_ref, *, send):
    act_ref, dgate_ref, dup_ref = (hidden_ref.at[:, 512 * n : 512 * n + 512] for n in range(3))
    for q in range(4):
        here = slice(256 * q, 256 * q + 256)
        x = in_ref[:, q, :, 0:256].reshape(512, 256)
        d = in_ref[:, q, :, 256:512].reshape(512, 256)
        g_gate = dot_tn(x, dgate_ref[...]).astype(bf16)
        g_up = dot_tn(x, dup_ref[...]).astype(bf16)
        g_down = dot_tn(act_ref[...], d).astype(bf16)
        for p in range(4):
            to = near_ref if p < 2 else far_ref
            to[p % 2, 0, here, :] = g_gate[:, 128 * p : 128 * p + 128]
            to[p % 2, 1, here, :] = g_up[:, 128 * p : 128 * p + 128]
            for n in range(2):
                at = 256 * q + 128 * n
                to[p % 2, 2, at : at + 128, :] = g_down[128 * p : 128 * p + 128, 128 * n : 128 * n + 128]


def combine_kernel(back_ref, gates_ref, cot_ref, sent_ref, dgates_ref, *, send
):
    rank_ref = gates_ref.at[32:64, :]
    d_normed = jnp.zeros((128, 256), f32)
    moe = jnp.zeros((128, 256), f32)
    for first in range(0, 32, 4):
        here = slice(64 * first, 64 * first + 256)
        chosen = selection(rank_ref, first, 4)
        gated = jnp.concatenate(
            [chosen[64 * n : 64 * n + 64] * gates_ref[first + n : first + n + 1, :] for n in range(4)], 0
        )
        high = gated.astype(bf16)
        low = (gated - high.astype(f32)).astype(bf16)
        picked = chosen.astype(bf16)
        part = back_ref[here, 0:256]
        d_normed += dot_tn(picked, back_ref[here, 256:512])
        moe += dot_tn(high, part) + dot_tn(low, part)
        along = jnp.sum(dot(picked, cot_ref[...]) * part.astype(f32), 1, keepdims=True)
        placed = chosen * along
        for n in range(4):
            dgates_ref[first + n : first + n + 1, :] = jnp.sum(
                placed[64 * n : 64 * n + 64], 0, keepdims=True
            )
    sent_ref[144:272, :] = moe.astype(bf16)
    sent_ref[0:128, :] = d_normed.astype(bf16)
    sent_ref[128:144, 0:128] = dgates_ref[0:16, :].astype(bf16)
    sent_ref[128:144, 128:256] = dgates_ref[16:32, :].astype(bf16)


def second_norm_kernel(
    own_ref, across_ref, beside_ref, diagonal_ref, gates_ref, middle_ref, normed_ref, cot_ref,
    gain_ref, router_ref, w_out_ref, context_ref,
    dmiddle_ref, dmine_ref, dgive_ref, parts_ref, output_ref, dnormed_ref, extra_ref, *, send
):
    _, side, wa, _ = places()
    pieces = [(own_ref, 0), (across_ref, 2), (beside_ref, 1), (diagonal_ref, 3)]
    for ref, flip in pieces:
        at = pl.multiple_of((wa ^ flip) * 256, 256)
        dnormed_ref[:, pl.ds(at, 256)] = ref[0:128, :].astype(f32)
        output_ref[:, pl.ds(at, 256)] = (
            middle_ref[:, pl.ds(at, 256)] + ref[144:272, :].astype(f32)
        ).astype(bf16)
    terms = [
        jnp.concatenate([ref[128:144, 0:128], ref[128:144, 128:256]], 0).astype(f32) for ref, _ in pieces
    ]
    d_gates = (terms[0] + terms[1]) + (terms[2] + terms[3])
    gates = gates_ref[0:32, :]
    d_logits = (gates * (d_gates - jnp.sum(gates * d_gates, 0, keepdims=True))).astype(bf16)
    gain = gain_ref[...]
    d_normed = dnormed_ref[...] + dot_tn(d_logits, router_ref[...])
    middle = middle_ref[...]
    root = lax.rsqrt(jnp.mean(middle * middle, -1, keepdims=True) + epsilon)
    unit = middle * root
    scaled = d_normed * gain
    gain_grad = jnp.sum(d_normed * unit, 0, keepdims=True)
    d_middle = cot_ref[...].astype(f32) + root * (
        scaled - unit * jnp.mean(scaled * unit, -1, keepdims=True)
    )
    dmiddle_ref[...] = d_middle
    send(0)
    d_mixed = d_middle.astype(bf16)
    d_context = dot_nt(w_out_ref[...], d_mixed)
    dmine_ref[...] = jnp.where(side == 0, d_context[0:128], d_context[128:256]).astype(bf16)
    dgive_ref[...] = jnp.where(side == 0, d_context[128:256], d_context[0:128]).astype(bf16)
    router_grad = dot(d_logits, normed_ref[...])
    extra_ref[...] = jnp.zeros(extra_ref.shape, f32)
    for q in range(4):
        here = slice(256 * q, 256 * q + 256)
        extra_ref[:, q, :] = router_grad[:, here]
        extra_ref[:, 4 + q, :] = jnp.broadcast_to(gain_grad[:, here], (32, 256))
        parts_ref[8 * q : 8 * q + 8, 0:32, :] = (
            dot(context_ref[...], d_mixed[:, here]).astype(bf16).reshape(8, 32, 256)
        )
    parts_ref[:, 32:48, :] = extra_ref[...].astype(bf16)


def late_kernel(
    back_ref, cos_ref, sin_ref, normed_ref, wk_ref, wv_ref, first_ref, filled_ref,
    parts_ref, keep_ref, give_ref,
    kv_ref, sems, *, send, ready
):
    _, _, _, core = places()
    move = pltpu.make_async_copy(kv_ref, parts_ref.at[:, 80:112, :], sems.at[0])
    ready(0)
    ready(1)
    ready(2)
    heads = []
    for j in range(2):
        total = jnp.zeros((128, 128), f32)
        for d in range(32):
            if (d >> 1) & 1 == j:
                total += back_ref[d].astype(f32)
        heads.append(turn_lanes(total, cos_ref[...], -sin_ref[...]))
    low = lanes_of((128, 128)) < 64
    d_k = jnp.where(low, heads[0], swap_halves(heads[1])).astype(bf16)
    d_v = jnp.where(low, swap_halves(heads[0]), heads[1]).astype(bf16)
    ready(3)
    kv_ref[:, :, 0:128] = dot_tn(normed_ref[...], d_k).astype(bf16).reshape(32, 32, 128)
    kv_ref[:, :, 128:256] = dot_tn(normed_ref[...], d_v).astype(bf16).reshape(32, 32, 128)
    move.start()
    ready(4)
    ready(5)
    ready(6)
    first = first_ref[...] + dot_nt(d_k, wk_ref[...]) + dot_nt(d_v, wv_ref[...])
    keep_ref[...] = jnp.where(core == 0, first[0:64], first[64:128]).astype(bf16)
    give_ref[...] = jnp.where(core == 0, first[64:128], first[0:64]).astype(bf16)
    move.wait()


def share_kernel(in_ref, gain_ref, out_ref, gain2_ref, total_ref, *, send):
    total_ref[...] = jnp.sum(in_ref[...].astype(f32), 0)
    for q in range(4):
        gain2_ref[:, 256 * q : 256 * q + 256] = total_ref[68 + q : 69 + q, :]
    total_ref[68:72, :] = gain_ref[...].astype(f32)
    out_ref[...] = jnp.broadcast_to(total_ref[...].astype(bf16)[None], (32, 112, 256))


def final_kernel(in_ref, query_ref, key_ref, value_ref, out_ref, router_ref, gain_ref, extra_ref, *, send):
    query_ref[...] = in_ref[:, 0:32, :].astype(f32).reshape(1024, 256)
    send(0)
    for q in range(4):
        here = slice(256 * q, 256 * q + 256)
        out_ref[:, here] = in_ref[8 * q : 8 * q + 8, 32:64, :].astype(f32).reshape(256, 256)
    send(3)
    key_ref[...] = in_ref[:, 80:112, 0:128].astype(f32).reshape(1024, 128)
    send(1)
    value_ref[...] = in_ref[:, 80:112, 128:256].astype(f32).reshape(1024, 128)
    send(2)
    extra_ref[...] = in_ref[:, 64:80, :].astype(f32)
    for q in range(4):
        router_ref[:, 256 * q : 256 * q + 256] = extra_ref[:, q, :]
    for q in range(4):
        gain_ref[:, 256 * q : 256 * q + 256] = jnp.sum(extra_ref[:, 4 + q, :], 0, keepdims=True)


def sum_over_wa(keep, give):
    got = lax.ppermute(give, "wa", CORE_SWAP)
    pair = (keep.astype(f32) + got.astype(f32)).astype(bf16)
    other = lax.ppermute(pair, "wa", CHIP_SWAP)
    mine = (pair.astype(f32) + other.astype(f32)).astype(bf16)
    return mine, lax.ppermute(mine, "wa", CORE_SWAP)


def pieces_over_wa(part):
    across = lax.ppermute(part, "wa", CHIP_SWAP)
    beside = lax.ppermute(part, "wa", CORE_SWAP)
    return across, beside, lax.ppermute(across, "wa", CORE_SWAP)


def local(
    tokens,
    norm1_gain,
    w_query,
    key_weight,
    value_weight,
    w_out,
    norm2_gain,
    w_router,
    w_gate,
    w_up,
    w_down,
    routes,
    cotangent,
):
    ctx = lax.axis_index("ctx").astype(jnp.int32)
    wa = lax.axis_index("wa").astype(jnp.int32)
    core, chip, side = wa % 2, wa // 2, (ctx >> 1) & 1
    rows, width, experts = 128, 1024, 32

    angles = angles_of(ctx)
    cosine, sine = jnp.cos(angles), jnp.sin(angles)
    one, zero = jnp.ones((rows, 64), f32), jnp.zeros((rows, 64), f32)
    cos_lanes = jnp.concatenate([cosine, cosine, one], 1)
    sin_lanes = jnp.concatenate([-sine, sine, zero], 1)
    cos_rows, sin_rows = cosine.T, sine.T
    gain1 = norm1_gain.reshape(1, width)
    kv_send, normed1, q_own, q_give = on_device(
        prelude_kernel,
        "prelude",
        "FFFFFVVVV",
        (
            ("S", shape((32, rows, 128))),
            ("S", shape((rows, width))),
            ("S", shape((rows, 128))),
            ("V", shape((rows, 128))),
        ),
        megabytes=56,
        us=2,
        lazy=True,
    )(tokens, gain1, w_query, key_weight, value_weight, cos_lanes, sin_lanes, cos_rows, sin_rows)
    kv = exchange(kv_send, "ctx")
    q_other = lax.ppermute(q_give, "ctx", PARTNER)

    member = jnp.any(
        routes[:, :, None] == jnp.arange(experts, dtype=jnp.int32)[None, None, :], axis=1
    )
    lower = (jnp.arange(rows)[:, None] >= jnp.arange(rows)[None, :]).astype(bf16)
    rank = jnp.where(member, dot(lower, member.astype(bf16)) - 1.0, -1.0).T
    router_t = w_router.T
    gain2 = norm2_gain.reshape(1, width)

    cot_quarter = lax.dynamic_slice_in_dim(cotangent, wa * 256, 256, 1)
    down_lanes = w_down[0].reshape(128, 8, 128).transpose(1, 0, 2).reshape(width, 128)
    weights = jnp.stack([w_gate[0], w_up[0]])
    down_across = lax.ppermute(down_lanes, "wa", CHIP_SWAP)
    kv, rank, q_other, weights, cot_quarter, down_across = lax.optimization_barrier(
        (kv, rank, q_other, weights, cot_quarter, down_across)
    )
    w_across, w_beside, w_diagonal = pieces_over_wa(weights)
    down_beside = lax.ppermute(down_lanes, "wa", CORE_SWAP)
    down_diagonal = lax.ppermute(down_across, "wa", CORE_SWAP)
    ctx_mine, ctx_give, context_o = on_device(
        attend_kernel,
        "attend",
        "VVV",
        (("V", shape((rows, 128))), ("V", shape((rows, 128))), ("V", shape((72, 512), f32))),
        [
            pltpu.VMEM((128, 512), bf16),
            pltpu.VMEM((1, 512), f32),
            pltpu.VMEM((1, 512), f32),
            pltpu.VMEM((128, 512), f32),
        ],
        us=0.5,
    )(q_own, q_other, kv)
    ctx_got = lax.ppermute(ctx_give, "ctx", PARTNER)
    context_t, mix_keep, mix_give = on_device(
        mix_kernel,
        "mix",
        "VVV",
        (("V", shape((256, rows))), ("V", shape((64, width))), ("V", shape((64, width)))),
        us=0.8,
    )(ctx_mine, ctx_got, w_out)
    mine, theirs = sum_over_wa(mix_keep, mix_give)
    middle, normed2, gates, outgoing = on_device(
        route_kernel,
        "route",
        "VVVVVVV",
        (
            ("V", shape((rows, width), f32)),
            ("V", shape((rows, width))),
            ("V", shape((2 * experts, rows), f32)),
            ("V", shape((2048, 512))),
        ),
        us=1.6,
    )(tokens, mine, theirs, gain2, router_t, rank, cot_quarter)

    outgoing, w_across, w_beside, w_diagonal, down_beside, down_diagonal = lax.optimization_barrier(
        (outgoing, w_across, w_beside, w_diagonal, down_beside, down_diagonal)
    )
    arrived = exchange(outgoing.reshape(128, 16, 512), ("ctx", "wa")).reshape(32, 4, 16, 512)
    returning, hidden = on_device(
        expert_kernel,
        "experts",
        "VVVVVVVVV",
        (("V", shape((32, 4, 16, 512))), ("V", shape((512, 1536)))),
        [pltpu.VMEM((width, 512), bf16), pltpu.VMEM((width, 512), bf16), pltpu.VMEM((512, width), bf16)],
        megabytes=24,
        us=5,
    )(
        arrived, weights, w_across, w_beside, w_diagonal,
        down_lanes, down_across, down_beside, down_diagonal,
    )
    back = exchange(returning.reshape(128, 16, 512), ("ctx", "wa")).reshape(2048, 512)
    near, far = on_device(
        expert_grad_kernel,
        "expert_grads",
        "VV",
        (("V", shape((2, 3, width, 128))), ("V", shape((2, 3, width, 128)))),
        us=3,
    )(arrived, hidden)
    far = lax.ppermute(far, "wa", CORE_SWAP)
    near_sum = near.astype(f32) + far.astype(f32)
    near_own, near_give = near_sum[0], near_sum[1].astype(bf16)
    back, near_own, near_give = lax.optimization_barrier((back, near_own, near_give))
    (sent,) = on_device(
        combine_kernel,
        "combine",
        "VVV",
        (("V", shape((272, 256))),),
        [pltpu.VMEM((32, 128), f32)],
        us=1,
    )(back, gates, cot_quarter)

    pieces = pieces_over_wa(sent)
    pieces, near_two = lax.optimization_barrier((pieces, near_give[:2]))
    near_got = lax.ppermute(near_two, "wa", CHIP_SWAP)
    d_middle, do_own, do_give, parts, output = on_device(
        second_norm_kernel,
        "second_norm",
        "VVVVVVVVVVVV",
        (
            ("V", shape((rows, width), f32)),
            ("V", shape((rows, 128))),
            ("V", shape((rows, 128))),
            ("V", shape((32, 48, 256))),
            ("V", shape((rows, width))),
        ),
        [pltpu.VMEM((rows, width), f32), pltpu.VMEM((32, 16, 256), f32)],
        us=1.6,
    )(sent, *pieces, gates, middle, normed2, cotangent, gain2, router_t, w_out, context_t)
    do_other = lax.ppermute(do_give, "ctx", PARTNER)

    angles2 = angles_of(ctx ^ 2)
    dq_own, dq_give, dkv = on_device(
        reverse_kernel,
        "reverse",
        "VVVVVVVVVV",
        (("V", shape((rows, 128))), ("V", shape((rows, 128))), ("V", shape((32, rows, 128)))),
        [
            pltpu.VMEM((128, 512), bf16),
            pltpu.VMEM((128, 512), bf16),
            pltpu.VMEM((1, 512), f32),
            pltpu.VMEM((128, 512), f32),
        ],
        us=1,
    )(
        q_own, q_other, kv, do_own, do_other, context_o,
        cos_rows, sin_rows, jnp.cos(angles2).T, jnp.sin(angles2).T,
    )
    dkv, near_got, near_last = lax.optimization_barrier((dkv, near_got, near_give[2]))
    kv_back = exchange(dkv, "ctx")
    near_last = lax.ppermute(near_last, "wa", CHIP_SWAP)

    dq_got = lax.ppermute(dq_give, "ctx", PARTNER)
    dq_got, near_last = lax.optimization_barrier((dq_got, near_last))
    d_query = jnp.where(
        side == 0, jnp.concatenate([dq_own, dq_got], 0), jnp.concatenate([dq_got, dq_own], 0)
    ).T
    parts_query = dot_tn(normed1, d_query).astype(bf16).reshape(32, 32, 256)
    first_query = dot_nt(d_query, w_query)
    filled = jnp.concatenate([parts_query, parts, jnp.zeros((32, 32, 256), bf16)], 1)
    kv_back, filled, first_query = lax.optimization_barrier((kv_back, filled, first_query))
    parts_all, first_keep, first_give = on_device(
        late_kernel,
        "late",
        "FFFFFFFH",
        (("H", shape((32, 112, 256))), ("V", shape((64, width))), ("V", shape((64, width)))),
        [pltpu.VMEM((32, 32, 256), bf16), pltpu.SemaphoreType.DMA((1,))],
        megabytes=56,
        us=1.3,
        lazy=True,
        aliases={7: 0},
    )(kv_back, cos_lanes, sin_lanes, normed1, key_weight, value_weight, first_query, filled)
    summed = exchange(parts_all, "ctx")

    first_mine, first_theirs = sum_over_wa(first_keep, first_give)
    d_first = jnp.where(
        core == 0, jnp.stack([first_mine, first_theirs]), jnp.stack([first_theirs, first_mine])
    ).reshape(rows, width).astype(f32)
    widened = tokens.astype(f32)
    root_first = lax.rsqrt(jnp.mean(widened * widened, -1, keepdims=True) + epsilon)
    unit_first = widened * root_first
    scaled_first = d_first * norm1_gain
    grad_gain_first = jnp.sum(d_first * unit_first, 0).astype(bf16).reshape(4, 256)
    shared, out_gain2 = on_device(
        share_kernel,
        "share",
        "VV",
        (("V", shape((32, 112, 256))), ("V", shape((1, width), f32))),
        [pltpu.VMEM((112, 256), f32)],
        us=0.5,
    )(summed, grad_gain_first)
    shared, d_first = lax.optimization_barrier((shared, d_first))
    spread_out = exchange(shared, "ctx")

    grad_tokens = (
        d_middle
        + root_first
        * (scaled_first - unit_first * jnp.mean(scaled_first * unit_first, -1, keepdims=True))
    ).astype(bf16)
    g_gate = near_own[0] + near_got[0].astype(f32)
    g_up = near_own[1] + near_got[1].astype(f32)
    g_down = (near_own[2] + near_last.astype(f32)).reshape(8, 128, 128)
    g_down = g_down.transpose(1, 0, 2).reshape(128, width)
    spread_out, output, grad_tokens, g_gate, g_up, g_down = lax.optimization_barrier(
        (spread_out, output, grad_tokens, g_gate, g_up, g_down)
    )
    out_query, out_key, out_value, out_out, out_router, out_gain1 = on_device(
        final_kernel,
        "final",
        "V",
        (
            ("S", shape((width, 256), f32)),
            ("S", shape((width, 128), f32)),
            ("S", shape((width, 128), f32)),
            ("S", shape((256, width), f32)),
            ("S", shape((experts, width), f32)),
            ("S", shape((1, width), f32)),
        ),
        [pltpu.VMEM((32, 16, 256), f32)],
        us=1.8,
    )(spread_out)
    return (
        output,
        grad_tokens,
        out_gain1.reshape(width),
        out_query,
        out_key,
        out_value,
        out_out,
        out_gain2.reshape(width),
        out_router.T,
        g_gate[None],
        g_up[None],
        g_down[None],
    )


def solution(mesh):
    in_specs = (
        P("ctx", None),
        P(),
        P(None, "wa"),
        P(None, "wa"),
        P(None, "wa"),
        P("wa", None),
        P(),
        P(),
        P("ctx", None, "wa"),
        P("ctx", None, "wa"),
        P("ctx", "wa", None),
        P("ctx", None),
        P("ctx", None),
    )
    out_specs = (
        P("ctx", None),
        P("ctx", None),
        P(),
        P(None, "wa"),
        P(None, "wa"),
        P(None, "wa"),
        P("wa", None),
        P(),
        P(),
        P("ctx", None, "wa"),
        P("ctx", None, "wa"),
        P("ctx", "wa", None),
    )
    return jax.shard_map(local, mesh=mesh, in_specs=in_specs, out_specs=out_specs, check_vma=False)
```

```python
import jax
import jax.numpy as jnp
from jax import lax
from jax.experimental import pallas as pl
from jax.experimental.pallas import tpu as pltpu
from jax.sharding import PartitionSpec as P

HEAD_DIM = 64
CHUNK = 8

epsilon = 1e-06
f32 = jnp.float32
bf16 = jnp.bfloat16
CORE_SWAP = [(0, 1), (1, 0), (2, 3), (3, 2)]
CHIP_SWAP = [(0, 2), (2, 0), (1, 3), (3, 1)]
PARTNER = [(i, i ^ 2) for i in range(32)]
def dot(a, b):
    return jnp.dot(a, b, preferred_element_type=f32)


def dot_nt(a, b):
    return lax.dot_general(a, b, (((1,), (1,)), ((), ())), preferred_element_type=f32)


def dot_tn(a, b):
    return lax.dot_general(a, b, (((0,), (0,)), ((), ())), preferred_element_type=f32)


def exchange(value, axes):
    return lax.all_to_all(value, axes, split_axis=0, concat_axis=0, tiled=True)


def shape(dims, dtype=bf16):
    return jax.ShapeDtypeStruct(dims, dtype)


def on_device(kernel, name, ins, outs, scratch=(), megabytes=16, us=1.0, lazy=False, aliases=None):
    spaces = {"V": pltpu.VMEM, "F": pltpu.HBM, "Q": pltpu.HBM, "H": pltpu.HBM, "S": pltpu.HBM}
    fetched = [n for n, kind in enumerate(ins) if kind in "FQ"]
    staged = [n for n, (kind, _) in enumerate(outs) if kind == "S"]

    def call(*operands):
        def held(n):
            dims = operands[n].shape
            return pltpu.VMEM((dims[0], 256) if ins[n] == "Q" else dims, operands[n].dtype)

        buffers = [held(n) for n in fetched]
        stages = [pltpu.VMEM(outs[n][1].shape, outs[n][1].dtype) for n in staged]

        def body(*refs):
            refs = list(refs)
            in_refs, refs = refs[: len(ins)], refs[len(ins) :]
            out_refs, refs = refs[: len(outs)], refs[len(outs) :]
            own, refs = refs[: len(scratch)], refs[len(scratch) :]
            held_refs, refs = refs[: len(buffers)], refs[len(buffers) :]
            stage_refs, sems = refs[: len(stages)], refs[len(stages)]
            copies = []
            for k, n in enumerate(fetched):
                source = in_refs[n]
                if ins[n] == "Q":
                    quarter = lax.axis_index("wa").astype(jnp.int32) * 256
                    source = source.at[:, pl.ds(pl.multiple_of(quarter, 256), 256)]
                copies.append(pltpu.make_async_copy(source, held_refs[k], sems.at[k]))
                in_refs[n] = held_refs[k]
            for copy in copies:
                copy.start()
            pending = {}
            for k, n in enumerate(staged):
                pending[n] = pltpu.make_async_copy(stage_refs[k], out_refs[n], sems.at[len(buffers) + k])
                out_refs[n] = stage_refs[k]
            sent = set()

            def send(n):
                if n in pending:
                    pending[n].start()
                    sent.add(n)

            if lazy:
                kernel(*in_refs, *out_refs, *own, send=send, ready=lambda n: copies[fetched.index(n)].wait())
            else:
                for copy in copies:
                    copy.wait()
                kernel(*in_refs, *out_refs, *own, send=send)
            for n in staged:
                if n not in sent:
                    send(n)
            for n in staged:
                pending[n].wait()

        return pl.pallas_call(
            body,
            out_shape=tuple(o for _, o in outs),
            in_specs=[pl.BlockSpec(memory_space=spaces[kind]) for kind in ins],
            out_specs=tuple(pl.BlockSpec(memory_space=spaces[kind]) for kind, _ in outs),
            scratch_shapes=[
                *scratch,
                *buffers,
                *stages,
                pltpu.SemaphoreType.DMA((max(1, len(buffers) + len(stages)),)),
            ],
            compiler_params=pltpu.CompilerParams(vmem_limit_bytes=megabytes * 1024 * 1024),
            cost_estimate=pl.CostEstimate(flops=int(us * 1.1e9), bytes_accessed=0, transcendentals=0),
            name=name,
            input_output_aliases=aliases or {},
        )(*operands)

    return call


def places():
    ctx = lax.axis_index("ctx").astype(jnp.int32)
    wa = lax.axis_index("wa").astype(jnp.int32)
    return ctx, (ctx >> 1) & 1, wa, wa & 1


def local_positions(first_row, row_count, device_rows, group_count):
    numbers = first_row + jnp.arange(row_count, dtype=jnp.int32)
    owner_index = numbers // device_rows
    within = numbers % device_rows
    halfway = device_rows // 2
    return jnp.where(
        within < halfway,
        owner_index * halfway + within,
        (2 * group_count - 1 - owner_index) * halfway + within - halfway,
    )


def angles_of(block):
    positions = local_positions(block * 128, 128, 128, 32)
    inverse = jnp.power(10000.0, -2.0 * jnp.arange(32, dtype=f32) / HEAD_DIM)
    return positions.astype(f32)[:, None] * inverse[None, :]


def lanes_of(dims):
    return lax.broadcasted_iota(jnp.int32, dims, len(dims) - 1)


def swap_halves(x):
    return pltpu.roll(x, 64, 1)


def turn_lanes(x, cosine, sine):
    lead = (lanes_of(x.shape) & 63) < 32
    return x * cosine + jnp.where(lead, pltpu.roll(x, 96, 1), pltpu.roll(x, 32, 1)) * sine


def turn_rows(x, cosine, sine):
    lead, trail = x[0:32], x[32:64]
    return jnp.concatenate([lead * cosine - trail * sine, trail * cosine + lead * sine], 0)


def prelude_kernel(
    tokens_ref, gain_ref, wq_ref, wk_ref, wv_ref, cos_ref, sin_ref, cos_t_ref, sin_t_ref,
    kv_ref, normed_ref, q_ref, q_give_ref, *, send, ready
):
    _, side, _, _ = places()
    ready(0)
    ready(1)
    x = tokens_ref[...].astype(f32)
    root = lax.rsqrt(jnp.mean(x * x, -1, keepdims=True) + epsilon)
    normed = (x * root * gain_ref[...]).astype(bf16)
    normed_ref[...] = normed
    send(1)
    ready(3)
    k = dot(normed, wk_ref[...])
    ready(4)
    v = dot(normed, wv_ref[...])
    low = lanes_of(k.shape) < 64
    heads = (
        jnp.where(low, k, swap_halves(v)),
        jnp.where(low, swap_halves(k), v),
    )
    heads = [turn_lanes(y, cos_ref[...], sin_ref[...]).astype(bf16) for y in heads]
    for d in range(32):
        kv_ref[d] = heads[(d >> 1) & 1]
    send(0)
    ready(2)
    qt = dot(normed, wq_ref[...]).T
    turned = [
        turn_rows(qt[64 * h : 64 * h + 64], cos_t_ref[...], sin_t_ref[...]).astype(bf16) * jnp.asarray(1.0 / HEAD_DIM, bf16)
        for h in range(4)
    ]
    pairs = [jnp.concatenate(turned[2 * j : 2 * j + 2], 0).astype(f32) for j in range(2)]
    q_ref[...] = jnp.where(side == 0, pairs[0], pairs[1]).astype(bf16)
    q_give_ref[...] = jnp.where(side == 0, pairs[1], pairs[0]).astype(bf16)


def to_columns(side, own_ref, other_ref, out_ref, first_row):
    for g in range(2):
        own = own_ref[64 * g : 64 * g + 64, :].astype(f32)
        other = other_ref[64 * g : 64 * g + 64, :].astype(f32)
        zero = jnp.where(side == 0, own, other)
        one = jnp.where(side == 0, other, own)
        low = lanes_of(own.shape) < 64
        out_ref[first_row : first_row + 64, 128 * g : 128 * g + 128] = jnp.where(
            low, zero, swap_halves(one)
        ).astype(bf16)
        out_ref[first_row : first_row + 64, 256 + 128 * g : 384 + 128 * g] = jnp.where(
            low, swap_halves(zero), one
        ).astype(bf16)


def from_columns(side, columns, g):
    a = columns[:, 128 * g : 128 * g + 128]
    b = columns[:, 256 + 128 * g : 384 + 128 * g]
    low = lanes_of(a.shape) < 64
    zero = jnp.where(low, a, swap_halves(b))
    one = jnp.where(low, swap_halves(a), b)
    return jnp.where(side == 0, zero, one), jnp.where(side == 0, one, zero)


def masked_early(scores, base, c):
    rows = lax.broadcasted_iota(jnp.int32, scores.shape, 0) + base * 64
    columns = lanes_of(scores.shape)
    block = (c & 29) + ((columns >> 6) & 1) * 2
    return jnp.where(rows <= block * 64 + (columns & 63), scores, -1e30)


def masked_late(scores, base, c):
    rows = lax.broadcasted_iota(jnp.int32, scores.shape, 0)
    columns = lanes_of(scores.shape)
    block = (c & 29) + ((columns >> 6) & 1) * 2
    key_at = (63 - base - (rows >> 6)) * 64 + (rows & 63)
    return jnp.where(key_at <= (63 - block) * 64 + (columns & 63), scores, -1e30)


def attend_kernel(
    own_ref, other_ref, kv_ref,
    mine_ref, give_ref, o_ref,
    q_ref, m_ref, l_ref, acc_ref, *, send
):
    c, side, _, _ = places()
    to_columns(side, own_ref, other_ref, q_ref, 0)
    q_ref[64:128, :] = jnp.zeros((64, 512), bf16)
    m_ref[...] = jnp.full(m_ref.shape, -1e30, f32)
    l_ref[...] = jnp.zeros(l_ref.shape, f32)
    acc_ref[...] = jnp.zeros(acc_ref.shape, f32)

    def step(base, keys_half, cols, mask):
        kv = kv_ref[base : base + CHUNK, keys_half, :].reshape(CHUNK * 64, 128)
        s = dot(kv, q_ref[:, cols])
        if mask is not None:
            s = mask(s, base, c)
        m_old = m_ref[:, cols]
        m_new = jnp.maximum(m_old, jnp.max(s, 0, keepdims=True))
        p = jnp.exp(s - m_new)
        factor = jnp.exp(m_old - m_new)
        m_ref[:, cols] = m_new
        l_ref[:, cols] = l_ref[:, cols] * factor + jnp.sum(p, 0, keepdims=True)
        acc_ref[:, cols] = acc_ref[:, cols] * factor + dot_tn(kv, p.astype(bf16))

    early, late = slice(0, 64), slice(64, 128)
    first, second = slice(0, 256), slice(256, 512)
    for base in range(0, 32, CHUNK):
        step(base, early, second, None)

        @pl.when(base <= (c | 2))
        def _():
            step(base, early, first, masked_early)

        @pl.when(base + CHUNK > (c & 29))
        def _():
            step(base, late, second, masked_late)

    total = l_ref[...]
    o_ref[0:64, :] = acc_ref[64:128, :] / total
    o_ref[64:72, :] = jnp.broadcast_to(m_ref[...] + jnp.log(total), (8, 512))
    send(2)
    for g in range(2):
        own, other = from_columns(side, o_ref[0:64, :], g)
        mine_ref[64 * g : 64 * g + 64, :] = own.astype(bf16)
        give_ref[64 * g : 64 * g + 64, :] = other.astype(bf16)


def reverse_kernel(
    own_ref, other_ref, kv_ref, do_own_ref, do_other_ref, o_ref,
    cos_ref, sin_ref, cos2_ref, sin2_ref,
    dq_ref, dq_give_ref, dkv_ref,
    q_ref, do_ref, delta_ref, acc_ref, *, send
):
    c, side, _, _ = places()
    to_columns(side, own_ref, other_ref, q_ref, 0)
    q_ref[64:128, :] = jnp.zeros((64, 512), bf16)
    to_columns(side, do_own_ref, do_other_ref, do_ref, 64)
    do_ref[0:64, :] = jnp.zeros((64, 512), bf16)
    delta_ref[...] = jnp.sum(do_ref[64:128, :].astype(f32) * o_ref[0:64, :], 0, keepdims=True)
    acc_ref[...] = jnp.zeros(acc_ref.shape, f32)

    def step(base, keys_half, cols, mask, add):
        kv = kv_ref[base : base + CHUNK, keys_half, :].reshape(CHUNK * 64, 128)
        q = q_ref[:, cols]
        do = do_ref[:, cols]
        s = dot(kv, q)
        if mask is not None:
            s = mask(s, base, c)
        p = jnp.exp(s - o_ref[64:65, cols])
        dp = dot(kv, do)
        ds = (p * (dp - delta_ref[:, cols])).astype(bf16)
        acc_ref[:, cols] += dot_tn(kv, ds)
        dkv = (dot_nt(ds, q) + dot_nt(p.astype(bf16), do)).reshape(CHUNK, 64, 128)
        if add:
            dkv += dkv_ref[base : base + CHUNK, keys_half, :].astype(f32)
        dkv_ref[base : base + CHUNK, keys_half, :] = dkv.astype(bf16)

    early, late = slice(0, 64), slice(64, 128)
    first, second = slice(0, 256), slice(256, 512)
    for base in range(0, 32, CHUNK):
        step(base, early, second, None, False)

        @pl.when(base <= (c | 2))
        def _():
            step(base, early, first, masked_early, True)

        @pl.when(base + CHUNK > (c & 29))
        def _():
            step(base, late, second, masked_late, False)

        @pl.when(base + CHUNK <= (c & 29))
        def _():
            dkv_ref[base : base + CHUNK, late, :] = jnp.zeros((CHUNK, 64, 128), bf16)

    for g in range(2):
        own, other = from_columns(side, acc_ref[0:64, :] * (1.0 / HEAD_DIM), g)
        here = slice(64 * g, 64 * g + 64)
        dq_ref[here, :] = turn_rows(own, cos_ref[...], -sin_ref[...]).astype(bf16)
        dq_give_ref[here, :] = turn_rows(other, cos2_ref[...], -sin2_ref[...]).astype(bf16)


def mix_kernel(mine_ref, got_ref, w_out_ref, context_ref, keep_ref, give_ref, *, send
):
    _, side, _, core = places()
    mine, got = mine_ref[...].astype(f32), got_ref[...].astype(f32)
    context_ref[0:128, :] = jnp.where(side == 0, mine, got).astype(bf16)
    context_ref[128:256, :] = jnp.where(side == 0, got, mine).astype(bf16)
    send(0)
    mixed = dot_tn(context_ref[...], w_out_ref[...])
    top, bottom = mixed[0:64], mixed[64:128]
    keep_ref[...] = jnp.where(core == 0, top, bottom).astype(bf16)
    give_ref[...] = jnp.where(core == 0, bottom, top).astype(bf16)


def selection(rank_ref, first, count):
    slot = lax.broadcasted_iota(jnp.int32, (64, 128), 0).astype(f32)
    return jnp.concatenate([(slot == rank_ref[e : e + 1, :]).astype(f32) for e in range(first, first + count)], 0)


def route_kernel(
    tokens_ref, mine_ref, theirs_ref, gain_ref, router_ref, rank_ref, cot_ref,
    middle_ref, normed_ref, gates_ref, out_ref, *, send
):
    _, _, wa, core = places()
    for half in range(2):
        here = slice(64 * half, 64 * half + 64)
        mixed = jnp.where(core == half, mine_ref[...].astype(f32), theirs_ref[...].astype(f32))
        middle = tokens_ref[here, :].astype(f32) + mixed
        middle_ref[here, :] = middle
        root = lax.rsqrt(jnp.mean(middle * middle, -1, keepdims=True) + epsilon)
        normed_ref[here, :] = (middle * root * gain_ref[...]).astype(bf16)
    send(0)
    send(1)
    logits = dot_nt(router_ref[...], normed_ref[...])
    member = rank_ref[...] >= 0.0
    top = jnp.max(jnp.where(member, logits, -1e30), 0, keepdims=True)
    raised = jnp.where(member, jnp.exp(jnp.where(member, logits - top, 0.0)), 0.0)
    gates_ref[0:32, :] = raised / jnp.sum(raised, 0, keepdims=True)
    gates_ref[32:64, :] = rank_ref[...]
    send(2)
    quarter = normed_ref[:, pl.ds(pl.multiple_of(wa * 256, 256), 256)]
    for first in range(0, 32, 4):
        chosen = selection(rank_ref, first, 4)
        weights = jnp.concatenate(
            [
                jnp.sum(chosen[64 * n : 64 * n + 64] * gates_ref[first + n : first + n + 1, :], 1, keepdims=True)
                for n in range(4)
            ],
            0,
        )
        chosen = chosen.astype(bf16)
        here = slice(64 * first, 64 * first + 256)
        out_ref[here, 0:256] = dot(chosen, quarter).astype(bf16)
        out_ref[here, 256:512] = (weights * dot(chosen, cot_ref[...])).astype(bf16)


def expert_kernel(
    in_ref, w0_ref, w1_ref, w2_ref, w3_ref, d0_ref, d1_ref, d2_ref, d3_ref,
    out_ref, hidden_ref,
    gate_ref, up_ref, down_ref, *, send
):
    downs = (d0_ref, d1_ref, d2_ref, d3_ref)
    for p, w in enumerate((w0_ref, w1_ref, w2_ref, w3_ref)):
        here = slice(128 * p, 128 * p + 128)
        gate_ref[:, here] = w[0]
        up_ref[:, here] = w[1]
        for n in range(8):
            down_ref[here, 128 * n : 128 * n + 128] = downs[p][128 * n : 128 * n + 128, :]
    act_ref, dgate_ref, dup_ref = (hidden_ref.at[:, 512 * n : 512 * n + 512] for n in range(3))
    gate_pre = jnp.zeros((512, 512), f32)
    up_pre = jnp.zeros((512, 512), f32)
    d_act = jnp.zeros((512, 512), f32)
    for q in range(4):
        here = slice(256 * q, 256 * q + 256)
        x = in_ref[:, q, :, 0:256].reshape(512, 256)
        gate_pre += dot(x, gate_ref[here, :])
        up_pre += dot(x, up_ref[here, :])
        d_act += dot_nt(in_ref[:, q, :, 256:512].reshape(512, 256), down_ref[:, here])
    sigma = jax.nn.sigmoid(gate_pre)
    act_ref[...] = (gate_pre * sigma * up_pre).astype(bf16)
    dgate_ref[...] = (d_act * up_pre * sigma * (1.0 + gate_pre * (1.0 - sigma))).astype(bf16)
    dup_ref[...] = (d_act * gate_pre * sigma).astype(bf16)
    for q in range(4):
        here = slice(256 * q, 256 * q + 256)
        part = dot(act_ref[...], down_ref[:, here])
        out_ref[:, q, :, 0:256] = part.astype(bf16).reshape(32, 16, 256)
        d_x = dot_nt(dgate_ref[...], gate_ref[here, :]) + dot_nt(dup_ref[...], up_ref[here, :])
        out_ref[:, q, :, 256:512] = d_x.astype(bf16).reshape(32, 16, 256)


def expert_grad_kernel(in_ref, hidden_ref, own_ref, give_ref, last_ref, far_ref, *, send):
    act_ref, dgate_ref, dup_ref = (hidden_ref.at[:, 512 * n : 512 * n + 512] for n in range(3))
    for q in range(4):
        here = slice(256 * q, 256 * q + 256)
        x = in_ref[:, q, :, 0:256].reshape(512, 256)
        d = in_ref[:, q, :, 256:512].reshape(512, 256)
        g_gate = dot_tn(x, dgate_ref[...]).astype(bf16)
        g_up = dot_tn(x, dup_ref[...]).astype(bf16)
        g_down = dot_tn(act_ref[...], d).astype(bf16)
        blocks = (
            (own_ref.at[0], own_ref.at[1], own_ref.at[2]),
            (give_ref.at[0], give_ref.at[1], last_ref),
            (far_ref.at[0, 0], far_ref.at[0, 1], far_ref.at[0, 2]),
            (far_ref.at[1, 0], far_ref.at[1, 1], far_ref.at[1, 2]),
        )
        for p, (gate, up, down) in enumerate(blocks):
            gate[here, :] = g_gate[:, 128 * p : 128 * p + 128]
            up[here, :] = g_up[:, 128 * p : 128 * p + 128]
            for n in range(2):
                at = 256 * q + 128 * n
                down[at : at + 128, :] = g_down[128 * p : 128 * p + 128, 128 * n : 128 * n + 128]


def combine_kernel(back_ref, gates_ref, cot_ref, sent_ref, dgates_ref, *, send
):
    rank_ref = gates_ref.at[32:64, :]
    d_normed = jnp.zeros((128, 256), f32)
    moe = jnp.zeros((128, 256), f32)
    for first in range(0, 32, 4):
        here = slice(64 * first, 64 * first + 256)
        chosen = selection(rank_ref, first, 4)
        gated = jnp.concatenate(
            [chosen[64 * n : 64 * n + 64] * gates_ref[first + n : first + n + 1, :] for n in range(4)], 0
        )
        high = gated.astype(bf16)
        low = (gated - high.astype(f32)).astype(bf16)
        picked = chosen.astype(bf16)
        part = back_ref[here, 0:256]
        d_normed += dot_tn(picked, back_ref[here, 256:512])
        moe += dot_tn(high, part) + dot_tn(low, part)
        along = jnp.sum(dot(picked, cot_ref[...]) * part.astype(f32), 1, keepdims=True)
        placed = chosen * along
        for n in range(4):
            dgates_ref[first + n : first + n + 1, :] = jnp.sum(
                placed[64 * n : 64 * n + 64], 0, keepdims=True
            )
    sent_ref[144:272, :] = moe.astype(bf16)
    sent_ref[0:128, :] = d_normed.astype(bf16)
    sent_ref[128:144, 0:128] = dgates_ref[0:16, :].astype(bf16)
    sent_ref[128:144, 128:256] = dgates_ref[16:32, :].astype(bf16)


def second_norm_kernel(
    own_ref, across_ref, beside_ref, diagonal_ref, gates_ref, middle_ref, normed_ref, cot_ref,
    gain_ref, router_ref, w_out_ref, context_ref,
    dmiddle_ref, dmine_ref, dgive_ref, parts_ref, output_ref, dnormed_ref, extra_ref, *, send
):
    _, side, wa, _ = places()
    pieces = [(own_ref, 0), (across_ref, 2), (beside_ref, 1), (diagonal_ref, 3)]
    for ref, flip in pieces:
        at = pl.multiple_of((wa ^ flip) * 256, 256)
        dnormed_ref[:, pl.ds(at, 256)] = ref[0:128, :].astype(f32)
        output_ref[:, pl.ds(at, 256)] = (
            middle_ref[:, pl.ds(at, 256)] + ref[144:272, :].astype(f32)
        ).astype(bf16)
    terms = [
        jnp.concatenate([ref[128:144, 0:128], ref[128:144, 128:256]], 0).astype(f32) for ref, _ in pieces
    ]
    d_gates = (terms[0] + terms[1]) + (terms[2] + terms[3])
    gates = gates_ref[0:32, :]
    d_logits = (gates * (d_gates - jnp.sum(gates * d_gates, 0, keepdims=True))).astype(bf16)
    gain = gain_ref[...]
    d_normed = dnormed_ref[...] + dot_tn(d_logits, router_ref[...])
    middle = middle_ref[...]
    root = lax.rsqrt(jnp.mean(middle * middle, -1, keepdims=True) + epsilon)
    unit = middle * root
    scaled = d_normed * gain
    gain_grad = jnp.sum(d_normed * unit, 0, keepdims=True)
    d_middle = cot_ref[...].astype(f32) + root * (
        scaled - unit * jnp.mean(scaled * unit, -1, keepdims=True)
    )
    dmiddle_ref[...] = d_middle
    send(0)
    d_mixed = d_middle.astype(bf16)
    d_context = dot_nt(w_out_ref[...], d_mixed)
    dmine_ref[...] = jnp.where(side == 0, d_context[0:128], d_context[128:256]).astype(bf16)
    dgive_ref[...] = jnp.where(side == 0, d_context[128:256], d_context[0:128]).astype(bf16)
    router_grad = dot(d_logits, normed_ref[...])
    extra_ref[...] = jnp.zeros(extra_ref.shape, f32)
    for q in range(4):
        here = slice(256 * q, 256 * q + 256)
        extra_ref[:, q, :] = router_grad[:, here]
        extra_ref[:, 4 + q, :] = jnp.broadcast_to(gain_grad[:, here], (32, 256))
        parts_ref[8 * q : 8 * q + 8, 0:32, :] = (
            dot(context_ref[...], d_mixed[:, here]).astype(bf16).reshape(8, 32, 256)
        )
    parts_ref[:, 32:48, :] = extra_ref[...].astype(bf16)


def late_kernel(
    back_ref, cos_ref, sin_ref, normed_ref, wk_ref, wv_ref, wq_ref, dq_ref, dq_got_ref, tokens_ref, filled_ref,
    parts_ref, keep_ref, give_ref,
    q_ref, kv_ref, sems, *, send, ready
):
    _, side, _, core = places()
    move_q = pltpu.make_async_copy(q_ref, parts_ref.at[:, 0:32, :], sems.at[0])
    move_kv = pltpu.make_async_copy(kv_ref, parts_ref.at[:, 80:112, :], sems.at[1])
    ready(3)
    ready(7)
    ready(8)
    own, got = dq_ref[...].astype(f32), dq_got_ref[...].astype(f32)
    d_q = jnp.concatenate([jnp.where(side == 0, own, got), jnp.where(side == 0, got, own)], 0).T
    d_q = d_q.astype(bf16)
    q_ref[...] = dot_tn(normed_ref[...], d_q).astype(bf16).reshape(32, 32, 256)
    move_q.start()
    ready(1)
    ready(2)
    heads = []
    for j in range(2):
        total = jnp.zeros((128, 128), f32)
        for d in range(32):
            if (d >> 1) & 1 == j:
                total += back_ref[d].astype(f32)
        heads.append(turn_lanes(total, cos_ref[...], -sin_ref[...]))
    low = lanes_of((128, 128)) < 64
    d_k = jnp.where(low, heads[0], swap_halves(heads[1])).astype(bf16)
    d_v = jnp.where(low, swap_halves(heads[0]), heads[1]).astype(bf16)
    kv_ref[:, :, 0:128] = dot_tn(normed_ref[...], d_k).astype(bf16).reshape(32, 32, 128)
    kv_ref[:, :, 128:256] = dot_tn(normed_ref[...], d_v).astype(bf16).reshape(32, 32, 128)
    move_kv.start()
    ready(4)
    ready(5)
    ready(6)
    ready(9)
    first = dot_nt(d_q, wq_ref[...]) + dot_nt(d_k, wk_ref[...]) + dot_nt(d_v, wv_ref[...])
    x = tokens_ref[...].astype(f32)
    unit = x * lax.rsqrt(jnp.mean(x * x, -1, keepdims=True) + epsilon)
    gain = jnp.sum(first * unit, 0, keepdims=True)
    for to, low_half in ((keep_ref, 0), (give_ref, 1)):
        to[0:64, :] = jnp.where(core == low_half, first[0:64], first[64:128]).astype(bf16)
        to[64:80, :] = jnp.broadcast_to(gain, (16, 1024)).astype(bf16)
    move_q.wait()
    move_kv.wait()


def share_kernel(in_ref, gain_ref, out_ref, gain2_ref, total_ref, *, send):
    total_ref[...] = jnp.sum(in_ref[...].astype(f32), 0)
    for q in range(4):
        here = slice(256 * q, 256 * q + 256)
        gain2_ref[:, here] = total_ref[68 + q : 69 + q, :]
        total_ref[72 + q : 73 + q, :] = gain_ref[0:1, here].astype(f32)
    out_ref[...] = jnp.broadcast_to(total_ref[...].astype(bf16)[None], (32, 112, 256))


def final_kernel(in_ref, query_ref, key_ref, value_ref, out_ref, router_ref, gain_ref, extra_ref, *, send):
    query_ref[...] = in_ref[:, 0:32, :].astype(f32).reshape(1024, 256)
    send(0)
    for q in range(4):
        here = slice(256 * q, 256 * q + 256)
        out_ref[:, here] = in_ref[8 * q : 8 * q + 8, 32:64, :].astype(f32).reshape(256, 256)
    send(3)
    key_ref[...] = in_ref[:, 80:112, 0:128].astype(f32).reshape(1024, 128)
    send(1)
    value_ref[...] = in_ref[:, 80:112, 128:256].astype(f32).reshape(1024, 128)
    send(2)
    extra_ref[...] = in_ref[:, 64:80, :].astype(f32)
    for q in range(4):
        router_ref[:, 256 * q : 256 * q + 256] = extra_ref[:, q, :]
        gain_ref[:, 256 * q : 256 * q + 256] = jnp.sum(extra_ref[:, 8 + q, :], 0, keepdims=True)


def pair_over_wa(keep, give):
    got = lax.ppermute(give, "wa", CORE_SWAP)
    pair = (keep.astype(f32) + got.astype(f32)).astype(bf16)
    return pair, lax.ppermute(pair, "wa", CHIP_SWAP)


def sum_over_wa(keep, give):
    pair, other = pair_over_wa(keep, give)
    mine = (pair.astype(f32) + other.astype(f32)).astype(bf16)
    return mine, lax.ppermute(mine, "wa", CORE_SWAP)


def pieces_over_wa(part):
    across = lax.ppermute(part, "wa", CHIP_SWAP)
    beside = lax.ppermute(part, "wa", CORE_SWAP)
    return across, beside, lax.ppermute(across, "wa", CORE_SWAP)


def local(
    tokens,
    norm1_gain,
    w_query,
    key_weight,
    value_weight,
    w_out,
    norm2_gain,
    w_router,
    w_gate,
    w_up,
    w_down,
    routes,
    cotangent,
):
    ctx = lax.axis_index("ctx").astype(jnp.int32)
    wa = lax.axis_index("wa").astype(jnp.int32)
    core, chip, side = wa % 2, wa // 2, (ctx >> 1) & 1
    rows, width, experts = 128, 1024, 32

    angles = angles_of(ctx)
    cosine, sine = jnp.cos(angles), jnp.sin(angles)
    one, zero = jnp.ones((rows, 64), f32), jnp.zeros((rows, 64), f32)
    cos_lanes = jnp.concatenate([cosine, cosine, one], 1)
    sin_lanes = jnp.concatenate([-sine, sine, zero], 1)
    cos_rows, sin_rows = cosine.T, sine.T
    gain1 = norm1_gain.reshape(1, width)
    kv_send, normed1, q_own, q_give = on_device(
        prelude_kernel,
        "prelude",
        "FFFFFVVVV",
        (
            ("S", shape((32, rows, 128))),
            ("S", shape((rows, width))),
            ("S", shape((rows, 128))),
            ("V", shape((rows, 128))),
        ),
        megabytes=56,
        us=2,
        lazy=True,
    )(tokens, gain1, w_query, key_weight, value_weight, cos_lanes, sin_lanes, cos_rows, sin_rows)
    kv = exchange(kv_send, "ctx")
    q_other = lax.ppermute(q_give, "ctx", PARTNER)

    member = jnp.any(
        routes[:, :, None] == jnp.arange(experts, dtype=jnp.int32)[None, None, :], axis=1
    )
    lower = (jnp.arange(rows)[:, None] >= jnp.arange(rows)[None, :]).astype(bf16)
    rank = jnp.where(member, dot(lower, member.astype(bf16)) - 1.0, -1.0).T
    router_t = w_router.T
    gain2 = norm2_gain.reshape(1, width)

    cot_quarter = lax.dynamic_slice_in_dim(cotangent, wa * 256, 256, 1)
    down_lanes = w_down[0].reshape(128, 8, 128).transpose(1, 0, 2).reshape(width, 128)
    weights = jnp.stack([w_gate[0], w_up[0]])
    down_across = lax.ppermute(down_lanes, "wa", CHIP_SWAP)
    kv, rank, q_other, weights, cot_quarter, down_across = lax.optimization_barrier(
        (kv, rank, q_other, weights, cot_quarter, down_across)
    )
    w_across, w_beside, w_diagonal = pieces_over_wa(weights)
    down_beside = lax.ppermute(down_lanes, "wa", CORE_SWAP)
    down_diagonal = lax.ppermute(down_across, "wa", CORE_SWAP)
    ctx_mine, ctx_give, context_o = on_device(
        attend_kernel,
        "attend",
        "VVV",
        (("V", shape((rows, 128))), ("V", shape((rows, 128))), ("V", shape((72, 512), f32))),
        [
            pltpu.VMEM((128, 512), bf16),
            pltpu.VMEM((1, 512), f32),
            pltpu.VMEM((1, 512), f32),
            pltpu.VMEM((128, 512), f32),
        ],
        us=0.5,
    )(q_own, q_other, kv)
    ctx_got = lax.ppermute(ctx_give, "ctx", PARTNER)
    context_t, mix_keep, mix_give = on_device(
        mix_kernel,
        "mix",
        "VVV",
        (("V", shape((256, rows))), ("V", shape((64, width))), ("V", shape((64, width)))),
        us=0.8,
    )(ctx_mine, ctx_got, w_out)
    mix_keep, mix_give, w_across = lax.optimization_barrier((mix_keep, mix_give, w_across))
    mine, theirs = sum_over_wa(mix_keep, mix_give)
    middle, normed2, gates, outgoing = on_device(
        route_kernel,
        "route",
        "VVVVVVV",
        (
            ("V", shape((rows, width), f32)),
            ("V", shape((rows, width))),
            ("V", shape((2 * experts, rows), f32)),
            ("V", shape((2048, 512))),
        ),
        us=1.6,
    )(tokens, mine, theirs, gain2, router_t, rank, cot_quarter)

    outgoing, w_across, w_beside, w_diagonal, down_beside, down_diagonal = lax.optimization_barrier(
        (outgoing, w_across, w_beside, w_diagonal, down_beside, down_diagonal)
    )
    arrived = exchange(outgoing.reshape(128, 16, 512), ("ctx", "wa")).reshape(32, 4, 16, 512)
    returning, hidden = on_device(
        expert_kernel,
        "experts",
        "VVVVVVVVV",
        (("V", shape((32, 4, 16, 512))), ("V", shape((512, 1536)))),
        [pltpu.VMEM((width, 512), bf16), pltpu.VMEM((width, 512), bf16), pltpu.VMEM((512, width), bf16)],
        megabytes=24,
        us=5,
    )(
        arrived, weights, w_across, w_beside, w_diagonal,
        down_lanes, down_across, down_beside, down_diagonal,
    )
    back = exchange(returning.reshape(128, 16, 512), ("ctx", "wa")).reshape(2048, 512)
    near_own, near_two, near_last, far = on_device(
        expert_grad_kernel,
        "expert_grads",
        "VV",
        (
            ("V", shape((3, width, 128))),
            ("V", shape((2, width, 128))),
            ("V", shape((width, 128))),
            ("V", shape((2, 3, width, 128))),
        ),
        us=3,
    )(arrived, hidden)
    far = lax.ppermute(far, "wa", CORE_SWAP)
    far = far.astype(f32)
    near_own = near_own.astype(f32) + far[0]
    near_two = (near_two.astype(f32) + far[1, :2]).astype(bf16)
    near_last = (near_last.astype(f32) + far[1, 2]).astype(bf16)
    back, near_own, near_two, near_last = lax.optimization_barrier((back, near_own, near_two, near_last))
    (sent,) = on_device(
        combine_kernel,
        "combine",
        "VVV",
        (("V", shape((272, 256))),),
        [pltpu.VMEM((32, 128), f32)],
        us=1,
    )(back, gates, cot_quarter)

    pieces = pieces_over_wa(sent)
    pieces, near_two = lax.optimization_barrier((pieces, near_two))
    near_got = lax.ppermute(near_two, "wa", CHIP_SWAP)
    d_middle, do_own, do_give, parts, output = on_device(
        second_norm_kernel,
        "second_norm",
        "VVVVVVVVVVVV",
        (
            ("V", shape((rows, width), f32)),
            ("V", shape((rows, 128))),
            ("V", shape((rows, 128))),
            ("V", shape((32, 48, 256))),
            ("V", shape((rows, width))),
        ),
        [pltpu.VMEM((rows, width), f32), pltpu.VMEM((32, 16, 256), f32)],
        us=1.6,
    )(sent, *pieces, gates, middle, normed2, cotangent, gain2, router_t, w_out, context_t)
    do_other = lax.ppermute(do_give, "ctx", PARTNER)

    angles2 = angles_of(ctx ^ 2)
    dq_own, dq_give, dkv = on_device(
        reverse_kernel,
        "reverse",
        "VVVVVVVVVV",
        (("V", shape((rows, 128))), ("V", shape((rows, 128))), ("V", shape((32, rows, 128)))),
        [
            pltpu.VMEM((128, 512), bf16),
            pltpu.VMEM((128, 512), bf16),
            pltpu.VMEM((1, 512), f32),
            pltpu.VMEM((128, 512), f32),
        ],
        us=1,
    )(
        q_own, q_other, kv, do_own, do_other, context_o,
        cos_rows, sin_rows, jnp.cos(angles2).T, jnp.sin(angles2).T,
    )
    dkv, near_got, near_last = lax.optimization_barrier((dkv, near_got, near_last))
    kv_back = exchange(dkv, "ctx")
    near_last = lax.ppermute(near_last, "wa", CHIP_SWAP)

    dq_got = lax.ppermute(dq_give, "ctx", PARTNER)
    dq_got, near_last = lax.optimization_barrier((dq_got, near_last))
    filled = jnp.pad(parts, ((0, 0), (32, 32), (0, 0)))
    kv_back, filled, dq_got = lax.optimization_barrier((kv_back, filled, dq_got))
    parts_all, first_keep, first_give = on_device(
        late_kernel,
        "late",
        "VFFFFFFFFFH",
        (("H", shape((32, 112, 256))), ("V", shape((80, width))), ("V", shape((80, width)))),
        [
            pltpu.VMEM((32, 32, 256), bf16),
            pltpu.VMEM((32, 32, 256), bf16),
            pltpu.SemaphoreType.DMA((2,)),
        ],
        megabytes=56,
        us=2,
        lazy=True,
        aliases={10: 0},
    )(
        kv_back, cos_lanes, sin_lanes, normed1, key_weight, value_weight, w_query, dq_own, dq_got,
        tokens, filled,
    )
    summed = exchange(parts_all, "ctx")

    first_pair, first_other = pair_over_wa(first_keep, first_give)
    summed, first_other = lax.optimization_barrier((summed, first_other))
    first_mine = (first_pair.astype(f32) + first_other.astype(f32)).astype(bf16)
    shared, out_gain2 = on_device(
        share_kernel,
        "share",
        "VV",
        (("V", shape((32, 112, 256))), ("V", shape((1, width), f32))),
        [pltpu.VMEM((112, 256), f32)],
        us=0.5,
    )(summed, first_mine[64:])
    spread_out = exchange(shared, "ctx")

    first_half = first_mine[:64]
    first_theirs = lax.ppermute(first_half, "wa", CORE_SWAP)
    d_first = jnp.where(
        core == 0, jnp.stack([first_half, first_theirs]), jnp.stack([first_theirs, first_half])
    ).reshape(rows, width).astype(f32)
    widened = tokens.astype(f32)
    root_first = lax.rsqrt(jnp.mean(widened * widened, -1, keepdims=True) + epsilon)
    unit_first = widened * root_first
    scaled_first = d_first * norm1_gain
    grad_tokens = (
        d_middle
        + root_first
        * (scaled_first - unit_first * jnp.mean(scaled_first * unit_first, -1, keepdims=True))
    ).astype(bf16)
    g_gate = near_own[0] + near_got[0].astype(f32)
    g_up = near_own[1] + near_got[1].astype(f32)
    g_down = (near_own[2] + near_last.astype(f32)).reshape(8, 128, 128)
    g_down = g_down.transpose(1, 0, 2).reshape(128, width)
    spread_out, output, grad_tokens, g_gate, g_up, g_down = lax.optimization_barrier(
        (spread_out, output, grad_tokens, g_gate, g_up, g_down)
    )
    out_query, out_key, out_value, out_out, out_router, out_gain1 = on_device(
        final_kernel,
        "final",
        "V",
        (
            ("S", shape((width, 256), f32)),
            ("S", shape((width, 128), f32)),
            ("S", shape((width, 128), f32)),
            ("S", shape((256, width), f32)),
            ("S", shape((experts, width), f32)),
            ("S", shape((1, width), f32)),
        ),
        [pltpu.VMEM((32, 16, 256), f32)],
        us=1.8,
    )(spread_out)
    return (
        output,
        grad_tokens,
        out_gain1.reshape(width),
        out_query,
        out_key,
        out_value,
        out_out,
        out_gain2.reshape(width),
        out_router.T,
        g_gate[None],
        g_up[None],
        g_down[None],
    )


def solution(mesh):
    in_specs = (
        P("ctx", None),
        P(),
        P(None, "wa"),
        P(None, "wa"),
        P(None, "wa"),
        P("wa", None),
        P(),
        P(),
        P("ctx", None, "wa"),
        P("ctx", None, "wa"),
        P("ctx", "wa", None),
        P("ctx", None),
        P("ctx", None),
    )
    out_specs = (
        P("ctx", None),
        P("ctx", None),
        P(),
        P(None, "wa"),
        P(None, "wa"),
        P(None, "wa"),
        P("wa", None),
        P(),
        P(),
        P("ctx", None, "wa"),
        P("ctx", None, "wa"),
        P("ctx", "wa", None),
    )
    return jax.shard_map(local, mesh=mesh, in_specs=in_specs, out_specs=out_specs, check_vma=False)
```

```python
import jax
import jax.numpy as jnp
from jax import lax
from jax.experimental import pallas as pl
from jax.experimental.pallas import tpu as pltpu
from jax.sharding import PartitionSpec as P

HEAD_DIM = 64
CHUNK = 8

epsilon = 1e-06
f32 = jnp.float32
bf16 = jnp.bfloat16
CORE_SWAP = [(0, 1), (1, 0), (2, 3), (3, 2)]
CHIP_SWAP = [(0, 2), (2, 0), (1, 3), (3, 1)]
PARTNER = [(i, i ^ 2) for i in range(32)]
def dot(a, b):
    return jnp.dot(a, b, preferred_element_type=f32)


def dot_nt(a, b):
    return lax.dot_general(a, b, (((1,), (1,)), ((), ())), preferred_element_type=f32)


def dot_tn(a, b):
    return lax.dot_general(a, b, (((0,), (0,)), ((), ())), preferred_element_type=f32)


def exchange(value, axes):
    return lax.all_to_all(value, axes, split_axis=0, concat_axis=0, tiled=True)


def shape(dims, dtype=bf16):
    return jax.ShapeDtypeStruct(dims, dtype)


def on_device(kernel, name, ins, outs, scratch=(), megabytes=16, us=1.0, lazy=False, aliases=None):
    spaces = {"V": pltpu.VMEM, "F": pltpu.HBM, "Q": pltpu.HBM, "H": pltpu.HBM, "S": pltpu.HBM}
    fetched = [n for n, kind in enumerate(ins) if kind in "FQ"]
    staged = [n for n, (kind, _) in enumerate(outs) if kind == "S"]

    def call(*operands):
        def held(n):
            dims = operands[n].shape
            return pltpu.VMEM((dims[0], 256) if ins[n] == "Q" else dims, operands[n].dtype)

        buffers = [held(n) for n in fetched]
        stages = [pltpu.VMEM(outs[n][1].shape, outs[n][1].dtype) for n in staged]

        def body(*refs):
            refs = list(refs)
            in_refs, refs = refs[: len(ins)], refs[len(ins) :]
            out_refs, refs = refs[: len(outs)], refs[len(outs) :]
            own, refs = refs[: len(scratch)], refs[len(scratch) :]
            held_refs, refs = refs[: len(buffers)], refs[len(buffers) :]
            stage_refs, sems = refs[: len(stages)], refs[len(stages)]
            copies = []
            for k, n in enumerate(fetched):
                source = in_refs[n]
                if ins[n] == "Q":
                    quarter = lax.axis_index("wa").astype(jnp.int32) * 256
                    source = source.at[:, pl.ds(pl.multiple_of(quarter, 256), 256)]
                copies.append(pltpu.make_async_copy(source, held_refs[k], sems.at[k]))
                in_refs[n] = held_refs[k]
            for copy in copies:
                copy.start()
            pending = {}
            for k, n in enumerate(staged):
                pending[n] = pltpu.make_async_copy(stage_refs[k], out_refs[n], sems.at[len(buffers) + k])
                out_refs[n] = stage_refs[k]
            sent = set()

            def send(n):
                if n in pending:
                    pending[n].start()
                    sent.add(n)

            if lazy:
                kernel(*in_refs, *out_refs, *own, send=send, ready=lambda n: copies[fetched.index(n)].wait())
            else:
                for copy in copies:
                    copy.wait()
                kernel(*in_refs, *out_refs, *own, send=send)
            for n in staged:
                if n not in sent:
                    send(n)
            for n in staged:
                pending[n].wait()

        return pl.pallas_call(
            body,
            out_shape=tuple(o for _, o in outs),
            in_specs=[pl.BlockSpec(memory_space=spaces[kind]) for kind in ins],
            out_specs=tuple(pl.BlockSpec(memory_space=spaces[kind]) for kind, _ in outs),
            scratch_shapes=[
                *scratch,
                *buffers,
                *stages,
                pltpu.SemaphoreType.DMA((max(1, len(buffers) + len(stages)),)),
            ],
            compiler_params=pltpu.CompilerParams(vmem_limit_bytes=megabytes * 1024 * 1024),
            cost_estimate=pl.CostEstimate(flops=int(us * 1.1e9), bytes_accessed=0, transcendentals=0),
            name=name,
            input_output_aliases=aliases or {},
        )(*operands)

    return call


def places():
    ctx = lax.axis_index("ctx").astype(jnp.int32)
    wa = lax.axis_index("wa").astype(jnp.int32)
    return ctx, (ctx >> 1) & 1, wa, wa & 1


def local_positions(first_row, row_count, device_rows, group_count):
    numbers = first_row + jnp.arange(row_count, dtype=jnp.int32)
    owner_index = numbers // device_rows
    within = numbers % device_rows
    halfway = device_rows // 2
    return jnp.where(
        within < halfway,
        owner_index * halfway + within,
        (2 * group_count - 1 - owner_index) * halfway + within - halfway,
    )


def angles_of(block):
    positions = local_positions(block * 128, 128, 128, 32)
    inverse = jnp.power(10000.0, -2.0 * jnp.arange(32, dtype=f32) / HEAD_DIM)
    return positions.astype(f32)[:, None] * inverse[None, :]


def lanes_of(dims):
    return lax.broadcasted_iota(jnp.int32, dims, len(dims) - 1)


def swap_halves(x):
    return pltpu.roll(x, 64, 1)


def turn_lanes(x, cosine, sine):
    lead = (lanes_of(x.shape) & 63) < 32
    return x * cosine + jnp.where(lead, pltpu.roll(x, 96, 1), pltpu.roll(x, 32, 1)) * sine


def turn_rows(x, cosine, sine):
    lead, trail = x[0:32], x[32:64]
    return jnp.concatenate([lead * cosine - trail * sine, trail * cosine + lead * sine], 0)


def prelude_kernel(
    tokens_ref, gain_ref, wq_ref, wk_ref, wv_ref, cos_ref, sin_ref, cos_t_ref, sin_t_ref,
    kv_ref, normed_ref, q_ref, q_give_ref, *, send, ready
):
    _, side, _, _ = places()
    ready(0)
    ready(1)
    x = tokens_ref[...].astype(f32)
    root = lax.rsqrt(jnp.mean(x * x, -1, keepdims=True) + epsilon)
    normed = (x * root * gain_ref[...]).astype(bf16)
    normed_ref[...] = normed
    send(1)
    ready(3)
    k = dot(normed, wk_ref[...])
    ready(4)
    v = dot(normed, wv_ref[...])
    low = lanes_of(k.shape) < 64
    heads = (
        jnp.where(low, k, swap_halves(v)),
        jnp.where(low, swap_halves(k), v),
    )
    heads = [turn_lanes(y, cos_ref[...], sin_ref[...]).astype(bf16) for y in heads]
    for d in range(32):
        kv_ref[d] = heads[(d >> 1) & 1]
    send(0)
    ready(2)
    qt = dot(normed, wq_ref[...]).T
    turned = [
        turn_rows(qt[64 * h : 64 * h + 64], cos_t_ref[...], sin_t_ref[...]).astype(bf16) * jnp.asarray(1.0 / HEAD_DIM, bf16)
        for h in range(4)
    ]
    pairs = [jnp.concatenate(turned[2 * j : 2 * j + 2], 0).astype(f32) for j in range(2)]
    q_ref[...] = jnp.where(side == 0, pairs[0], pairs[1]).astype(bf16)
    q_give_ref[...] = jnp.where(side == 0, pairs[1], pairs[0]).astype(bf16)


def to_columns(side, own_ref, other_ref, out_ref, first_row):
    for g in range(2):
        own = own_ref[64 * g : 64 * g + 64, :].astype(f32)
        other = other_ref[64 * g : 64 * g + 64, :].astype(f32)
        zero = jnp.where(side == 0, own, other)
        one = jnp.where(side == 0, other, own)
        low = lanes_of(own.shape) < 64
        out_ref[first_row : first_row + 64, 128 * g : 128 * g + 128] = jnp.where(
            low, zero, swap_halves(one)
        ).astype(bf16)
        out_ref[first_row : first_row + 64, 256 + 128 * g : 384 + 128 * g] = jnp.where(
            low, swap_halves(zero), one
        ).astype(bf16)


def from_columns(side, columns, g):
    a = columns[:, 128 * g : 128 * g + 128]
    b = columns[:, 256 + 128 * g : 384 + 128 * g]
    low = lanes_of(a.shape) < 64
    zero = jnp.where(low, a, swap_halves(b))
    one = jnp.where(low, swap_halves(a), b)
    return jnp.where(side == 0, zero, one), jnp.where(side == 0, one, zero)


def masked_early(scores, base, c):
    rows = lax.broadcasted_iota(jnp.int32, scores.shape, 0) + base * 64
    columns = lanes_of(scores.shape)
    block = (c & 29) + ((columns >> 6) & 1) * 2
    return jnp.where(rows <= block * 64 + (columns & 63), scores, -1e30)


def masked_late(scores, base, c):
    rows = lax.broadcasted_iota(jnp.int32, scores.shape, 0)
    columns = lanes_of(scores.shape)
    block = (c & 29) + ((columns >> 6) & 1) * 2
    key_at = (63 - base - (rows >> 6)) * 64 + (rows & 63)
    return jnp.where(key_at <= (63 - block) * 64 + (columns & 63), scores, -1e30)


def attend_kernel(
    own_ref, other_ref, kv_ref,
    mine_ref, give_ref, o_ref,
    q_ref, m_ref, l_ref, acc_ref, *, send
):
    c, side, _, _ = places()
    to_columns(side, own_ref, other_ref, q_ref, 0)
    q_ref[64:128, :] = jnp.zeros((64, 512), bf16)
    m_ref[...] = jnp.full(m_ref.shape, -1e30, f32)
    l_ref[...] = jnp.zeros(l_ref.shape, f32)
    acc_ref[...] = jnp.zeros(acc_ref.shape, f32)

    def step(base, keys_half, cols, mask):
        kv = kv_ref[base : base + CHUNK, keys_half, :].reshape(CHUNK * 64, 128)
        s = dot(kv, q_ref[:, cols])
        if mask is not None:
            s = mask(s, base, c)
        m_old = m_ref[:, cols]
        m_new = jnp.maximum(m_old, jnp.max(s, 0, keepdims=True))
        p = jnp.exp(s - m_new)
        factor = jnp.exp(m_old - m_new)
        m_ref[:, cols] = m_new
        l_ref[:, cols] = l_ref[:, cols] * factor + jnp.sum(p, 0, keepdims=True)
        acc_ref[:, cols] = acc_ref[:, cols] * factor + dot_tn(kv, p.astype(bf16))

    early, late = slice(0, 64), slice(64, 128)
    first, second = slice(0, 256), slice(256, 512)
    for base in range(0, 32, CHUNK):
        step(base, early, second, None)

        @pl.when(base <= (c | 2))
        def _():
            step(base, early, first, masked_early)

        @pl.when(base + CHUNK > (c & 29))
        def _():
            step(base, late, second, masked_late)

    total = l_ref[...]
    o_ref[0:64, :] = acc_ref[64:128, :] / total
    o_ref[64:72, :] = jnp.broadcast_to(m_ref[...] + jnp.log(total), (8, 512))
    send(2)
    for g in range(2):
        own, other = from_columns(side, o_ref[0:64, :], g)
        mine_ref[64 * g : 64 * g + 64, :] = own.astype(bf16)
        give_ref[64 * g : 64 * g + 64, :] = other.astype(bf16)


def reverse_kernel(
    own_ref, other_ref, kv_ref, do_own_ref, do_other_ref, o_ref,
    cos_ref, sin_ref, cos2_ref, sin2_ref,
    dq_ref, dq_give_ref, dkv_ref,
    q_ref, do_ref, delta_ref, acc_ref, *, send
):
    c, side, _, _ = places()
    to_columns(side, own_ref, other_ref, q_ref, 0)
    q_ref[64:128, :] = jnp.zeros((64, 512), bf16)
    to_columns(side, do_own_ref, do_other_ref, do_ref, 64)
    do_ref[0:64, :] = jnp.zeros((64, 512), bf16)
    delta_ref[...] = jnp.sum(do_ref[64:128, :].astype(f32) * o_ref[0:64, :], 0, keepdims=True)
    acc_ref[...] = jnp.zeros(acc_ref.shape, f32)

    def step(base, keys_half, cols, mask, add):
        kv = kv_ref[base : base + CHUNK, keys_half, :].reshape(CHUNK * 64, 128)
        q = q_ref[:, cols]
        do = do_ref[:, cols]
        s = dot(kv, q)
        if mask is not None:
            s = mask(s, base, c)
        p = jnp.exp(s - o_ref[64:65, cols])
        dp = dot(kv, do)
        ds = (p * (dp - delta_ref[:, cols])).astype(bf16)
        acc_ref[:, cols] += dot_tn(kv, ds)
        dkv = (dot_nt(ds, q) + dot_nt(p.astype(bf16), do)).reshape(CHUNK, 64, 128)
        if add:
            dkv += dkv_ref[base : base + CHUNK, keys_half, :].astype(f32)
        dkv_ref[base : base + CHUNK, keys_half, :] = dkv.astype(bf16)

    early, late = slice(0, 64), slice(64, 128)
    first, second = slice(0, 256), slice(256, 512)
    for base in range(0, 32, CHUNK):
        step(base, early, second, None, False)

        @pl.when(base <= (c | 2))
        def _():
            step(base, early, first, masked_early, True)

        @pl.when(base + CHUNK > (c & 29))
        def _():
            step(base, late, second, masked_late, False)

        @pl.when(base + CHUNK <= (c & 29))
        def _():
            dkv_ref[base : base + CHUNK, late, :] = jnp.zeros((CHUNK, 64, 128), bf16)

    for g in range(2):
        own, other = from_columns(side, acc_ref[0:64, :] * (1.0 / HEAD_DIM), g)
        here = slice(64 * g, 64 * g + 64)
        dq_ref[here, :] = turn_rows(own, cos_ref[...], -sin_ref[...]).astype(bf16)
        dq_give_ref[here, :] = turn_rows(other, cos2_ref[...], -sin2_ref[...]).astype(bf16)


def mix_kernel(mine_ref, got_ref, w_out_ref, context_ref, keep_ref, give_ref, *, send
):
    _, side, _, core = places()
    mine, got = mine_ref[...].astype(f32), got_ref[...].astype(f32)
    context_ref[0:128, :] = jnp.where(side == 0, mine, got).astype(bf16)
    context_ref[128:256, :] = jnp.where(side == 0, got, mine).astype(bf16)
    send(0)
    mixed = dot_tn(context_ref[...], w_out_ref[...])
    top, bottom = mixed[0:64], mixed[64:128]
    keep_ref[...] = jnp.where(core == 0, top, bottom).astype(bf16)
    give_ref[...] = jnp.where(core == 0, bottom, top).astype(bf16)


def selection(rank_ref, first, count):
    slot = lax.broadcasted_iota(jnp.int32, (64, 128), 0).astype(f32)
    return jnp.concatenate([(slot == rank_ref[e : e + 1, :]).astype(f32) for e in range(first, first + count)], 0)


def route_kernel(
    tokens_ref, mine_ref, theirs_ref, gain_ref, router_ref, rank_ref, cot_ref,
    middle_ref, normed_ref, gates_ref, out_ref, *, send
):
    _, _, wa, core = places()
    for half in range(2):
        here = slice(64 * half, 64 * half + 64)
        mixed = jnp.where(core == half, mine_ref[...].astype(f32), theirs_ref[...].astype(f32))
        middle = tokens_ref[here, :].astype(f32) + mixed
        middle_ref[here, :] = middle
        root = lax.rsqrt(jnp.mean(middle * middle, -1, keepdims=True) + epsilon)
        normed_ref[here, :] = (middle * root * gain_ref[...]).astype(bf16)
    send(0)
    send(1)
    logits = dot_nt(router_ref[...], normed_ref[...])
    member = rank_ref[...] >= 0.0
    top = jnp.max(jnp.where(member, logits, -1e30), 0, keepdims=True)
    raised = jnp.where(member, jnp.exp(jnp.where(member, logits - top, 0.0)), 0.0)
    gates_ref[0:32, :] = raised / jnp.sum(raised, 0, keepdims=True)
    gates_ref[32:64, :] = rank_ref[...]
    send(2)
    quarter = normed_ref[:, pl.ds(pl.multiple_of(wa * 256, 256), 256)]
    for first in range(0, 32, 4):
        chosen = selection(rank_ref, first, 4)
        weights = jnp.concatenate(
            [
                jnp.sum(chosen[64 * n : 64 * n + 64] * gates_ref[first + n : first + n + 1, :], 1, keepdims=True)
                for n in range(4)
            ],
            0,
        )
        chosen = chosen.astype(bf16)
        here = slice(64 * first, 64 * first + 256)
        out_ref[here, 0:256] = dot(chosen, quarter).astype(bf16)
        out_ref[here, 256:512] = (weights * dot(chosen, cot_ref[...])).astype(bf16)


def expert_kernel(
    in_ref, w0_ref, w1_ref, w2_ref, w3_ref, d0_ref, d1_ref, d2_ref, d3_ref,
    out_ref, hidden_ref,
    gate_ref, up_ref, down_ref, *, send
):
    downs = (d0_ref, d1_ref, d2_ref, d3_ref)
    for p, w in enumerate((w0_ref, w1_ref, w2_ref, w3_ref)):
        here = slice(128 * p, 128 * p + 128)
        gate_ref[:, here] = w[0]
        up_ref[:, here] = w[1]
        for n in range(8):
            down_ref[here, 128 * n : 128 * n + 128] = downs[p][128 * n : 128 * n + 128, :]
    act_ref, dgate_ref, dup_ref = (hidden_ref.at[:, 512 * n : 512 * n + 512] for n in range(3))
    gate_pre = jnp.zeros((512, 512), f32)
    up_pre = jnp.zeros((512, 512), f32)
    d_act = jnp.zeros((512, 512), f32)
    for q in range(4):
        here = slice(256 * q, 256 * q + 256)
        x = in_ref[:, q, :, 0:256].reshape(512, 256)
        gate_pre += dot(x, gate_ref[here, :])
        up_pre += dot(x, up_ref[here, :])
        d_act += dot_nt(in_ref[:, q, :, 256:512].reshape(512, 256), down_ref[:, here])
    sigma = jax.nn.sigmoid(gate_pre)
    act_ref[...] = (gate_pre * sigma * up_pre).astype(bf16)
    dgate_ref[...] = (d_act * up_pre * sigma * (1.0 + gate_pre * (1.0 - sigma))).astype(bf16)
    dup_ref[...] = (d_act * gate_pre * sigma).astype(bf16)
    for q in range(4):
        here = slice(256 * q, 256 * q + 256)
        part = dot(act_ref[...], down_ref[:, here])
        out_ref[:, q, :, 0:256] = part.astype(bf16).reshape(32, 16, 256)
        d_x = dot_nt(dgate_ref[...], gate_ref[here, :]) + dot_nt(dup_ref[...], up_ref[here, :])
        out_ref[:, q, :, 256:512] = d_x.astype(bf16).reshape(32, 16, 256)


def expert_grad_kernel(in_ref, hidden_ref, own_ref, give_ref, last_ref, far_ref, *, send):
    act_ref, dgate_ref, dup_ref = (hidden_ref.at[:, 512 * n : 512 * n + 512] for n in range(3))
    for q in range(4):
        here = slice(256 * q, 256 * q + 256)
        x = in_ref[:, q, :, 0:256].reshape(512, 256)
        d = in_ref[:, q, :, 256:512].reshape(512, 256)
        g_gate = dot_tn(x, dgate_ref[...]).astype(bf16)
        g_up = dot_tn(x, dup_ref[...]).astype(bf16)
        g_down = dot_tn(act_ref[...], d).astype(bf16)
        blocks = (
            (own_ref.at[0], own_ref.at[1], own_ref.at[2]),
            (give_ref.at[0], give_ref.at[1], last_ref),
            (far_ref.at[0, 0], far_ref.at[0, 1], far_ref.at[0, 2]),
            (far_ref.at[1, 0], far_ref.at[1, 1], far_ref.at[1, 2]),
        )
        for p, (gate, up, down) in enumerate(blocks):
            gate[here, :] = g_gate[:, 128 * p : 128 * p + 128]
            up[here, :] = g_up[:, 128 * p : 128 * p + 128]
            for n in range(2):
                at = 256 * q + 128 * n
                down[at : at + 128, :] = g_down[128 * p : 128 * p + 128, 128 * n : 128 * n + 128]


def combine_kernel(back_ref, gates_ref, cot_ref, sent_ref, dgates_ref, *, send
):
    rank_ref = gates_ref.at[32:64, :]
    d_normed = jnp.zeros((128, 256), f32)
    moe = jnp.zeros((128, 256), f32)
    for first in range(0, 32, 4):
        here = slice(64 * first, 64 * first + 256)
        chosen = selection(rank_ref, first, 4)
        gated = jnp.concatenate(
            [chosen[64 * n : 64 * n + 64] * gates_ref[first + n : first + n + 1, :] for n in range(4)], 0
        )
        high = gated.astype(bf16)
        low = (gated - high.astype(f32)).astype(bf16)
        picked = chosen.astype(bf16)
        part = back_ref[here, 0:256]
        d_normed += dot_tn(picked, back_ref[here, 256:512])
        moe += dot_tn(high, part) + dot_tn(low, part)
        along = jnp.sum(dot(picked, cot_ref[...]) * part.astype(f32), 1, keepdims=True)
        placed = chosen * along
        for n in range(4):
            dgates_ref[first + n : first + n + 1, :] = jnp.sum(
                placed[64 * n : 64 * n + 64], 0, keepdims=True
            )
    sent_ref[144:272, :] = moe.astype(bf16)
    sent_ref[0:128, :] = d_normed.astype(bf16)
    sent_ref[128:144, 0:128] = dgates_ref[0:16, :].astype(bf16)
    sent_ref[128:144, 128:256] = dgates_ref[16:32, :].astype(bf16)


def second_norm_kernel(
    own_ref, across_ref, beside_ref, diagonal_ref, gates_ref, middle_ref, normed_ref, cot_ref,
    gain_ref, router_ref, w_out_ref, context_ref,
    dmiddle_ref, dmine_ref, dgive_ref, parts_ref, output_ref, dnormed_ref, extra_ref, *, send
):
    _, side, wa, _ = places()
    pieces = [(own_ref, 0), (across_ref, 2), (beside_ref, 1), (diagonal_ref, 3)]
    for ref, flip in pieces:
        at = pl.multiple_of((wa ^ flip) * 256, 256)
        dnormed_ref[:, pl.ds(at, 256)] = ref[0:128, :].astype(f32)
        output_ref[:, pl.ds(at, 256)] = (
            middle_ref[:, pl.ds(at, 256)] + ref[144:272, :].astype(f32)
        ).astype(bf16)
    terms = [
        jnp.concatenate([ref[128:144, 0:128], ref[128:144, 128:256]], 0).astype(f32) for ref, _ in pieces
    ]
    d_gates = (terms[0] + terms[1]) + (terms[2] + terms[3])
    gates = gates_ref[0:32, :]
    d_logits = (gates * (d_gates - jnp.sum(gates * d_gates, 0, keepdims=True))).astype(bf16)
    gain = gain_ref[...]
    d_normed = dnormed_ref[...] + dot_tn(d_logits, router_ref[...])
    middle = middle_ref[...]
    root = lax.rsqrt(jnp.mean(middle * middle, -1, keepdims=True) + epsilon)
    unit = middle * root
    scaled = d_normed * gain
    gain_grad = jnp.sum(d_normed * unit, 0, keepdims=True)
    d_middle = cot_ref[...].astype(f32) + root * (
        scaled - unit * jnp.mean(scaled * unit, -1, keepdims=True)
    )
    dmiddle_ref[...] = d_middle
    send(0)
    d_mixed = d_middle.astype(bf16)
    d_context = dot_nt(w_out_ref[...], d_mixed)
    dmine_ref[...] = jnp.where(side == 0, d_context[0:128], d_context[128:256]).astype(bf16)
    dgive_ref[...] = jnp.where(side == 0, d_context[128:256], d_context[0:128]).astype(bf16)
    router_grad = dot(d_logits, normed_ref[...])
    extra_ref[...] = jnp.zeros(extra_ref.shape, f32)
    for q in range(4):
        here = slice(256 * q, 256 * q + 256)
        extra_ref[:, q, :] = router_grad[:, here]
        extra_ref[:, 4 + q, :] = jnp.broadcast_to(gain_grad[:, here], (32, 256))
        parts_ref[8 * q : 8 * q + 8, 0:32, :] = (
            dot(context_ref[...], d_mixed[:, here]).astype(bf16).reshape(8, 32, 256)
        )
    parts_ref[:, 32:48, :] = extra_ref[...].astype(bf16)


def late_kernel(
    back_ref, cos_ref, sin_ref, normed_ref, wk_ref, wv_ref, wq_ref, dq_ref, dq_got_ref, tokens_ref, filled_ref,
    parts_ref, keep_ref, give_ref,
    q_ref, kv_ref, sems, *, send, ready
):
    _, side, _, core = places()
    move_q = pltpu.make_async_copy(q_ref, parts_ref.at[:, 0:32, :], sems.at[0])
    move_kv = pltpu.make_async_copy(kv_ref, parts_ref.at[:, 80:112, :], sems.at[1])
    ready(3)
    ready(7)
    ready(8)
    own, got = dq_ref[...].astype(f32), dq_got_ref[...].astype(f32)
    d_q = jnp.concatenate([jnp.where(side == 0, own, got), jnp.where(side == 0, got, own)], 0).T
    d_q = d_q.astype(bf16)
    q_ref[...] = dot_tn(normed_ref[...], d_q).astype(bf16).reshape(32, 32, 256)
    move_q.start()
    ready(1)
    ready(2)
    heads = []
    for j in range(2):
        total = jnp.zeros((128, 128), f32)
        for d in range(32):
            if (d >> 1) & 1 == j:
                total += back_ref[d].astype(f32)
        heads.append(turn_lanes(total, cos_ref[...], -sin_ref[...]))
    low = lanes_of((128, 128)) < 64
    d_k = jnp.where(low, heads[0], swap_halves(heads[1])).astype(bf16)
    d_v = jnp.where(low, swap_halves(heads[0]), heads[1]).astype(bf16)
    kv_ref[:, :, 0:128] = dot_tn(normed_ref[...], d_k).astype(bf16).reshape(32, 32, 128)
    kv_ref[:, :, 128:256] = dot_tn(normed_ref[...], d_v).astype(bf16).reshape(32, 32, 128)
    move_kv.start()
    ready(4)
    ready(5)
    ready(6)
    ready(9)
    first = dot_nt(d_q, wq_ref[...]) + dot_nt(d_k, wk_ref[...]) + dot_nt(d_v, wv_ref[...])
    x = tokens_ref[...].astype(f32)
    unit = x * lax.rsqrt(jnp.mean(x * x, -1, keepdims=True) + epsilon)
    gain = jnp.sum(first * unit, 0, keepdims=True)
    for to, low_half in ((keep_ref, 0), (give_ref, 1)):
        to[0:64, :] = jnp.where(core == low_half, first[0:64], first[64:128]).astype(bf16)
        to[64:80, :] = jnp.broadcast_to(gain, (16, 1024)).astype(bf16)
    move_q.wait()
    move_kv.wait()


def share_kernel(in_ref, gain_ref, out_ref, gain2_ref, total_ref, *, send):
    total_ref[...] = jnp.sum(in_ref[...].astype(f32), 0)
    for q in range(4):
        here = slice(256 * q, 256 * q + 256)
        gain2_ref[:, here] = total_ref[68 + q : 69 + q, :]
        total_ref[72 + q : 73 + q, :] = gain_ref[0:1, here].astype(f32)
    out_ref[...] = jnp.broadcast_to(total_ref[...].astype(bf16)[None], (32, 112, 256))


def final_kernel(in_ref, query_ref, key_ref, value_ref, out_ref, router_ref, gain_ref, extra_ref, *, send):
    query_ref[...] = in_ref[:, 0:32, :].astype(f32).reshape(1024, 256)
    send(0)
    for q in range(4):
        here = slice(256 * q, 256 * q + 256)
        out_ref[:, here] = in_ref[8 * q : 8 * q + 8, 32:64, :].astype(f32).reshape(256, 256)
    send(3)
    key_ref[...] = in_ref[:, 80:112, 0:128].astype(f32).reshape(1024, 128)
    send(1)
    value_ref[...] = in_ref[:, 80:112, 128:256].astype(f32).reshape(1024, 128)
    send(2)
    extra_ref[...] = in_ref[:, 64:80, :].astype(f32)
    for q in range(4):
        router_ref[:, 256 * q : 256 * q + 256] = extra_ref[:, q, :]
        gain_ref[:, 256 * q : 256 * q + 256] = jnp.sum(extra_ref[:, 8 + q, :], 0, keepdims=True)


def pair_over_wa(keep, give):
    got = lax.ppermute(give, "wa", CORE_SWAP)
    pair = (keep.astype(f32) + got.astype(f32)).astype(bf16)
    return pair, lax.ppermute(pair, "wa", CHIP_SWAP)


def sum_over_wa(keep, give):
    pair, other = pair_over_wa(keep, give)
    mine = (pair.astype(f32) + other.astype(f32)).astype(bf16)
    return mine, lax.ppermute(mine, "wa", CORE_SWAP)


def pieces_over_wa(part):
    across = lax.ppermute(part, "wa", CHIP_SWAP)
    beside = lax.ppermute(part, "wa", CORE_SWAP)
    return across, beside, lax.ppermute(across, "wa", CORE_SWAP)


def local(
    tokens,
    norm1_gain,
    w_query,
    key_weight,
    value_weight,
    w_out,
    norm2_gain,
    w_router,
    w_gate,
    w_up,
    w_down,
    routes,
    cotangent,
):
    ctx = lax.axis_index("ctx").astype(jnp.int32)
    wa = lax.axis_index("wa").astype(jnp.int32)
    core, chip, side = wa % 2, wa // 2, (ctx >> 1) & 1
    rows, width, experts = 128, 1024, 32

    angles = angles_of(ctx)
    cosine, sine = jnp.cos(angles), jnp.sin(angles)
    one, zero = jnp.ones((rows, 64), f32), jnp.zeros((rows, 64), f32)
    cos_lanes = jnp.concatenate([cosine, cosine, one], 1)
    sin_lanes = jnp.concatenate([-sine, sine, zero], 1)
    cos_rows, sin_rows = cosine.T, sine.T
    gain1 = norm1_gain.reshape(1, width)
    kv_send, normed1, q_own, q_give = on_device(
        prelude_kernel,
        "prelude",
        "FFFFFVVVV",
        (
            ("S", shape((32, rows, 128))),
            ("S", shape((rows, width))),
            ("S", shape((rows, 128))),
            ("V", shape((rows, 128))),
        ),
        megabytes=56,
        us=2,
        lazy=True,
    )(tokens, gain1, w_query, key_weight, value_weight, cos_lanes, sin_lanes, cos_rows, sin_rows)
    kv = exchange(kv_send, "ctx")
    q_other = lax.ppermute(q_give, "ctx", PARTNER)

    member = jnp.any(
        routes[:, :, None] == jnp.arange(experts, dtype=jnp.int32)[None, None, :], axis=1
    )
    lower = (jnp.arange(rows)[:, None] >= jnp.arange(rows)[None, :]).astype(bf16)
    rank = jnp.where(member, dot(lower, member.astype(bf16)) - 1.0, -1.0).T
    router_t = w_router.T
    gain2 = norm2_gain.reshape(1, width)

    cot_quarter = lax.dynamic_slice_in_dim(cotangent, wa * 256, 256, 1)
    down_lanes = w_down[0].reshape(128, 8, 128).transpose(1, 0, 2).reshape(width, 128)
    weights = jnp.stack([w_gate[0], w_up[0]])
    down_across = lax.ppermute(down_lanes, "wa", CHIP_SWAP)
    kv, rank, q_other, weights, cot_quarter, down_across = lax.optimization_barrier(
        (kv, rank, q_other, weights, cot_quarter, down_across)
    )
    w_across, w_beside, w_diagonal = pieces_over_wa(weights)
    down_beside = lax.ppermute(down_lanes, "wa", CORE_SWAP)
    down_diagonal = lax.ppermute(down_across, "wa", CORE_SWAP)
    ctx_mine, ctx_give, context_o = on_device(
        attend_kernel,
        "attend",
        "VVV",
        (("V", shape((rows, 128))), ("V", shape((rows, 128))), ("V", shape((72, 512), f32))),
        [
            pltpu.VMEM((128, 512), bf16),
            pltpu.VMEM((1, 512), f32),
            pltpu.VMEM((1, 512), f32),
            pltpu.VMEM((128, 512), f32),
        ],
        us=0.5,
    )(q_own, q_other, kv)
    ctx_got = lax.ppermute(ctx_give, "ctx", PARTNER)
    context_t, mix_keep, mix_give = on_device(
        mix_kernel,
        "mix",
        "VVV",
        (("V", shape((256, rows))), ("V", shape((64, width))), ("V", shape((64, width)))),
        us=0.8,
    )(ctx_mine, ctx_got, w_out)
    mix_keep, mix_give, w_across = lax.optimization_barrier((mix_keep, mix_give, w_across))
    mine, theirs = sum_over_wa(mix_keep, mix_give)
    middle, normed2, gates, outgoing = on_device(
        route_kernel,
        "route",
        "VVVVVVV",
        (
            ("V", shape((rows, width), f32)),
            ("V", shape((rows, width))),
            ("V", shape((2 * experts, rows), f32)),
            ("V", shape((2048, 512))),
        ),
        us=1.6,
    )(tokens, mine, theirs, gain2, router_t, rank, cot_quarter)

    outgoing, w_across, w_beside, w_diagonal, down_beside, down_diagonal = lax.optimization_barrier(
        (outgoing, w_across, w_beside, w_diagonal, down_beside, down_diagonal)
    )
    arrived = exchange(outgoing.reshape(128, 16, 512), ("ctx", "wa")).reshape(32, 4, 16, 512)
    returning, hidden = on_device(
        expert_kernel,
        "experts",
        "VVVVVVVVV",
        (("V", shape((32, 4, 16, 512))), ("V", shape((512, 1536)))),
        [pltpu.VMEM((width, 512), bf16), pltpu.VMEM((width, 512), bf16), pltpu.VMEM((512, width), bf16)],
        megabytes=24,
        us=5,
    )(
        arrived, weights, w_across, w_beside, w_diagonal,
        down_lanes, down_across, down_beside, down_diagonal,
    )
    back = exchange(returning.reshape(128, 16, 512), ("ctx", "wa")).reshape(2048, 512)
    near_own, near_two, near_last, far = on_device(
        expert_grad_kernel,
        "expert_grads",
        "VV",
        (
            ("V", shape((3, width, 128))),
            ("V", shape((2, width, 128))),
            ("V", shape((width, 128))),
            ("V", shape((2, 3, width, 128))),
        ),
        us=3,
    )(arrived, hidden)
    back, near_own, near_two, near_last, far = lax.optimization_barrier(
        (back, near_own, near_two, near_last, far)
    )
    far = lax.ppermute(far, "wa", CORE_SWAP)
    far = far.astype(f32)
    near_own = near_own.astype(f32) + far[0]
    near_two = (near_two.astype(f32) + far[1, :2]).astype(bf16)
    near_last = (near_last.astype(f32) + far[1, 2]).astype(bf16)
    (sent,) = on_device(
        combine_kernel,
        "combine",
        "VVV",
        (("V", shape((272, 256))),),
        [pltpu.VMEM((32, 128), f32)],
        us=1,
    )(back, gates, cot_quarter)

    pieces = pieces_over_wa(sent)
    pieces, near_two = lax.optimization_barrier((pieces, near_two))
    near_got = lax.ppermute(near_two, "wa", CHIP_SWAP)
    d_middle, do_own, do_give, parts, output = on_device(
        second_norm_kernel,
        "second_norm",
        "VVVVVVVVVVVV",
        (
            ("V", shape((rows, width), f32)),
            ("V", shape((rows, 128))),
            ("V", shape((rows, 128))),
            ("V", shape((32, 48, 256))),
            ("V", shape((rows, width))),
        ),
        [pltpu.VMEM((rows, width), f32), pltpu.VMEM((32, 16, 256), f32)],
        us=1.6,
    )(sent, *pieces, gates, middle, normed2, cotangent, gain2, router_t, w_out, context_t)
    do_other = lax.ppermute(do_give, "ctx", PARTNER)

    angles2 = angles_of(ctx ^ 2)
    dq_own, dq_give, dkv = on_device(
        reverse_kernel,
        "reverse",
        "VVVVVVVVVV",
        (("V", shape((rows, 128))), ("V", shape((rows, 128))), ("V", shape((32, rows, 128)))),
        [
            pltpu.VMEM((128, 512), bf16),
            pltpu.VMEM((128, 512), bf16),
            pltpu.VMEM((1, 512), f32),
            pltpu.VMEM((128, 512), f32),
        ],
        us=1,
    )(
        q_own, q_other, kv, do_own, do_other, context_o,
        cos_rows, sin_rows, jnp.cos(angles2).T, jnp.sin(angles2).T,
    )
    dkv, near_got, near_last = lax.optimization_barrier((dkv, near_got, near_last))
    kv_back = exchange(dkv, "ctx")

    dq_got = lax.ppermute(dq_give, "ctx", PARTNER)
    filled = jnp.pad(parts, ((0, 0), (32, 32), (0, 0)))
    kv_back, filled, dq_got = lax.optimization_barrier((kv_back, filled, dq_got))
    parts_all, first_keep, first_give = on_device(
        late_kernel,
        "late",
        "VFFFFFFFFFH",
        (("H", shape((32, 112, 256))), ("V", shape((80, width))), ("V", shape((80, width)))),
        [
            pltpu.VMEM((32, 32, 256), bf16),
            pltpu.VMEM((32, 32, 256), bf16),
            pltpu.SemaphoreType.DMA((2,)),
        ],
        megabytes=56,
        us=2,
        lazy=True,
        aliases={10: 0},
    )(
        kv_back, cos_lanes, sin_lanes, normed1, key_weight, value_weight, w_query, dq_own, dq_got,
        tokens, filled,
    )
    summed = exchange(parts_all, "ctx")

    first_pair, first_other = pair_over_wa(first_keep, first_give)
    summed, first_other = lax.optimization_barrier((summed, first_other))
    first_mine = (first_pair.astype(f32) + first_other.astype(f32)).astype(bf16)
    shared, out_gain2 = on_device(
        share_kernel,
        "share",
        "VV",
        (("V", shape((32, 112, 256))), ("V", shape((1, width), f32))),
        [pltpu.VMEM((112, 256), f32)],
        us=0.5,
    )(summed, first_mine[64:])
    shared, near_last = lax.optimization_barrier((shared, near_last))
    spread_out = exchange(shared, "ctx")
    near_last = lax.ppermute(near_last, "wa", CHIP_SWAP)

    first_half = first_mine[:64]
    first_theirs = lax.ppermute(first_half, "wa", CORE_SWAP)
    d_first = jnp.where(
        core == 0, jnp.stack([first_half, first_theirs]), jnp.stack([first_theirs, first_half])
    ).reshape(rows, width).astype(f32)
    widened = tokens.astype(f32)
    root_first = lax.rsqrt(jnp.mean(widened * widened, -1, keepdims=True) + epsilon)
    unit_first = widened * root_first
    scaled_first = d_first * norm1_gain
    grad_tokens = (
        d_middle
        + root_first
        * (scaled_first - unit_first * jnp.mean(scaled_first * unit_first, -1, keepdims=True))
    ).astype(bf16)
    g_gate = near_own[0] + near_got[0].astype(f32)
    g_up = near_own[1] + near_got[1].astype(f32)
    g_down = (near_own[2] + near_last.astype(f32)).reshape(8, 128, 128)
    g_down = g_down.transpose(1, 0, 2).reshape(128, width)
    spread_out, output, grad_tokens, g_gate, g_up, g_down = lax.optimization_barrier(
        (spread_out, output, grad_tokens, g_gate, g_up, g_down)
    )
    out_query, out_key, out_value, out_out, out_router, out_gain1 = on_device(
        final_kernel,
        "final",
        "V",
        (
            ("S", shape((width, 256), f32)),
            ("S", shape((width, 128), f32)),
            ("S", shape((width, 128), f32)),
            ("S", shape((256, width), f32)),
            ("S", shape((experts, width), f32)),
            ("S", shape((1, width), f32)),
        ),
        [pltpu.VMEM((32, 16, 256), f32)],
        us=1.8,
    )(spread_out)
    return (
        output,
        grad_tokens,
        out_gain1.reshape(width),
        out_query,
        out_key,
        out_value,
        out_out,
        out_gain2.reshape(width),
        out_router.T,
        g_gate[None],
        g_up[None],
        g_down[None],
    )


def solution(mesh):
    in_specs = (
        P("ctx", None),
        P(),
        P(None, "wa"),
        P(None, "wa"),
        P(None, "wa"),
        P("wa", None),
        P(),
        P(),
        P("ctx", None, "wa"),
        P("ctx", None, "wa"),
        P("ctx", "wa", None),
        P("ctx", None),
        P("ctx", None),
    )
    out_specs = (
        P("ctx", None),
        P("ctx", None),
        P(),
        P(None, "wa"),
        P(None, "wa"),
        P(None, "wa"),
        P("wa", None),
        P(),
        P(),
        P("ctx", None, "wa"),
        P("ctx", None, "wa"),
        P("ctx", "wa", None),
    )
    return jax.shard_map(local, mesh=mesh, in_specs=in_specs, out_specs=out_specs, check_vma=False)
```

```python
import jax
import jax.numpy as jnp
from jax import lax
from jax.experimental import pallas as pl
from jax.experimental.pallas import tpu as pltpu
from jax.sharding import PartitionSpec as P

HEAD_DIM = 64
CHUNK = 8

epsilon = 1e-06
f32 = jnp.float32
bf16 = jnp.bfloat16
CORE_SWAP = [(0, 1), (1, 0), (2, 3), (3, 2)]
CHIP_SWAP = [(0, 2), (2, 0), (1, 3), (3, 1)]
PARTNER = [(i, i ^ 2) for i in range(32)]
def dot(a, b):
    return jnp.dot(a, b, preferred_element_type=f32)


def dot_nt(a, b):
    return lax.dot_general(a, b, (((1,), (1,)), ((), ())), preferred_element_type=f32)


def dot_tn(a, b):
    return lax.dot_general(a, b, (((0,), (0,)), ((), ())), preferred_element_type=f32)


def exchange(value, axes):
    return lax.all_to_all(value, axes, split_axis=0, concat_axis=0, tiled=True)


def shape(dims, dtype=bf16):
    return jax.ShapeDtypeStruct(dims, dtype)


def on_device(kernel, name, ins, outs, scratch=(), megabytes=16, us=1.0, lazy=False, aliases=None):
    spaces = {"V": pltpu.VMEM, "F": pltpu.HBM, "Q": pltpu.HBM, "H": pltpu.HBM, "S": pltpu.HBM}
    fetched = [n for n, kind in enumerate(ins) if kind in "FQ"]
    staged = [n for n, (kind, _) in enumerate(outs) if kind == "S"]

    def call(*operands):
        def held(n):
            dims = operands[n].shape
            return pltpu.VMEM((dims[0], 256) if ins[n] == "Q" else dims, operands[n].dtype)

        buffers = [held(n) for n in fetched]
        stages = [pltpu.VMEM(outs[n][1].shape, outs[n][1].dtype) for n in staged]

        def body(*refs):
            refs = list(refs)
            in_refs, refs = refs[: len(ins)], refs[len(ins) :]
            out_refs, refs = refs[: len(outs)], refs[len(outs) :]
            own, refs = refs[: len(scratch)], refs[len(scratch) :]
            held_refs, refs = refs[: len(buffers)], refs[len(buffers) :]
            stage_refs, sems = refs[: len(stages)], refs[len(stages)]
            copies = []
            for k, n in enumerate(fetched):
                source = in_refs[n]
                if ins[n] == "Q":
                    quarter = lax.axis_index("wa").astype(jnp.int32) * 256
                    source = source.at[:, pl.ds(pl.multiple_of(quarter, 256), 256)]
                copies.append(pltpu.make_async_copy(source, held_refs[k], sems.at[k]))
                in_refs[n] = held_refs[k]
            for copy in copies:
                copy.start()
            pending = {}
            for k, n in enumerate(staged):
                pending[n] = pltpu.make_async_copy(stage_refs[k], out_refs[n], sems.at[len(buffers) + k])
                out_refs[n] = stage_refs[k]
            sent = set()

            def send(n):
                if n in pending:
                    pending[n].start()
                    sent.add(n)

            if lazy:
                kernel(*in_refs, *out_refs, *own, send=send, ready=lambda n: copies[fetched.index(n)].wait())
            else:
                for copy in copies:
                    copy.wait()
                kernel(*in_refs, *out_refs, *own, send=send)
            for n in staged:
                if n not in sent:
                    send(n)
            for n in staged:
                pending[n].wait()

        return pl.pallas_call(
            body,
            out_shape=tuple(o for _, o in outs),
            in_specs=[pl.BlockSpec(memory_space=spaces[kind]) for kind in ins],
            out_specs=tuple(pl.BlockSpec(memory_space=spaces[kind]) for kind, _ in outs),
            scratch_shapes=[
                *scratch,
                *buffers,
                *stages,
                pltpu.SemaphoreType.DMA((max(1, len(buffers) + len(stages)),)),
            ],
            compiler_params=pltpu.CompilerParams(vmem_limit_bytes=megabytes * 1024 * 1024),
            cost_estimate=pl.CostEstimate(flops=int(us * 1.1e9), bytes_accessed=0, transcendentals=0),
            name=name,
            input_output_aliases=aliases or {},
        )(*operands)

    return call


def places():
    ctx = lax.axis_index("ctx").astype(jnp.int32)
    wa = lax.axis_index("wa").astype(jnp.int32)
    return ctx, (ctx >> 1) & 1, wa, wa & 1


def local_positions(first_row, row_count, device_rows, group_count):
    numbers = first_row + jnp.arange(row_count, dtype=jnp.int32)
    owner_index = numbers // device_rows
    within = numbers % device_rows
    halfway = device_rows // 2
    return jnp.where(
        within < halfway,
        owner_index * halfway + within,
        (2 * group_count - 1 - owner_index) * halfway + within - halfway,
    )


def angles_of(block):
    positions = local_positions(block * 128, 128, 128, 32)
    inverse = jnp.power(10000.0, -2.0 * jnp.arange(32, dtype=f32) / HEAD_DIM)
    return positions.astype(f32)[:, None] * inverse[None, :]


def lanes_of(dims):
    return lax.broadcasted_iota(jnp.int32, dims, len(dims) - 1)


def swap_halves(x):
    return pltpu.roll(x, 64, 1)


def turn_lanes(x, cosine, sine):
    lead = (lanes_of(x.shape) & 63) < 32
    return x * cosine + jnp.where(lead, pltpu.roll(x, 96, 1), pltpu.roll(x, 32, 1)) * sine


def turn_rows(x, cosine, sine):
    lead, trail = x[0:32], x[32:64]
    return jnp.concatenate([lead * cosine - trail * sine, trail * cosine + lead * sine], 0)


def prelude_kernel(
    tokens_ref, gain_ref, wq_ref, wk_ref, wv_ref, cos_t_ref, sin_t_ref,
    kv_ref, normed_ref, q_ref, q_give_ref, *, send, ready
):
    _, side, _, _ = places()
    ready(0)
    ready(1)
    x = tokens_ref[...].astype(f32)
    root = lax.rsqrt(jnp.mean(x * x, -1, keepdims=True) + epsilon)
    normed = (x * root * gain_ref[...]).astype(bf16)
    normed_ref[...] = normed
    send(1)
    ready(3)
    k = dot(normed, wk_ref[...])
    ready(4)
    v = dot(normed, wv_ref[...])
    low = lanes_of(k.shape) < 64
    heads = (
        jnp.where(low, k, swap_halves(v)),
        jnp.where(low, swap_halves(k), v),
    )
    cosine, sine = cos_t_ref[...], sin_t_ref[...]
    cos_lanes = jnp.concatenate([cosine, cosine, jnp.ones((64, 128), f32)], 0).T
    sin_lanes = jnp.concatenate([-sine, sine, jnp.zeros((64, 128), f32)], 0).T
    heads = [turn_lanes(y, cos_lanes, sin_lanes).astype(bf16) for y in heads]
    for d in range(32):
        kv_ref[d] = heads[(d >> 1) & 1]
    send(0)
    ready(2)
    qt = dot(normed, wq_ref[...]).T
    turned = [
        turn_rows(qt[64 * h : 64 * h + 64], cos_t_ref[...], sin_t_ref[...]).astype(bf16) * jnp.asarray(1.0 / HEAD_DIM, bf16)
        for h in range(4)
    ]
    pairs = [jnp.concatenate(turned[2 * j : 2 * j + 2], 0).astype(f32) for j in range(2)]
    q_ref[...] = jnp.where(side == 0, pairs[0], pairs[1]).astype(bf16)
    q_give_ref[...] = jnp.where(side == 0, pairs[1], pairs[0]).astype(bf16)


def to_columns(side, own_ref, other_ref, out_ref, first_row):
    for g in range(2):
        own = own_ref[64 * g : 64 * g + 64, :].astype(f32)
        other = other_ref[64 * g : 64 * g + 64, :].astype(f32)
        zero = jnp.where(side == 0, own, other)
        one = jnp.where(side == 0, other, own)
        low = lanes_of(own.shape) < 64
        out_ref[first_row : first_row + 64, 128 * g : 128 * g + 128] = jnp.where(
            low, zero, swap_halves(one)
        ).astype(bf16)
        out_ref[first_row : first_row + 64, 256 + 128 * g : 384 + 128 * g] = jnp.where(
            low, swap_halves(zero), one
        ).astype(bf16)


def from_columns(side, columns, g):
    a = columns[:, 128 * g : 128 * g + 128]
    b = columns[:, 256 + 128 * g : 384 + 128 * g]
    low = lanes_of(a.shape) < 64
    zero = jnp.where(low, a, swap_halves(b))
    one = jnp.where(low, swap_halves(a), b)
    return jnp.where(side == 0, zero, one), jnp.where(side == 0, one, zero)


def masked_early(scores, base, c):
    rows = lax.broadcasted_iota(jnp.int32, scores.shape, 0) + base * 64
    columns = lanes_of(scores.shape)
    block = (c & 29) + ((columns >> 6) & 1) * 2
    return jnp.where(rows <= block * 64 + (columns & 63), scores, -1e30)


def masked_late(scores, base, c):
    rows = lax.broadcasted_iota(jnp.int32, scores.shape, 0)
    columns = lanes_of(scores.shape)
    block = (c & 29) + ((columns >> 6) & 1) * 2
    key_at = (63 - base - (rows >> 6)) * 64 + (rows & 63)
    return jnp.where(key_at <= (63 - block) * 64 + (columns & 63), scores, -1e30)


def attend_kernel(
    own_ref, other_ref, kv_ref,
    mine_ref, give_ref, o_ref,
    q_ref, m_ref, l_ref, acc_ref, *, send
):
    c, side, _, _ = places()
    to_columns(side, own_ref, other_ref, q_ref, 0)
    q_ref[64:128, :] = jnp.zeros((64, 512), bf16)
    m_ref[...] = jnp.full(m_ref.shape, -1e30, f32)
    l_ref[...] = jnp.zeros(l_ref.shape, f32)
    acc_ref[...] = jnp.zeros(acc_ref.shape, f32)

    def step(base, keys_half, cols, mask):
        kv = kv_ref[base : base + CHUNK, keys_half, :].reshape(CHUNK * 64, 128)
        s = dot(kv, q_ref[:, cols])
        if mask is not None:
            s = mask(s, base, c)
        m_old = m_ref[:, cols]
        m_new = jnp.maximum(m_old, jnp.max(s, 0, keepdims=True))
        p = jnp.exp(s - m_new)
        factor = jnp.exp(m_old - m_new)
        m_ref[:, cols] = m_new
        l_ref[:, cols] = l_ref[:, cols] * factor + jnp.sum(p, 0, keepdims=True)
        acc_ref[:, cols] = acc_ref[:, cols] * factor + dot_tn(kv, p.astype(bf16))

    early, late = slice(0, 64), slice(64, 128)
    first, second = slice(0, 256), slice(256, 512)
    for base in range(0, 32, CHUNK):
        step(base, early, second, None)

        @pl.when(base <= (c | 2))
        def _():
            step(base, early, first, masked_early)

        @pl.when(base + CHUNK > (c & 29))
        def _():
            step(base, late, second, masked_late)

    total = l_ref[...]
    o_ref[0:64, :] = acc_ref[64:128, :] / total
    o_ref[64:72, :] = jnp.broadcast_to(m_ref[...] + jnp.log(total), (8, 512))
    send(2)
    for g in range(2):
        own, other = from_columns(side, o_ref[0:64, :], g)
        mine_ref[64 * g : 64 * g + 64, :] = own.astype(bf16)
        give_ref[64 * g : 64 * g + 64, :] = other.astype(bf16)


def reverse_kernel(
    own_ref, other_ref, kv_ref, do_own_ref, do_other_ref, o_ref,
    cos_ref, sin_ref, cos2_ref, sin2_ref,
    dq_ref, dq_give_ref, dkv_ref,
    q_ref, do_ref, delta_ref, acc_ref, *, send
):
    c, side, _, _ = places()
    to_columns(side, own_ref, other_ref, q_ref, 0)
    q_ref[64:128, :] = jnp.zeros((64, 512), bf16)
    to_columns(side, do_own_ref, do_other_ref, do_ref, 64)
    do_ref[0:64, :] = jnp.zeros((64, 512), bf16)
    delta_ref[...] = jnp.sum(do_ref[64:128, :].astype(f32) * o_ref[0:64, :], 0, keepdims=True)
    acc_ref[...] = jnp.zeros(acc_ref.shape, f32)

    def step(base, keys_half, cols, mask, add):
        kv = kv_ref[base : base + CHUNK, keys_half, :].reshape(CHUNK * 64, 128)
        q = q_ref[:, cols]
        do = do_ref[:, cols]
        s = dot(kv, q)
        if mask is not None:
            s = mask(s, base, c)
        p = jnp.exp(s - o_ref[64:65, cols])
        dp = dot(kv, do)
        ds = (p * (dp - delta_ref[:, cols])).astype(bf16)
        acc_ref[:, cols] += dot_tn(kv, ds)
        dkv = (dot_nt(ds, q) + dot_nt(p.astype(bf16), do)).reshape(CHUNK, 64, 128)
        if add:
            dkv += dkv_ref[base : base + CHUNK, keys_half, :].astype(f32)
        dkv_ref[base : base + CHUNK, keys_half, :] = dkv.astype(bf16)

    early, late = slice(0, 64), slice(64, 128)
    first, second = slice(0, 256), slice(256, 512)
    for base in range(0, 32, CHUNK):
        step(base, early, second, None, False)

        @pl.when(base <= (c | 2))
        def _():
            step(base, early, first, masked_early, True)

        @pl.when(base + CHUNK > (c & 29))
        def _():
            step(base, late, second, masked_late, False)

        @pl.when(base + CHUNK <= (c & 29))
        def _():
            dkv_ref[base : base + CHUNK, late, :] = jnp.zeros((CHUNK, 64, 128), bf16)

    for g in range(2):
        own, other = from_columns(side, acc_ref[0:64, :] * (1.0 / HEAD_DIM), g)
        here = slice(64 * g, 64 * g + 64)
        dq_ref[here, :] = turn_rows(own, cos_ref[...], -sin_ref[...]).astype(bf16)
        dq_give_ref[here, :] = turn_rows(other, cos2_ref[...], -sin2_ref[...]).astype(bf16)


def mix_kernel(mine_ref, got_ref, w_out_ref, context_ref, keep_ref, give_ref, *, send
):
    _, side, _, core = places()
    mine, got = mine_ref[...].astype(f32), got_ref[...].astype(f32)
    context_ref[0:128, :] = jnp.where(side == 0, mine, got).astype(bf16)
    context_ref[128:256, :] = jnp.where(side == 0, got, mine).astype(bf16)
    send(0)
    mixed = dot_tn(context_ref[...], w_out_ref[...])
    top, bottom = mixed[0:64], mixed[64:128]
    keep_ref[...] = jnp.where(core == 0, top, bottom).astype(bf16)
    give_ref[...] = jnp.where(core == 0, bottom, top).astype(bf16)


def selection(rank_ref, first, count):
    slot = lax.broadcasted_iota(jnp.int32, (64, 128), 0).astype(f32)
    return jnp.concatenate([(slot == rank_ref[e : e + 1, :]).astype(f32) for e in range(first, first + count)], 0)


def route_kernel(
    tokens_ref, mine_ref, theirs_ref, gain_ref, router_ref, rank_ref, cot_ref,
    middle_ref, normed_ref, gates_ref, out_ref, *, send
):
    _, _, wa, core = places()
    for half in range(2):
        here = slice(64 * half, 64 * half + 64)
        mixed = jnp.where(core == half, mine_ref[...].astype(f32), theirs_ref[...].astype(f32))
        middle = tokens_ref[here, :].astype(f32) + mixed
        middle_ref[here, :] = middle
        root = lax.rsqrt(jnp.mean(middle * middle, -1, keepdims=True) + epsilon)
        normed_ref[here, :] = (middle * root * gain_ref[...]).astype(bf16)
    send(0)
    send(1)
    logits = dot_nt(router_ref[...], normed_ref[...])
    member = rank_ref[...] >= 0.0
    top = jnp.max(jnp.where(member, logits, -1e30), 0, keepdims=True)
    raised = jnp.where(member, jnp.exp(jnp.where(member, logits - top, 0.0)), 0.0)
    gates_ref[0:32, :] = raised / jnp.sum(raised, 0, keepdims=True)
    gates_ref[32:64, :] = rank_ref[...]
    send(2)
    quarter = normed_ref[:, pl.ds(pl.multiple_of(wa * 256, 256), 256)]
    for first in range(0, 32, 4):
        chosen = selection(rank_ref, first, 4)
        weights = jnp.concatenate(
            [
                jnp.sum(chosen[64 * n : 64 * n + 64] * gates_ref[first + n : first + n + 1, :], 1, keepdims=True)
                for n in range(4)
            ],
            0,
        )
        chosen = chosen.astype(bf16)
        here = slice(64 * first, 64 * first + 256)
        out_ref[here, 0:256] = dot(chosen, quarter).astype(bf16)
        out_ref[here, 256:512] = (weights * dot(chosen, cot_ref[...])).astype(bf16)


def expert_kernel(
    in_ref, w0_ref, w1_ref, w2_ref, w3_ref, d0_ref, d1_ref, d2_ref, d3_ref,
    out_ref, hidden_ref,
    gate_ref, up_ref, down_ref, *, send
):
    downs = (d0_ref, d1_ref, d2_ref, d3_ref)
    for p, w in enumerate((w0_ref, w1_ref, w2_ref, w3_ref)):
        here = slice(128 * p, 128 * p + 128)
        gate_ref[:, here] = w[0]
        up_ref[:, here] = w[1]
        for n in range(8):
            down_ref[here, 128 * n : 128 * n + 128] = downs[p][128 * n : 128 * n + 128, :]
    act_ref, dgate_ref, dup_ref = (hidden_ref.at[:, 512 * n : 512 * n + 512] for n in range(3))
    gate_pre = jnp.zeros((512, 512), f32)
    up_pre = jnp.zeros((512, 512), f32)
    d_act = jnp.zeros((512, 512), f32)
    for q in range(4):
        here = slice(256 * q, 256 * q + 256)
        x = in_ref[:, q, :, 0:256].reshape(512, 256)
        gate_pre += dot(x, gate_ref[here, :])
        up_pre += dot(x, up_ref[here, :])
        d_act += dot_nt(in_ref[:, q, :, 256:512].reshape(512, 256), down_ref[:, here])
    sigma = jax.nn.sigmoid(gate_pre)
    act_ref[...] = (gate_pre * sigma * up_pre).astype(bf16)
    dgate_ref[...] = (d_act * up_pre * sigma * (1.0 + gate_pre * (1.0 - sigma))).astype(bf16)
    dup_ref[...] = (d_act * gate_pre * sigma).astype(bf16)
    for q in range(4):
        here = slice(256 * q, 256 * q + 256)
        part = dot(act_ref[...], down_ref[:, here])
        out_ref[:, q, :, 0:256] = part.astype(bf16).reshape(32, 16, 256)
        d_x = dot_nt(dgate_ref[...], gate_ref[here, :]) + dot_nt(dup_ref[...], up_ref[here, :])
        out_ref[:, q, :, 256:512] = d_x.astype(bf16).reshape(32, 16, 256)


def expert_grad_kernel(in_ref, hidden_ref, own_ref, give_ref, last_ref, far_ref, *, send):
    act_ref, dgate_ref, dup_ref = (hidden_ref.at[:, 512 * n : 512 * n + 512] for n in range(3))
    for q in range(4):
        here = slice(256 * q, 256 * q + 256)
        x = in_ref[:, q, :, 0:256].reshape(512, 256)
        d = in_ref[:, q, :, 256:512].reshape(512, 256)
        g_gate = dot_tn(x, dgate_ref[...]).astype(bf16)
        g_up = dot_tn(x, dup_ref[...]).astype(bf16)
        g_down = dot_tn(act_ref[...], d).astype(bf16)
        blocks = (
            (own_ref.at[0], own_ref.at[1], own_ref.at[2]),
            (give_ref.at[0], give_ref.at[1], last_ref),
            (far_ref.at[0, 0], far_ref.at[0, 1], far_ref.at[0, 2]),
            (far_ref.at[1, 0], far_ref.at[1, 1], far_ref.at[1, 2]),
        )
        for p, (gate, up, down) in enumerate(blocks):
            gate[here, :] = g_gate[:, 128 * p : 128 * p + 128]
            up[here, :] = g_up[:, 128 * p : 128 * p + 128]
            for n in range(2):
                at = 256 * q + 128 * n
                down[at : at + 128, :] = g_down[128 * p : 128 * p + 128, 128 * n : 128 * n + 128]


def combine_kernel(back_ref, gates_ref, cot_ref, sent_ref, dgates_ref, *, send
):
    rank_ref = gates_ref.at[32:64, :]
    d_normed = jnp.zeros((128, 256), f32)
    moe = jnp.zeros((128, 256), f32)
    for first in range(0, 32, 4):
        here = slice(64 * first, 64 * first + 256)
        chosen = selection(rank_ref, first, 4)
        gated = jnp.concatenate(
            [chosen[64 * n : 64 * n + 64] * gates_ref[first + n : first + n + 1, :] for n in range(4)], 0
        )
        high = gated.astype(bf16)
        low = (gated - high.astype(f32)).astype(bf16)
        picked = chosen.astype(bf16)
        part = back_ref[here, 0:256]
        d_normed += dot_tn(picked, back_ref[here, 256:512])
        moe += dot_tn(high, part) + dot_tn(low, part)
        along = jnp.sum(dot(picked, cot_ref[...]) * part.astype(f32), 1, keepdims=True)
        placed = chosen * along
        for n in range(4):
            dgates_ref[first + n : first + n + 1, :] = jnp.sum(
                placed[64 * n : 64 * n + 64], 0, keepdims=True
            )
    sent_ref[144:272, :] = moe.astype(bf16)
    sent_ref[0:128, :] = d_normed.astype(bf16)
    sent_ref[128:144, 0:128] = dgates_ref[0:16, :].astype(bf16)
    sent_ref[128:144, 128:256] = dgates_ref[16:32, :].astype(bf16)


def second_norm_kernel(
    own_ref, across_ref, beside_ref, diagonal_ref, gates_ref, middle_ref, normed_ref, cot_ref,
    gain_ref, router_ref, w_out_ref, context_ref,
    dmiddle_ref, dmine_ref, dgive_ref, parts_ref, output_ref, dnormed_ref, extra_ref, *, send
):
    _, side, wa, _ = places()
    pieces = [(own_ref, 0), (across_ref, 2), (beside_ref, 1), (diagonal_ref, 3)]
    for ref, flip in pieces:
        at = pl.multiple_of((wa ^ flip) * 256, 256)
        dnormed_ref[:, pl.ds(at, 256)] = ref[0:128, :].astype(f32)
        output_ref[:, pl.ds(at, 256)] = (
            middle_ref[:, pl.ds(at, 256)] + ref[144:272, :].astype(f32)
        ).astype(bf16)
    terms = [
        jnp.concatenate([ref[128:144, 0:128], ref[128:144, 128:256]], 0).astype(f32) for ref, _ in pieces
    ]
    d_gates = (terms[0] + terms[1]) + (terms[2] + terms[3])
    gates = gates_ref[0:32, :]
    d_logits = (gates * (d_gates - jnp.sum(gates * d_gates, 0, keepdims=True))).astype(bf16)
    gain = gain_ref[...]
    d_normed = dnormed_ref[...] + dot_tn(d_logits, router_ref[...])
    middle = middle_ref[...]
    root = lax.rsqrt(jnp.mean(middle * middle, -1, keepdims=True) + epsilon)
    unit = middle * root
    scaled = d_normed * gain
    gain_grad = jnp.sum(d_normed * unit, 0, keepdims=True)
    d_middle = cot_ref[...].astype(f32) + root * (
        scaled - unit * jnp.mean(scaled * unit, -1, keepdims=True)
    )
    dmiddle_ref[...] = d_middle
    send(0)
    d_mixed = d_middle.astype(bf16)
    d_context = dot_nt(w_out_ref[...], d_mixed)
    dmine_ref[...] = jnp.where(side == 0, d_context[0:128], d_context[128:256]).astype(bf16)
    dgive_ref[...] = jnp.where(side == 0, d_context[128:256], d_context[0:128]).astype(bf16)
    router_grad = dot(d_logits, normed_ref[...])
    extra_ref[...] = jnp.zeros(extra_ref.shape, f32)
    for q in range(4):
        here = slice(256 * q, 256 * q + 256)
        extra_ref[:, q, :] = router_grad[:, here]
        extra_ref[:, 4 + q, :] = jnp.broadcast_to(gain_grad[:, here], (32, 256))
        parts_ref[8 * q : 8 * q + 8, 0:32, :] = (
            dot(context_ref[...], d_mixed[:, here]).astype(bf16).reshape(8, 32, 256)
        )
    parts_ref[:, 32:48, :] = extra_ref[...].astype(bf16)


def late_kernel(
    back_ref, cos_ref, sin_ref, normed_ref, wk_ref, wv_ref, wq_ref, dq_ref, dq_got_ref, tokens_ref, filled_ref,
    parts_ref, keep_ref, give_ref,
    q_ref, kv_ref, sems, *, send, ready
):
    _, side, _, core = places()
    move_q = pltpu.make_async_copy(q_ref, parts_ref.at[:, 0:32, :], sems.at[0])
    move_kv = pltpu.make_async_copy(kv_ref, parts_ref.at[:, 80:112, :], sems.at[1])
    ready(3)
    ready(7)
    ready(8)
    own, got = dq_ref[...].astype(f32), dq_got_ref[...].astype(f32)
    d_q = jnp.concatenate([jnp.where(side == 0, own, got), jnp.where(side == 0, got, own)], 0).T
    d_q = d_q.astype(bf16)
    q_ref[...] = dot_tn(normed_ref[...], d_q).astype(bf16).reshape(32, 32, 256)
    move_q.start()
    ready(1)
    ready(2)
    heads = []
    for j in range(2):
        total = jnp.zeros((128, 128), f32)
        for d in range(32):
            if (d >> 1) & 1 == j:
                total += back_ref[d].astype(f32)
        heads.append(turn_lanes(total, cos_ref[...], -sin_ref[...]))
    low = lanes_of((128, 128)) < 64
    d_k = jnp.where(low, heads[0], swap_halves(heads[1])).astype(bf16)
    d_v = jnp.where(low, swap_halves(heads[0]), heads[1]).astype(bf16)
    kv_ref[:, :, 0:128] = dot_tn(normed_ref[...], d_k).astype(bf16).reshape(32, 32, 128)
    kv_ref[:, :, 128:256] = dot_tn(normed_ref[...], d_v).astype(bf16).reshape(32, 32, 128)
    move_kv.start()
    ready(4)
    ready(5)
    ready(6)
    ready(9)
    first = dot_nt(d_q, wq_ref[...]) + dot_nt(d_k, wk_ref[...]) + dot_nt(d_v, wv_ref[...])
    x = tokens_ref[...].astype(f32)
    unit = x * lax.rsqrt(jnp.mean(x * x, -1, keepdims=True) + epsilon)
    gain = jnp.sum(first * unit, 0, keepdims=True)
    for to, low_half in ((keep_ref, 0), (give_ref, 1)):
        to[0:64, :] = jnp.where(core == low_half, first[0:64], first[64:128]).astype(bf16)
        to[64:80, :] = jnp.broadcast_to(gain, (16, 1024)).astype(bf16)
    move_q.wait()
    move_kv.wait()


def share_kernel(in_ref, gain_ref, out_ref, gain2_ref, total_ref, *, send):
    total_ref[...] = jnp.sum(in_ref[...].astype(f32), 0)
    for q in range(4):
        here = slice(256 * q, 256 * q + 256)
        gain2_ref[:, here] = total_ref[68 + q : 69 + q, :]
        total_ref[72 + q : 73 + q, :] = gain_ref[:, here].astype(f32)[0:1]
    out_ref[...] = jnp.broadcast_to(total_ref[...].astype(bf16)[None], (32, 112, 256))


def final_kernel(in_ref, query_ref, key_ref, value_ref, out_ref, router_ref, gain_ref, extra_ref, *, send):
    query_ref[...] = in_ref[:, 0:32, :].astype(f32).reshape(1024, 256)
    send(0)
    for q in range(4):
        here = slice(256 * q, 256 * q + 256)
        out_ref[:, here] = in_ref[8 * q : 8 * q + 8, 32:64, :].astype(f32).reshape(256, 256)
    send(3)
    key_ref[...] = in_ref[:, 80:112, 0:128].astype(f32).reshape(1024, 128)
    send(1)
    value_ref[...] = in_ref[:, 80:112, 128:256].astype(f32).reshape(1024, 128)
    send(2)
    extra_ref[...] = in_ref[:, 64:80, :].astype(f32)
    for q in range(4):
        router_ref[:, 256 * q : 256 * q + 256] = extra_ref[:, q, :]
        gain_ref[:, 256 * q : 256 * q + 256] = jnp.sum(extra_ref[:, 8 + q, :], 0, keepdims=True)


def pair_over_wa(keep, give):
    got = lax.ppermute(give, "wa", CORE_SWAP)
    pair = (keep.astype(f32) + got.astype(f32)).astype(bf16)
    return pair, lax.ppermute(pair, "wa", CHIP_SWAP)


def sum_over_wa(keep, give):
    pair, other = pair_over_wa(keep, give)
    mine = (pair.astype(f32) + other.astype(f32)).astype(bf16)
    return mine, lax.ppermute(mine, "wa", CORE_SWAP)


def pieces_over_wa(part):
    across = lax.ppermute(part, "wa", CHIP_SWAP)
    beside = lax.ppermute(part, "wa", CORE_SWAP)
    return across, beside, lax.ppermute(across, "wa", CORE_SWAP)


def local(
    tokens,
    norm1_gain,
    w_query,
    key_weight,
    value_weight,
    w_out,
    norm2_gain,
    w_router,
    w_gate,
    w_up,
    w_down,
    routes,
    cotangent,
):
    ctx = lax.axis_index("ctx").astype(jnp.int32)
    wa = lax.axis_index("wa").astype(jnp.int32)
    core, chip, side = wa % 2, wa // 2, (ctx >> 1) & 1
    rows, width, experts = 128, 1024, 32

    angles = angles_of(ctx)
    cosine, sine = jnp.cos(angles), jnp.sin(angles)
    one, zero = jnp.ones((rows, 64), f32), jnp.zeros((rows, 64), f32)
    cos_lanes = jnp.concatenate([cosine, cosine, one], 1)
    sin_lanes = jnp.concatenate([-sine, sine, zero], 1)
    cos_rows, sin_rows = cosine.T, sine.T
    gain1 = norm1_gain.reshape(1, width)
    kv_send, normed1, q_own, q_give = on_device(
        prelude_kernel,
        "prelude",
        "FFFFFVV",
        (
            ("S", shape((32, rows, 128))),
            ("S", shape((rows, width))),
            ("S", shape((rows, 128))),
            ("V", shape((rows, 128))),
        ),
        megabytes=56,
        us=2,
        lazy=True,
    )(tokens, gain1, w_query, key_weight, value_weight, cos_rows, sin_rows)
    kv = exchange(kv_send, "ctx")
    q_other = lax.ppermute(q_give, "ctx", PARTNER)

    member = jnp.any(
        routes[:, :, None] == jnp.arange(experts, dtype=jnp.int32)[None, None, :], axis=1
    )
    lower = (jnp.arange(rows)[:, None] >= jnp.arange(rows)[None, :]).astype(bf16)
    rank = jnp.where(member, dot(lower, member.astype(bf16)) - 1.0, -1.0).T
    router_t = w_router.T
    gain2 = norm2_gain.reshape(1, width)

    cot_quarter = lax.dynamic_slice_in_dim(cotangent, wa * 256, 256, 1)
    down_lanes = w_down[0].reshape(128, 8, 128).transpose(1, 0, 2).reshape(width, 128)
    weights = jnp.stack([w_gate[0], w_up[0]])
    down_across = lax.ppermute(down_lanes, "wa", CHIP_SWAP)
    kv, rank, q_other, weights, cot_quarter, down_across = lax.optimization_barrier(
        (kv, rank, q_other, weights, cot_quarter, down_across)
    )
    w_across, w_beside, w_diagonal = pieces_over_wa(weights)
    down_beside = lax.ppermute(down_lanes, "wa", CORE_SWAP)
    down_diagonal = lax.ppermute(down_across, "wa", CORE_SWAP)
    ctx_mine, ctx_give, context_o = on_device(
        attend_kernel,
        "attend",
        "VVV",
        (("V", shape((rows, 128))), ("V", shape((rows, 128))), ("V", shape((72, 512), f32))),
        [
            pltpu.VMEM((128, 512), bf16),
            pltpu.VMEM((1, 512), f32),
            pltpu.VMEM((1, 512), f32),
            pltpu.VMEM((128, 512), f32),
        ],
        us=0.5,
    )(q_own, q_other, kv)
    ctx_got = lax.ppermute(ctx_give, "ctx", PARTNER)
    context_t, mix_keep, mix_give = on_device(
        mix_kernel,
        "mix",
        "VVV",
        (("V", shape((256, rows))), ("V", shape((64, width))), ("V", shape((64, width)))),
        us=0.8,
    )(ctx_mine, ctx_got, w_out)
    mix_keep, mix_give, w_across = lax.optimization_barrier((mix_keep, mix_give, w_across))
    mine, theirs = sum_over_wa(mix_keep, mix_give)
    middle, normed2, gates, outgoing = on_device(
        route_kernel,
        "route",
        "VVVVVVV",
        (
            ("V", shape((rows, width), f32)),
            ("V", shape((rows, width))),
            ("V", shape((2 * experts, rows), f32)),
            ("V", shape((2048, 512))),
        ),
        us=1.6,
    )(tokens, mine, theirs, gain2, router_t, rank, cot_quarter)

    outgoing, w_across, w_beside, w_diagonal, down_beside, down_diagonal = lax.optimization_barrier(
        (outgoing, w_across, w_beside, w_diagonal, down_beside, down_diagonal)
    )
    arrived = exchange(outgoing.reshape(128, 16, 512), ("ctx", "wa")).reshape(32, 4, 16, 512)
    returning, hidden = on_device(
        expert_kernel,
        "experts",
        "VVVVVVVVV",
        (("V", shape((32, 4, 16, 512))), ("V", shape((512, 1536)))),
        [pltpu.VMEM((width, 512), bf16), pltpu.VMEM((width, 512), bf16), pltpu.VMEM((512, width), bf16)],
        megabytes=24,
        us=5,
    )(
        arrived, weights, w_across, w_beside, w_diagonal,
        down_lanes, down_across, down_beside, down_diagonal,
    )
    back = exchange(returning.reshape(128, 16, 512), ("ctx", "wa")).reshape(2048, 512)
    near_own, near_two, near_last, far = on_device(
        expert_grad_kernel,
        "expert_grads",
        "VV",
        (
            ("V", shape((3, width, 128))),
            ("V", shape((2, width, 128))),
            ("V", shape((width, 128))),
            ("V", shape((2, 3, width, 128))),
        ),
        us=3,
    )(arrived, hidden)
    back, near_own, near_two, near_last, far = lax.optimization_barrier(
        (back, near_own, near_two, near_last, far)
    )
    far = lax.ppermute(far, "wa", CORE_SWAP)
    far = far.astype(f32)
    near_own = near_own.astype(f32) + far[0]
    near_two = (near_two.astype(f32) + far[1, :2]).astype(bf16)
    near_last = (near_last.astype(f32) + far[1, 2]).astype(bf16)
    (sent,) = on_device(
        combine_kernel,
        "combine",
        "VVV",
        (("V", shape((272, 256))),),
        [pltpu.VMEM((32, 128), f32)],
        us=1,
    )(back, gates, cot_quarter)

    pieces = pieces_over_wa(sent)
    pieces, near_two = lax.optimization_barrier((pieces, near_two))
    near_got = lax.ppermute(near_two, "wa", CHIP_SWAP)
    d_middle, do_own, do_give, parts, output = on_device(
        second_norm_kernel,
        "second_norm",
        "VVVVVVVVVVVV",
        (
            ("V", shape((rows, width), f32)),
            ("V", shape((rows, 128))),
            ("V", shape((rows, 128))),
            ("V", shape((32, 48, 256))),
            ("V", shape((rows, width))),
        ),
        [pltpu.VMEM((rows, width), f32), pltpu.VMEM((32, 16, 256), f32)],
        us=1.6,
    )(sent, *pieces, gates, middle, normed2, cotangent, gain2, router_t, w_out, context_t)
    do_other = lax.ppermute(do_give, "ctx", PARTNER)

    angles2 = angles_of(ctx ^ 2)
    dq_own, dq_give, dkv = on_device(
        reverse_kernel,
        "reverse",
        "VVVVVVVVVV",
        (("V", shape((rows, 128))), ("V", shape((rows, 128))), ("V", shape((32, rows, 128)))),
        [
            pltpu.VMEM((128, 512), bf16),
            pltpu.VMEM((128, 512), bf16),
            pltpu.VMEM((1, 512), f32),
            pltpu.VMEM((128, 512), f32),
        ],
        us=1,
    )(
        q_own, q_other, kv, do_own, do_other, context_o,
        cos_rows, sin_rows, jnp.cos(angles2).T, jnp.sin(angles2).T,
    )
    dkv, near_got, near_last = lax.optimization_barrier((dkv, near_got, near_last))
    kv_back = exchange(dkv, "ctx")

    dq_got = lax.ppermute(dq_give, "ctx", PARTNER)
    filled = jnp.pad(parts, ((0, 0), (32, 32), (0, 0)))
    kv_back, filled, dq_got = lax.optimization_barrier((kv_back, filled, dq_got))
    parts_all, first_keep, first_give = on_device(
        late_kernel,
        "late",
        "VFFFFFFFFFH",
        (("H", shape((32, 112, 256))), ("V", shape((80, width))), ("V", shape((80, width)))),
        [
            pltpu.VMEM((32, 32, 256), bf16),
            pltpu.VMEM((32, 32, 256), bf16),
            pltpu.SemaphoreType.DMA((2,)),
        ],
        megabytes=56,
        us=2,
        lazy=True,
        aliases={10: 0},
    )(
        kv_back, cos_lanes, sin_lanes, normed1, key_weight, value_weight, w_query, dq_own, dq_got,
        tokens, filled,
    )
    summed = exchange(parts_all, "ctx")

    first_pair, first_other = pair_over_wa(first_keep, first_give)
    summed, first_other = lax.optimization_barrier((summed, first_other))
    first_mine = (first_pair.astype(f32) + first_other.astype(f32)).astype(bf16)
    shared, out_gain2 = on_device(
        share_kernel,
        "share",
        "VV",
        (("V", shape((32, 112, 256))), ("V", shape((1, width), f32))),
        [pltpu.VMEM((112, 256), f32)],
        us=0.5,
    )(summed, first_mine[64:])
    shared, near_last = lax.optimization_barrier((shared, near_last))
    spread_out = exchange(shared, "ctx")
    near_last = lax.ppermute(near_last, "wa", CHIP_SWAP)

    first_half = first_mine[:64]
    first_theirs = lax.ppermute(first_half, "wa", CORE_SWAP)
    d_first = jnp.where(
        core == 0, jnp.stack([first_half, first_theirs]), jnp.stack([first_theirs, first_half])
    ).reshape(rows, width).astype(f32)
    widened = tokens.astype(f32)
    root_first = lax.rsqrt(jnp.mean(widened * widened, -1, keepdims=True) + epsilon)
    unit_first = widened * root_first
    scaled_first = d_first * norm1_gain
    grad_tokens = (
        d_middle
        + root_first
        * (scaled_first - unit_first * jnp.mean(scaled_first * unit_first, -1, keepdims=True))
    ).astype(bf16)
    g_gate = near_own[0] + near_got[0].astype(f32)
    g_up = near_own[1] + near_got[1].astype(f32)
    g_down = (near_own[2] + near_last.astype(f32)).reshape(8, 128, 128)
    g_down = g_down.transpose(1, 0, 2).reshape(128, width)
    spread_out, output, grad_tokens, g_gate, g_up, g_down = lax.optimization_barrier(
        (spread_out, output, grad_tokens, g_gate, g_up, g_down)
    )
    out_query, out_key, out_value, out_out, out_router, out_gain1 = on_device(
        final_kernel,
        "final",
        "V",
        (
            ("S", shape((width, 256), f32)),
            ("S", shape((width, 128), f32)),
            ("S", shape((width, 128), f32)),
            ("S", shape((256, width), f32)),
            ("S", shape((experts, width), f32)),
            ("S", shape((1, width), f32)),
        ),
        [pltpu.VMEM((32, 16, 256), f32)],
        us=1.8,
    )(spread_out)
    return (
        output,
        grad_tokens,
        out_gain1.reshape(width),
        out_query,
        out_key,
        out_value,
        out_out,
        out_gain2.reshape(width),
        out_router.T,
        g_gate[None],
        g_up[None],
        g_down[None],
    )


def solution(mesh):
    in_specs = (
        P("ctx", None),
        P(),
        P(None, "wa"),
        P(None, "wa"),
        P(None, "wa"),
        P("wa", None),
        P(),
        P(),
        P("ctx", None, "wa"),
        P("ctx", None, "wa"),
        P("ctx", "wa", None),
        P("ctx", None),
        P("ctx", None),
    )
    out_specs = (
        P("ctx", None),
        P("ctx", None),
        P(),
        P(None, "wa"),
        P(None, "wa"),
        P(None, "wa"),
        P("wa", None),
        P(),
        P(),
        P("ctx", None, "wa"),
        P("ctx", None, "wa"),
        P("ctx", "wa", None),
    )
    return jax.shard_map(local, mesh=mesh, in_specs=in_specs, out_specs=out_specs, check_vma=False)
```
